32 devices in a mesh: replica: 16 (over z, y, core), shard: 2 (over x).
Axes of the slice: x: 2, y: 2, z: 4, core: 2. Of those that a mesh axis runs over, the one named last changes fastest.
Arguments:
- tokens: bfloat16 [16, 1024, 1088], P('replica', 'shard'), may hold values from -6 to 6
- qkv_weight: bfloat16 [1088, 3264], P('shard'), may hold values from -0.1875 to 0.1875
- out_weight: bfloat16 [1088, 1088], P('shard'), may hold values from -4 to 4
- up_weight: bfloat16 [1088, 4352], P('shard'), may hold values from -0.1875 to 0.1875
- down_weight: bfloat16 [4352, 1088], P('shard'), may hold values from -0.09375 to 0.09375
- attn_gain: bfloat16 [1088], P('shard'), may hold values from 0.099609375 to 1.8984375
- attn_shift: bfloat16 [1088], P('shard'), may hold values from -3 to 3
- query_bias: bfloat16 [1088], P('shard'), may hold values from -3 to 3
- value_bias: bfloat16 [1088], P('shard'), may hold values from -3 to 3
- out_bias: bfloat16 [1088], P('shard'), may hold values from -3 to 3
- mlp_gain: bfloat16 [1088], P('shard'), may hold values from 0.099609375 to 1.8984375
- mlp_shift: bfloat16 [1088], P('shard'), may hold values from -3 to 3
- up_bias: bfloat16 [4352], P('shard'), may hold values from -3 to 3
- down_bias: bfloat16 [1088], P('shard'), may hold values from -3 to 3
- cotangent: bfloat16 [16, 1024, 1088], P('replica', 'shard'), may hold values from -6 to 6
Outputs:
- block_out: bfloat16 [16, 1024, 1088], P('replica', 'shard')
- grad_tokens: bfloat16 [16, 1024, 1088], P('replica', 'shard')
- grad_qkv_weight: float32 [1088, 3264], P('shard')
- grad_out_weight: float32 [1088, 1088], P('shard')
- grad_up_weight: float32 [1088, 4352], P('shard')
- grad_down_weight: float32 [4352, 1088], P('shard')
- grad_attn_gain: float32 [1088], P('shard')
- grad_attn_shift: float32 [1088], P('shard')
- grad_query_bias: float32 [1088], P('shard')
- grad_value_bias: float32 [1088], P('shard')
- grad_out_bias: float32 [1088], P('shard')
- grad_mlp_gain: float32 [1088], P('shard')
- grad_mlp_shift: float32 [1088], P('shard')
- grad_up_bias: float32 [4352], P('shard')
- grad_down_bias: float32 [1088], P('shard')
The draws below stay inside these ranges and needn't reach their ends.
All inputs are finite; a program needn't handle non-finite values.
Results may differ from the reference program's by a relative error of at most 0.019.
Values may be sent and summed in bfloat16 or wider, within the bound.
No kernel may reach another device: no remote copies, remote signals or barrier semaphores. Data moves between devices by JAX's collectives and lax.ppermute only.
A program may use at most 256 MiB of HBM per device.

```python
import jax
import jax.numpy as jnp
from jax import lax

D = 1088
HEADS = 17
HD = 64
FF = 4352
LEN = 1024
BATCH = 16


def level_of(stream_key, dims, pieces, least, top_value):
    factor_of = 1.0
    for axis_at, shards_of in pieces:
        steps = jax.random.uniform(jax.random.fold_in(jax.random.fold_in(stream_key, 6), axis_at), (shards_of,), jnp.float32, least / len(pieces), top_value / len(pieces))
        factor_of = factor_of * jnp.repeat(jnp.exp(steps), dims[axis_at] // shards_of).reshape((-1,) + (1,) * (len(dims) - 1 - axis_at))
    return factor_of


def noise(rng, extent, spread, most, cuts=(), kind=jnp.bfloat16):
    factor_of = level_of(rng, extent, cuts, -0.22, 0.18) if cuts else 1.0
    drawn = jax.random.normal(rng, extent, jnp.float32) * spread * factor_of
    return jnp.minimum(jnp.maximum(drawn, -most), most).astype(kind)


def setup_inputs(seed: int = 0) -> dict:
    splits = jax.random.split(jax.random.key(seed), 16)
    return {
        "tokens": noise(splits[0], (BATCH, LEN, D), 1.0, 6.0, ((0, 16), (1, 2))),
        "qkv_weight": noise(splits[1], (D, 3 * D), D ** -0.5, 0.1875, ((0, 2),)),
        "out_weight": noise(splits[2], (D, D), (max(1, 2 * D // LEN)) ** -0.5, 4.0, ((0, 2),)),
        "up_weight": noise(splits[3], (D, FF), D ** -0.5, 0.1875, ((0, 2),)),
        "down_weight": noise(splits[4], (FF, D), FF ** -0.5, 0.09375, ((0, 2),)),
        "attn_gain": jnp.clip(1.0 + 0.18 * jax.random.normal(splits[5], (D,), jnp.float32), 0.099609375, 1.8984375).astype(jnp.bfloat16),
        "attn_shift": noise(splits[6], (D,), 0.5, 3.0, ((0, 2),)),
        "query_bias": noise(splits[7], (D,), 0.5, 3.0, ((0, 2),)),
        "value_bias": noise(splits[8], (D,), 0.5, 3.0, ((0, 2),)),
        "out_bias": noise(splits[9], (D,), 0.5, 3.0, ((0, 2),)),
        "mlp_gain": jnp.clip(1.0 + 0.18 * jax.random.normal(splits[10], (D,), jnp.float32), 0.099609375, 1.8984375).astype(jnp.bfloat16),
        "mlp_shift": noise(splits[11], (D,), 0.5, 3.0, ((0, 2),)),
        "up_bias": noise(splits[12], (FF,), 0.5, 3.0, ((0, 2),)),
        "down_bias": noise(splits[13], (D,), 0.5, 3.0, ((0, 2),)),
        "cotangent": noise(splits[14], (BATCH, LEN, D), 1.0, 6.0, ((0, 16), (1, 2))),
    }


@jax.custom_vjp
def low(v):
    return lax.optimization_barrier(v.astype(jnp.bfloat16)).astype(jnp.float32)

@jax.custom_vjp
def low_back(v):
    return v

def low_keep(v):
    return (low(v), None)

def low_pass(kept, grad):
    return (grad,)

def back_keep(v):
    return (v, None)

def back_low(kept, grad):
    return (low(grad),)
low.defvjp(low_keep, low_pass)
low_back.defvjp(back_keep, back_low)
EPSILON = 1e-05

def matmul_high(left, right):
    return jnp.dot(left, right, precision=lax.Precision.HIGHEST)

def norm_rows(values, gain, shift):
    average = lax.optimization_barrier(jnp.mean(values, axis=-1, keepdims=True))
    centered = values - average
    variance = lax.optimization_barrier(jnp.mean(centered * centered, axis=-1, keepdims=True))
    return centered * lax.rsqrt(variance + EPSILON) * gain + shift

def gelu_curve(values):
    inner = 0.7978845608 * (values + 0.044715 * values * values * values)
    return 0.5 * values * (1.0 + jnp.tanh(inner))

def attend_block(queries, keys, values, first):
    scores = jnp.einsum('qhd,khd->hqk', queries, keys, precision=lax.Precision.HIGHEST) * 0.125
    scores = low_back(scores)
    rows_pos = first + jnp.arange(queries.shape[0], dtype=jnp.int32)
    cols_pos = jnp.arange(keys.shape[0], dtype=jnp.int32)
    allowed = cols_pos[None, :] <= rows_pos[:, None]
    scores = jnp.where(allowed[None], scores, -1e+30)
    shifted = scores - lax.optimization_barrier(jnp.max(scores, axis=-1, keepdims=True))
    expons = jnp.exp(shifted)
    probs = expons / lax.optimization_barrier(jnp.sum(expons, axis=-1, keepdims=True))
    return jnp.einsum('hqk,khd->qhd', low(probs), values, precision=lax.Precision.HIGHEST)

def attention(queries, keys, values):
    block = min(512, LEN)
    count = LEN // block
    query_blocks = queries.reshape(count, block, HEADS, HD)
    key_heads = keys.reshape(LEN, HEADS, HD)
    value_heads = values.reshape(LEN, HEADS, HD)
    starts = jnp.arange(count, dtype=jnp.int32) * block

    def one_block(items):
        return attend_block(items[0], key_heads, value_heads, items[1])
    outputs = lax.map(jax.checkpoint(one_block), (query_blocks, starts))
    return outputs.reshape(LEN, D)

def layer(inputs, params):
    qkv_weight, out_weight, up_weight, down_weight, attn_gain, attn_shift, query_bias, value_bias, out_bias, mlp_gain, mlp_shift, up_bias, down_bias = params
    normed = low(norm_rows(inputs, attn_gain, attn_shift))
    mixed = matmul_high(normed, qkv_weight)
    queries = low(low_back(mixed[:, :D] + query_bias))
    keys = low(low_back(mixed[:, D:2 * D]))
    values = low(low_back(mixed[:, 2 * D:] + value_bias))
    context = low(low_back(attention(queries, keys, values)))
    branch = low_back(matmul_high(context, out_weight) + out_bias)
    middle = inputs + branch
    normed_two = low(norm_rows(middle, mlp_gain, mlp_shift))
    hidden = low_back(matmul_high(normed_two, up_weight) + up_bias)
    active = low(gelu_curve(hidden))
    return middle + matmul_high(active, down_weight) + down_bias

def reference(tokens, qkv_weight, out_weight, up_weight, down_weight, attn_gain, attn_shift, query_bias, value_bias, out_bias, mlp_gain, mlp_shift, up_bias, down_bias, cotangent):
    params = tuple((item.astype(jnp.float32) for item in (qkv_weight, out_weight, up_weight, down_weight, attn_gain, attn_shift, query_bias, value_bias, out_bias, mlp_gain, mlp_shift, up_bias, down_bias)))

    def per_sequence(totals, pair):
        seq_tokens, seq_grad = pair
        output, pullback = jax.vjp(layer, seq_tokens.astype(jnp.float32), params)
        grad_inputs, grad_params = pullback(seq_grad.astype(jnp.float32))
        totals = jax.tree.map(lambda first, second: first + second, totals, grad_params)
        return (totals, (output.astype(jnp.bfloat16), grad_inputs.astype(jnp.bfloat16)))
    zeros = tuple((jnp.zeros_like(item) for item in params))
    totals, (outputs, grads) = lax.scan(per_sequence, zeros, (tokens, cotangent))
    return (outputs, grads, totals[0], totals[1], totals[2], totals[3], totals[4], totals[5], totals[6], totals[7], totals[8], totals[9], totals[10], totals[11], totals[12])
```

```python
import functools
import jax
import jax.numpy as jnp
from jax import lax
from jax.experimental import pallas as pl
from jax.experimental.pallas import tpu as pltpu
from jax.sharding import PartitionSpec as P

HD = 64
SCALING = 0.125
NEG = -1e30
LANES = 128


def _nt(a, b):
    return lax.dot_general(a, b, (((1,), (1,)), ((), ())), preferred_element_type=jnp.float32)


def _nn(a, b):
    return lax.dot_general(a, b, (((1,), (0,)), ((), ())), preferred_element_type=jnp.float32)


def _lane_valid(shape, width):
    left = width - pl.program_id(1) * LANES
    return lax.broadcasted_iota(jnp.int32, shape, 1) < left


def _clean(ref, width):
    block = ref[...]
    return jnp.where(_lane_valid(block.shape, width), block, jnp.zeros_like(block))


def _head_part(block, head):
    lane = lax.broadcasted_iota(jnp.int32, block.shape, 1)
    keep = (lane < HD) if head == 0 else (lane >= HD)
    return jnp.where(keep, block, jnp.zeros_like(block))


def _diag_mask(keys, rows, first):
    key_at = lax.broadcasted_iota(jnp.int32, (keys, rows), 0)
    row_at = lax.broadcasted_iota(jnp.int32, (keys, rows), 1) + first
    return key_at <= row_at


def forward_kernel(pos_ref, q_ref, k_ref, v_ref, ctx_ref, lse_ref, kc_ref, vt_ref, *, span, width):
    pos = pos_ref[0]
    block = min(256, span)
    queries = _clean(q_ref, width)
    kc_ref[...] = _clean(k_ref, width)
    length = k_ref.shape[0]
    for j in range(length // span):
        vt_ref[j] = _clean(v_ref.at[pl.ds(j * span, span), :], width).T
    chains = []
    for head in range(2):
        part = _head_part(queries, head)
        for at in range(0, span, block):
            chains.append((part[at : at + block], at))

    def update(state, scores, vt):
        peak, total, acc = state
        top = jnp.maximum(peak, jnp.max(scores, axis=0, keepdims=True))
        fade = jnp.exp(peak - top)
        expons = jnp.exp(scores - top)
        total = total * fade + jnp.sum(expons, axis=0, keepdims=True)
        acc = acc * fade + _nn(vt, expons.astype(jnp.bfloat16))
        return top, total, acc

    states = []
    own_vt = vt_ref[pos]
    for part, at in chains:
        keys = at + block
        own_k = kc_ref[pl.ds(pl.multiple_of(pos * span, span), keys), :]
        scores = jnp.where(_diag_mask(keys, block, at), _nt(own_k, part), NEG)
        peak = jnp.max(scores, axis=0, keepdims=True)
        expons = jnp.exp(scores - peak)
        total = jnp.sum(expons, axis=0, keepdims=True)
        acc = _nn(own_vt[:, :keys], expons.astype(jnp.bfloat16))
        states.append((peak, total, acc))

    def past(j, states):
        key_block = kc_ref[pl.ds(pl.multiple_of(j * span, span), span), :]
        vt = vt_ref[j]
        return tuple(
            update(state, _nt(key_block, part), vt) for state, (part, _) in zip(states, chains)
        )

    states = lax.fori_loop(0, pos, past, tuple(states))
    per_head = len(chains) // 2
    for i in range(per_head):
        at = i * block
        (peak0, total0, acc0), (peak1, total1, acc1) = states[i], states[per_head + i]
        row = lax.broadcasted_iota(jnp.int32, acc0.shape, 0)
        both = jnp.where(row < HD, acc0 / total0, acc1 / total1)
        ctx_ref[at : at + block, :] = both.T.astype(ctx_ref.dtype)
        lse_ref[0, 0:1, at : at + block] = peak0 + jnp.log(total0)
        lse_ref[0, 1:2, at : at + block] = peak1 + jnp.log(total1)


def backward_kernel(pos_ref, q_ref, k_ref, v_ref, g_ref, ctx_ref, lse_ref, dq_ref, dk_ref, dv_ref,
                    kc_ref, vc_ref, kt_ref, dk_acc, dv_acc, *, span, width):
    pos = pos_ref[0]
    block = min(256, span)
    queries = _clean(q_ref, width)
    grads = _clean(g_ref, width)
    context = _clean(ctx_ref, width)
    kc_ref[...] = _clean(k_ref, width)
    vc_ref[...] = _clean(v_ref, width)
    length = k_ref.shape[0]
    for j in range(length // span):
        kt_ref[j] = kc_ref[pl.ds(j * span, span), :].T
    dk_acc[...] = jnp.zeros_like(dk_acc)
    dv_acc[...] = jnp.zeros_like(dv_acc)
    product = (grads.astype(jnp.float32) * context.astype(jnp.float32)).T
    chains = []
    for head in range(2):
        q_part = _head_part(queries, head)
        g_part = _head_part(grads, head)
        inner = jnp.sum(product[head * HD : (head + 1) * HD], axis=0, keepdims=True)
        for at in range(0, span, block):
            chains.append((
                q_part[at : at + block], g_part[at : at + block], inner[:, at : at + block],
                lse_ref[0, head : head + 1, at : at + block], at,
            ))

    def piece(chain, key_block, value_block, kt, masked):
        q_part, g_part, inner, lse, at = chain
        scores = _nt(key_block, q_part)
        if masked:
            scores = jnp.where(_diag_mask(key_block.shape[0], q_part.shape[0], at), scores, NEG)
        probs = jnp.exp(scores - lse)
        grad_probs = _nt(value_block, g_part)
        grad_scores = (probs * (grad_probs - inner)).astype(jnp.bfloat16)
        dq = _nn(kt, grad_scores)
        dk = _nn(grad_scores, q_part)
        dv = _nn(probs.astype(jnp.bfloat16), g_part)
        return dq, dk, dv

    start = pl.multiple_of(pos * span, span)
    own_kt = kt_ref[pos]
    dqs = []
    for chain in chains:
        keys = chain[4] + block
        where = pl.ds(start, keys)
        dq, dk, dv = piece(chain, kc_ref[where, :], vc_ref[where, :], own_kt[:, :keys], True)
        dk_acc[where, :] += dk
        dv_acc[where, :] += dv
        dqs.append(dq)

    def past(j, dqs):
        where = pl.ds(pl.multiple_of(j * span, span), span)
        key_block, value_block, kt = kc_ref[where, :], vc_ref[where, :], kt_ref[j]
        out, dk_sum, dv_sum = [], None, None
        for chain, dq_old in zip(chains, dqs):
            dq, dk, dv = piece(chain, key_block, value_block, kt, False)
            dk_sum = dk if dk_sum is None else dk_sum + dk
            dv_sum = dv if dv_sum is None else dv_sum + dv
            out.append(dq_old + dq)
        dk_acc[where, :] = dk_sum
        dv_acc[where, :] = dv_sum
        return tuple(out)

    dqs = lax.fori_loop(0, pos, past, tuple(dqs))
    per_head = len(chains) // 2
    for i in range(per_head):
        at = i * block
        row = lax.broadcasted_iota(jnp.int32, dqs[0].shape, 0)
        both = jnp.where(row < HD, dqs[i], dqs[per_head + i]) * SCALING
        dq_ref[at : at + block, :] = both.T.astype(dq_ref.dtype)
    dk_ref[...] = dk_acc[...].astype(dk_ref.dtype)
    dv_ref[...] = dv_acc[...].astype(dv_ref.dtype)


def attention_forward(position, queries, keys, values, seqs, span):
    rows, width = queries.shape
    length = keys.shape[0] // seqs
    pairs = pl.cdiv(width, LANES)
    own = pl.BlockSpec((span, LANES), lambda s, h, p: (s, h))
    whole = pl.BlockSpec((length, LANES), lambda s, h, p: (s, h))
    lse = pl.BlockSpec((1, 2, span), lambda s, h, p: (s * pairs + h, 0, 0))
    return pl.pallas_call(
        functools.partial(forward_kernel, span=span, width=width),
        grid_spec=pltpu.PrefetchScalarGridSpec(
            num_scalar_prefetch=1,
            grid=(seqs, pairs),
            in_specs=[own, whole, whole],
            out_specs=[own, lse],
            scratch_shapes=[
                pltpu.VMEM((length, LANES), jnp.bfloat16),
                pltpu.VMEM((length // span, LANES, span), jnp.bfloat16),
            ],
        ),
        out_shape=[
            jax.ShapeDtypeStruct((rows, width), jnp.bfloat16),
            jax.ShapeDtypeStruct((seqs * pairs, 2, span), jnp.float32),
        ],
        compiler_params=pltpu.CompilerParams(vmem_limit_bytes=48 * 1024 * 1024),
        cost_estimate=pl.CostEstimate(flops=4 * rows * length * width * 2, bytes_accessed=8 * rows * width * 2, transcendentals=rows * length * 17),
        name="attention_forward",
    )(position, queries, keys, values)


def attention_backward(position, queries, keys, values, grads, context, lse_rows, seqs, span):
    rows, width = queries.shape
    length = keys.shape[0] // seqs
    pairs = pl.cdiv(width, LANES)
    own = pl.BlockSpec((span, LANES), lambda s, h, p: (s, h))
    whole = pl.BlockSpec((length, LANES), lambda s, h, p: (s, h))
    lse = pl.BlockSpec((1, 2, span), lambda s, h, p: (s * pairs + h, 0, 0))
    return pl.pallas_call(
        functools.partial(backward_kernel, span=span, width=width),
        grid_spec=pltpu.PrefetchScalarGridSpec(
            num_scalar_prefetch=1,
            grid=(seqs, pairs),
            in_specs=[own, whole, whole, own, own, lse],
            out_specs=[own, whole, whole],
            scratch_shapes=[
                pltpu.VMEM((length, LANES), jnp.bfloat16),
                pltpu.VMEM((length, LANES), jnp.bfloat16),
                pltpu.VMEM((length // span, LANES, span), jnp.bfloat16),
                pltpu.VMEM((length, LANES), jnp.float32),
                pltpu.VMEM((length, LANES), jnp.float32),
            ],
        ),
        out_shape=[
            jax.ShapeDtypeStruct((rows, width), jnp.bfloat16),
            jax.ShapeDtypeStruct(keys.shape, jnp.bfloat16),
            jax.ShapeDtypeStruct(keys.shape, jnp.bfloat16),
        ],
        compiler_params=pltpu.CompilerParams(vmem_limit_bytes=48 * 1024 * 1024),
        cost_estimate=pl.CostEstimate(flops=10 * rows * length * width * 2, bytes_accessed=12 * rows * width * 2, transcendentals=rows * length * 17),
        name="attention_backward",
    )(position, queries, keys, values, grads, context, lse_rows)


EPSILON = 1e-05
CORE_BIT = 1


def centred(values):
    average = jnp.mean(values, axis=-1, keepdims=True)
    off = values - average
    rstd = lax.rsqrt(jnp.mean(off * off, axis=-1, keepdims=True) + EPSILON)
    return off * rstd, rstd


def norm_pull(grad, unit, rstd, gain):
    scaled = grad * gain
    first = jnp.mean(scaled, axis=-1, keepdims=True)
    second = jnp.mean(scaled * unit, axis=-1, keepdims=True)
    return rstd * (scaled - first - unit * second)


def gelu_parts(values):
    square = values * values
    tanh = jnp.tanh(0.7978845608 * values * (1.0 + 0.044715 * square))
    half = 0.5 * (1.0 + tanh)
    slope = half + 0.5 * values * (1.0 - tanh * tanh) * (
        0.7978845608 * (1.0 + 3.0 * 0.044715 * square)
    )
    return values * half, slope


def dot(left, right):
    return jnp.dot(left, right, preferred_element_type=jnp.float32)


def dot_nt(left, right):
    return lax.dot_general(
        left, right, (((1,), (1,)), ((), ())), preferred_element_type=jnp.float32
    )


def dot_tn(left, right):
    return lax.dot_general(
        left, right, (((0,), (0,)), ((), ())), preferred_element_type=jnp.float32
    )


def low(values):
    return values.astype(jnp.bfloat16)


def swap(values, bit):
    size = lax.axis_size("replica")
    return lax.ppermute(values, "replica", [(i, i ^ bit) for i in range(size)])


def cross(values):
    return lax.ppermute(values, "shard", [(0, 1), (1, 0)])


def after(values, earlier):
    return lax.optimization_barrier((values, earlier))[0]


def has_bit(bit):
    return (lax.axis_index("replica") & bit) != 0


def choose(flag, left, right):
    return jnp.where(flag, left, right)


def in_order(bit, mine, other):
    flag = has_bit(bit)
    return jnp.concatenate([choose(flag, other, mine), choose(flag, mine, other)], axis=0)


def spread_start(weight, bits):
    rows = weight.shape[0]
    count = 2 ** len(bits)
    size = -(-rows // (8 * count)) * 8
    index = jnp.int32(0)
    for bit in bits:
        index = index * 2 + has_bit(bit).astype(jnp.int32)
    start = jnp.minimum(index * size, rows - size)
    return cross(lax.dynamic_slice_in_dim(weight, start, size, axis=0))


def spread_end(weight, got, bits):
    rows = weight.shape[0]
    count = 2 ** len(bits)
    size = got.shape[0]
    for bit in bits[::-1]:
        got = in_order(bit, got, swap(got, bit))
    extra = count * size - rows
    if extra:
        got = jnp.concatenate([got[: (count - 1) * size], got[(count - 1) * size + extra :]], axis=0)
    first = lax.axis_index("shard") == 0
    return jnp.concatenate([choose(first, weight, got), choose(first, got, weight)], axis=0)


def reduce_start(give, keep):
    return low(keep.astype(jnp.float32) + cross(low(give)).astype(jnp.float32))


def halves(values):
    rows = values.shape[0]
    size = -(-rows // 16) * 8
    return values[:size], values[rows - size :]


def reduce_rest(values, bits):
    stack = []
    for bit in bits[:-1]:
        lower, upper = halves(values)
        flag = has_bit(bit)
        sent = swap(choose(flag, lower, upper), bit)
        stack.append((bit, values.shape[0]))
        values = low(choose(flag, upper, lower).astype(jnp.float32) + sent.astype(jnp.float32))
    values = low(values.astype(jnp.float32) + swap(values, bits[-1]).astype(jnp.float32))
    for bit, rows in stack[::-1]:
        both = in_order(bit, values, swap(values, bit))
        size = values.shape[0]
        if 2 * size != rows:
            both = jnp.concatenate([both[: rows - size], both[size:]], axis=0)
        values = both
    return values


def columns_of(values, axis, index):
    size = values.shape[axis] // 2
    low_part = lax.slice_in_dim(values, 0, size, axis=axis)
    high_part = lax.slice_in_dim(values, size, 2 * size, axis=axis)
    return choose(index == 0, low_part, high_part)


def on_device(
    tokens, qkv_weight, out_weight, up_weight, down_weight, attn_gain, attn_shift, query_bias,
    value_bias, out_bias, mlp_gain, mlp_shift, up_bias, down_bias, cotangent,
):
    seqs, span, width = tokens.shape
    rows = seqs * span
    shards = lax.axis_size("shard")
    replicas = lax.axis_size("replica")
    position = lax.axis_index("shard")
    core = lax.axis_index("replica") & CORE_BIT
    length = span * shards
    hidden_units = up_weight.shape[1]
    pairwise = shards == 2
    bits = []
    bit = 2
    while bit < replicas:
        bits.append(bit)
        bit *= 2
    fast_bits = [CORE_BIT] + bits[:2]

    shards_of = (attn_gain, attn_shift, query_bias, value_bias, out_bias, mlp_gain, mlp_shift,
                 up_bias, down_bias)
    flat_vectors = jnp.concatenate(shards_of)
    all_vectors = lax.all_gather(flat_vectors, "shard", axis=0, tiled=False)
    vectors, at = [], 0
    for item in shards_of:
        size = item.shape[0]
        vectors.append(all_vectors[:, at : at + size].reshape(-1).astype(jnp.float32))
        at += size
    (gain_first, shift_first, bias_query, bias_value, bias_out, gain_second, shift_second, bias_up,
     bias_down) = vectors

    if pairwise:
        order = (0, 1)
        own_tokens = tokens.reshape(rows, width)
        got_qkv = spread_start(qkv_weight, fast_bits)
        got_out = spread_start(after(out_weight, got_qkv), fast_bits)
        other = cross(after(own_tokens, got_out))
        got_up = spread_start(after(up_weight, other), fast_bits)
        got_down = spread_start(after(down_weight, got_up), fast_bits)
        full_qkv = spread_end(qkv_weight, got_qkv, fast_bits)
        full_out = spread_end(out_weight, got_out, fast_bits)
        full_up = spread_end(up_weight, got_up, fast_bits)
        full_down = spread_end(down_weight, got_down, fast_bits)
        first = position == 0
        pair = tokens.shape[0], 1, span, width
        own_part, other_part = own_tokens.reshape(pair), other.reshape(pair)
        all_tokens = jnp.concatenate(
            [choose(first, own_part, other_part), choose(first, other_part, own_part)], axis=1
        ).reshape(seqs * length, width)
    else:
        full_qkv, full_out, full_up, full_down = [
            lax.all_gather(item, "shard", axis=0, tiled=True)
            for item in (qkv_weight, out_weight, up_weight, down_weight)
        ]
        all_tokens = lax.all_gather(tokens, "shard", axis=1, tiled=True).reshape(-1, width)

    def own_rows(values):
        per_seq = values.reshape(seqs, length, values.shape[-1])
        return lax.dynamic_slice_in_dim(per_seq, position * span, span, axis=1).reshape(rows, -1)

    grad_out = cotangent.reshape(rows, width)
    grad_out_both = jnp.concatenate([grad_out, swap(grad_out, CORE_BIT)], axis=0)

    flat = tokens.reshape(rows, width).astype(jnp.float32)
    unit_all, rstd_all = centred(all_tokens.astype(jnp.float32))
    normed_all = low(unit_all * gain_first + shift_first)
    normed_sib = swap(normed_all, CORE_BIT)
    normed = own_rows(normed_all)
    full_q, full_k, full_v = (full_qkv[:, i * width : (i + 1) * width] for i in range(3))
    queries = low(low(dot(normed, full_q) + bias_query) * SCALING)
    keys = low(dot(normed_all, full_k))
    values = low(dot(normed_all, full_v) + bias_value)
    spot = position.astype(jnp.int32).reshape(1)
    context, lse = attention_forward(spot, queries, keys, values, seqs, span)
    context_sib = swap(context, CORE_BIT)
    middle = flat + dot(context, full_out) + bias_out
    unit_second, rstd_second = centred(middle)
    normed_two = low(unit_second * gain_second + shift_second)
    normed_two_sib = swap(normed_two, CORE_BIT)
    active_float, slope = gelu_parts(dot(normed_two, full_up) + bias_up)
    active = low(active_float)
    slope = low(slope)

    def split_rows(lhs, rhs):
        if pairwise:
            give = dot_tn(columns_of(lhs, 1, 1 - position), rhs)
            keep = dot_tn(columns_of(lhs, 1, position), rhs)
            return reduce_start(low(give), low(keep))
        return lax.psum_scatter(low(dot_tn(lhs, rhs)), "shard", scatter_dimension=0, tiled=True)

    grouped = active.reshape(rows, shards, 2, -1)
    taken = jnp.where(core == 0, grouped[:, :, 0], grouped[:, :, 1]).reshape(rows, -1)
    given = jnp.where(core == 0, grouped[:, :, 1], grouped[:, :, 0]).reshape(rows, -1)
    active_both = jnp.concatenate([taken, swap(given, CORE_BIT)], axis=0)
    sum_down = split_rows(active_both, grad_out_both)
    sum_down = reduce_rest(sum_down, bits)
    sum_down = in_order(CORE_BIT, sum_down, swap(sum_down, CORE_BIT))

    result = middle + dot(active, full_down) + bias_down
    block_out = low(result).reshape(seqs, span, width)

    def by_columns(lhs_both, part):
        taken = columns_of(part, 1, core)
        given = columns_of(part, 1, 1 - core)
        return split_rows(lhs_both, jnp.concatenate([taken, swap(given, CORE_BIT)], axis=0))

    def join_columns(values):
        other = swap(values, CORE_BIT)
        left = choose(core == 0, values, other)
        right = choose(core == 0, other, values)
        return left, right

    grad_float = grad_out.astype(jnp.float32)
    grad_hidden = low(dot_nt(grad_out, full_down) * slope.astype(jnp.float32))
    normed_two_both = jnp.concatenate([normed_two, normed_two_sib], axis=0)
    sum_up = by_columns(normed_two_both, grad_hidden)
    sum_up = reduce_rest(sum_up, bits)
    sum_up = jnp.concatenate(join_columns(sum_up), axis=1)
    grad_normed_two = dot_nt(grad_hidden, full_up)
    grad_middle = norm_pull(grad_normed_two, unit_second, rstd_second, gain_second) + grad_float
    grad_branch = low(grad_middle)
    grad_context = low(dot_nt(grad_branch, full_out))
    context_both = jnp.concatenate([context, context_sib], axis=0)
    sum_out = by_columns(context_both, grad_branch)
    sum_out = reduce_rest(sum_out, bits)
    sum_out = jnp.concatenate(join_columns(sum_out), axis=1)

    grad_q, grad_k, grad_v = attention_backward(
        spot, queries, keys, values, grad_context, context, lse, seqs, span
    )
    normed_both = jnp.concatenate([normed_all, normed_sib], axis=0)
    own_both = jnp.concatenate([normed, own_rows(normed_sib)], axis=0)
    third = width // 2
    half_q, half_k, half_v = (
        jnp.concatenate(
            [columns_of(part, 1, core), swap(columns_of(part, 1, 1 - core), CORE_BIT)], axis=0
        )
        for part in (grad_q, grad_k, grad_v)
    )
    if pairwise:
        def three(index):
            left_own = columns_of(own_both, 1, index)
            left_all = columns_of(normed_both, 1, index)
            return low(jnp.concatenate(
                [dot_tn(left_own, half_q), dot_tn(left_all, half_k), dot_tn(left_all, half_v)],
                axis=1,
            ))
        sum_qkv = reduce_start(three(1 - position), three(position))
    else:
        sum_qkv = lax.psum_scatter(
            low(jnp.concatenate(
                [dot_tn(own_both, half_q), dot_tn(normed_both, half_k), dot_tn(normed_both, half_v)],
                axis=1,
            )),
            "shard", scatter_dimension=0, tiled=True,
        )
    sum_qkv = reduce_rest(sum_qkv, bits)
    left, right = join_columns(sum_qkv)
    sum_qkv = jnp.concatenate(
        [part[:, i * third : (i + 1) * third] for i in range(3) for part in (left, right)], axis=1
    )

    from_query = dot_nt(grad_q, full_q)
    from_rest = dot_nt(grad_k, full_k) + dot_nt(grad_v, full_v)
    if pairwise:
        halves_of = from_rest.reshape(seqs, 2, span, width)
        mine = choose(position == 0, halves_of[:, 0], halves_of[:, 1]).reshape(rows, width)
        theirs = choose(position == 0, halves_of[:, 1], halves_of[:, 0]).reshape(rows, width)
        grad_normed = from_query + mine + cross(low(theirs)).astype(jnp.float32)
    else:
        grad_normed = from_query + lax.psum_scatter(
            from_rest.reshape(seqs, length, width), "shard", scatter_dimension=1, tiled=True
        ).reshape(rows, width)
    unit_first, rstd_first = own_rows(unit_all), own_rows(rstd_all)
    grad_tokens = low(norm_pull(grad_normed, unit_first, rstd_first, gain_first) + grad_middle)

    def column_sum(values):
        return jnp.sum(values.astype(jnp.float32), axis=0)

    sums = (
        column_sum(grad_normed * unit_first),
        column_sum(grad_normed),
        column_sum(grad_q),
        column_sum(grad_v),
        column_sum(grad_branch),
        column_sum(grad_normed_two * unit_second),
        column_sum(grad_normed_two),
        column_sum(grad_hidden),
        column_sum(grad_float),
    )
    packed = jnp.concatenate([item.reshape(shards, -1) for item in sums], axis=1)
    packed = lax.psum(packed, ("replica", "shard"))
    packed = lax.dynamic_index_in_dim(packed, position, axis=0, keepdims=False)
    outs, at = [], 0
    for item in sums:
        size = item.shape[0] // shards
        outs.append(packed[at : at + size])
        at += size
    return (
        block_out,
        grad_tokens.reshape(seqs, span, width),
        sum_qkv.astype(jnp.float32),
        sum_out.astype(jnp.float32),
        sum_up.astype(jnp.float32),
        sum_down.astype(jnp.float32),
        *outs,
    )


def solution(mesh):
    vector, matrix, rows = P("shard"), P("shard", None), P("replica", "shard", None)
    return jax.shard_map(
        on_device,
        mesh=mesh,
        in_specs=(rows, *[matrix] * 4, *[vector] * 9, rows),
        out_specs=(rows, rows, *[matrix] * 4, *[vector] * 9),
        check_vma=False,
    )
```

```python
import functools
import jax
import jax.numpy as jnp
from jax import lax
from jax.experimental import pallas as pl
from jax.experimental.pallas import tpu as pltpu
from jax.sharding import PartitionSpec as P

HD = 64
SCALING = 0.125
NEG = -1e30
LANES = 128


def _nt(a, b):
    return lax.dot_general(a, b, (((1,), (1,)), ((), ())), preferred_element_type=jnp.float32)


def _nn(a, b):
    return lax.dot_general(a, b, (((1,), (0,)), ((), ())), preferred_element_type=jnp.float32)


def _lane_valid(shape, width):
    left = width - pl.program_id(1) * LANES
    return lax.broadcasted_iota(jnp.int32, shape, 1) < left


def _clean(ref, width):
    block = ref[...]
    return jnp.where(_lane_valid(block.shape, width), block, jnp.zeros_like(block))


def _head_part(block, head):
    lane = lax.broadcasted_iota(jnp.int32, block.shape, 1)
    keep = (lane < HD) if head == 0 else (lane >= HD)
    return jnp.where(keep, block, jnp.zeros_like(block))


def _diag_mask(keys, rows, first):
    key_at = lax.broadcasted_iota(jnp.int32, (keys, rows), 0)
    row_at = lax.broadcasted_iota(jnp.int32, (keys, rows), 1) + first
    return key_at <= row_at


def forward_kernel(pos_ref, q_ref, k_ref, v_ref, ctx_ref, ctx_t_ref, lse_ref, kc_ref, vt_ref, *, span, width):
    pos = pos_ref[0]
    block = min(256, span)
    queries = _clean(q_ref, width)
    kc_ref[...] = _clean(k_ref, width)
    length = k_ref.shape[0]
    for j in range(length // span):
        vt_ref[j] = _clean(v_ref.at[pl.ds(j * span, span), :], width).T
    chains = []
    for head in range(2):
        part = _head_part(queries, head)
        for at in range(0, span, block):
            chains.append((part[at : at + block], at))

    def update(state, scores, vt):
        peak, total, acc = state
        top = jnp.maximum(peak, jnp.max(scores, axis=0, keepdims=True))
        fade = jnp.exp(peak - top)
        expons = jnp.exp(scores - top)
        total = total * fade + jnp.sum(expons, axis=0, keepdims=True)
        acc = acc * fade + _nn(vt, expons.astype(jnp.bfloat16))
        return top, total, acc

    states = []
    own_vt = vt_ref[pos]
    for part, at in chains:
        keys = at + block
        own_k = kc_ref[pl.ds(pl.multiple_of(pos * span, span), keys), :]
        scores = jnp.where(_diag_mask(keys, block, at), _nt(own_k, part), NEG)
        peak = jnp.max(scores, axis=0, keepdims=True)
        expons = jnp.exp(scores - peak)
        total = jnp.sum(expons, axis=0, keepdims=True)
        acc = _nn(own_vt[:, :keys], expons.astype(jnp.bfloat16))
        states.append((peak, total, acc))

    def past(j, states):
        key_block = kc_ref[pl.ds(pl.multiple_of(j * span, span), span), :]
        vt = vt_ref[j]
        return tuple(
            update(state, _nt(key_block, part), vt) for state, (part, _) in zip(states, chains)
        )

    states = lax.fori_loop(0, pos, past, tuple(states))
    per_head = len(chains) // 2
    for i in range(per_head):
        at = i * block
        (peak0, total0, acc0), (peak1, total1, acc1) = states[i], states[per_head + i]
        row = lax.broadcasted_iota(jnp.int32, acc0.shape, 0)
        both = jnp.where(row < HD, acc0 / total0, acc1 / total1)
        ctx_ref[at : at + block, :] = both.T.astype(ctx_ref.dtype)
        ctx_t_ref[:, at : at + block] = both.astype(ctx_t_ref.dtype)
        lse_ref[0, 0:1, at : at + block] = peak0 + jnp.log(total0)
        lse_ref[0, 1:2, at : at + block] = peak1 + jnp.log(total1)


def backward_kernel(pos_ref, q_ref, k_ref, v_ref, g_ref, ctx_ref, lse_ref, dq_ref, dk_ref, dv_ref,
                    kc_ref, vc_ref, kt_ref, dk_acc, dv_acc, *, span, width):
    pos = pos_ref[0]
    block = min(256, span)
    queries = _clean(q_ref, width)
    grads = _clean(g_ref, width)
    context = _clean(ctx_ref, width)
    kc_ref[...] = _clean(k_ref, width)
    vc_ref[...] = _clean(v_ref, width)
    length = k_ref.shape[0]
    for j in range(length // span):
        kt_ref[j] = kc_ref[pl.ds(j * span, span), :].T
    dk_acc[...] = jnp.zeros_like(dk_acc)
    dv_acc[...] = jnp.zeros_like(dv_acc)
    product = (grads.astype(jnp.float32) * context.astype(jnp.float32)).T
    chains = []
    for head in range(2):
        q_part = _head_part(queries, head)
        g_part = _head_part(grads, head)
        inner = jnp.sum(product[head * HD : (head + 1) * HD], axis=0, keepdims=True)
        for at in range(0, span, block):
            chains.append((
                q_part[at : at + block], g_part[at : at + block], inner[:, at : at + block],
                lse_ref[0, head : head + 1, at : at + block], at,
            ))

    def piece(chain, key_block, value_block, kt, masked):
        q_part, g_part, inner, lse, at = chain
        scores = _nt(key_block, q_part)
        if masked:
            scores = jnp.where(_diag_mask(key_block.shape[0], q_part.shape[0], at), scores, NEG)
        probs = jnp.exp(scores - lse)
        grad_probs = _nt(value_block, g_part)
        grad_scores = (probs * (grad_probs - inner)).astype(jnp.bfloat16)
        dq = _nn(kt, grad_scores)
        dk = _nn(grad_scores, q_part)
        dv = _nn(probs.astype(jnp.bfloat16), g_part)
        return dq, dk, dv

    start = pl.multiple_of(pos * span, span)
    own_kt = kt_ref[pos]
    dqs = []
    for chain in chains:
        keys = chain[4] + block
        where = pl.ds(start, keys)
        dq, dk, dv = piece(chain, kc_ref[where, :], vc_ref[where, :], own_kt[:, :keys], True)
        dk_acc[where, :] += dk
        dv_acc[where, :] += dv
        dqs.append(dq)

    def past(j, dqs):
        where = pl.ds(pl.multiple_of(j * span, span), span)
        key_block, value_block, kt = kc_ref[where, :], vc_ref[where, :], kt_ref[j]
        out, dk_sum, dv_sum = [], None, None
        for chain, dq_old in zip(chains, dqs):
            dq, dk, dv = piece(chain, key_block, value_block, kt, False)
            dk_sum = dk if dk_sum is None else dk_sum + dk
            dv_sum = dv if dv_sum is None else dv_sum + dv
            out.append(dq_old + dq)
        dk_acc[where, :] = dk_sum
        dv_acc[where, :] = dv_sum
        return tuple(out)

    dqs = lax.fori_loop(0, pos, past, tuple(dqs))
    per_head = len(chains) // 2
    for i in range(per_head):
        at = i * block
        row = lax.broadcasted_iota(jnp.int32, dqs[0].shape, 0)
        both = jnp.where(row < HD, dqs[i], dqs[per_head + i]) * SCALING
        dq_ref[at : at + block, :] = both.T.astype(dq_ref.dtype)
    dk_ref[...] = dk_acc[...].astype(dk_ref.dtype)
    dv_ref[...] = dv_acc[...].astype(dv_ref.dtype)


def attention_forward(position, queries, keys, values, seqs, span):
    rows, width = queries.shape
    length = keys.shape[0] // seqs
    pairs = pl.cdiv(width, LANES)
    own = pl.BlockSpec((span, LANES), lambda s, h, p: (s, h))
    whole = pl.BlockSpec((length, LANES), lambda s, h, p: (s, h))
    lse = pl.BlockSpec((1, 2, span), lambda s, h, p: (s * pairs + h, 0, 0))
    return pl.pallas_call(
        functools.partial(forward_kernel, span=span, width=width),
        grid_spec=pltpu.PrefetchScalarGridSpec(
            num_scalar_prefetch=1,
            grid=(seqs, pairs),
            in_specs=[own, whole, whole],
            out_specs=[own, pl.BlockSpec((LANES, span), lambda s, h, p: (h, s)), lse],
            scratch_shapes=[
                pltpu.VMEM((length, LANES), jnp.bfloat16),
                pltpu.VMEM((length // span, LANES, span), jnp.bfloat16),
            ],
        ),
        out_shape=[
            jax.ShapeDtypeStruct((rows, width), jnp.bfloat16),
            jax.ShapeDtypeStruct((width, rows), jnp.bfloat16),
            jax.ShapeDtypeStruct((seqs * pairs, 2, span), jnp.float32),
        ],
        compiler_params=pltpu.CompilerParams(vmem_limit_bytes=48 * 1024 * 1024),
        cost_estimate=pl.CostEstimate(flops=4 * rows * length * width * 2, bytes_accessed=8 * rows * width * 2, transcendentals=rows * length * 17),
        name="attention_forward",
    )(position, queries, keys, values)


def attention_backward(position, queries, keys, values, grads, context, lse_rows, seqs, span):
    rows, width = queries.shape
    length = keys.shape[0] // seqs
    pairs = pl.cdiv(width, LANES)
    own = pl.BlockSpec((span, LANES), lambda s, h, p: (s, h))
    whole = pl.BlockSpec((length, LANES), lambda s, h, p: (s, h))
    lse = pl.BlockSpec((1, 2, span), lambda s, h, p: (s * pairs + h, 0, 0))
    return pl.pallas_call(
        functools.partial(backward_kernel, span=span, width=width),
        grid_spec=pltpu.PrefetchScalarGridSpec(
            num_scalar_prefetch=1,
            grid=(seqs, pairs),
            in_specs=[own, whole, whole, own, own, lse],
            out_specs=[own, whole, whole],
            scratch_shapes=[
                pltpu.VMEM((length, LANES), jnp.bfloat16),
                pltpu.VMEM((length, LANES), jnp.bfloat16),
                pltpu.VMEM((length // span, LANES, span), jnp.bfloat16),
                pltpu.VMEM((length, LANES), jnp.float32),
                pltpu.VMEM((length, LANES), jnp.float32),
            ],
        ),
        out_shape=[
            jax.ShapeDtypeStruct((rows, width), jnp.bfloat16),
            jax.ShapeDtypeStruct(keys.shape, jnp.bfloat16),
            jax.ShapeDtypeStruct(keys.shape, jnp.bfloat16),
        ],
        compiler_params=pltpu.CompilerParams(vmem_limit_bytes=48 * 1024 * 1024),
        cost_estimate=pl.CostEstimate(flops=10 * rows * length * width * 2, bytes_accessed=12 * rows * width * 2, transcendentals=rows * length * 17),
        name="attention_backward",
    )(position, queries, keys, values, grads, context, lse_rows)


EPSILON = 1e-05
CORE_BIT = 1


def centred(values):
    average = jnp.mean(values, axis=-1, keepdims=True)
    off = values - average
    rstd = lax.rsqrt(jnp.mean(off * off, axis=-1, keepdims=True) + EPSILON)
    return off * rstd, rstd


def norm_pull(grad, unit, rstd, gain):
    scaled = grad * gain
    first = jnp.mean(scaled, axis=-1, keepdims=True)
    second = jnp.mean(scaled * unit, axis=-1, keepdims=True)
    return rstd * (scaled - first - unit * second)


def gelu_parts(values):
    square = values * values
    tanh = jnp.tanh(0.7978845608 * values * (1.0 + 0.044715 * square))
    half = 0.5 * (1.0 + tanh)
    slope = half + 0.5 * values * (1.0 - tanh * tanh) * (
        0.7978845608 * (1.0 + 3.0 * 0.044715 * square)
    )
    return values * half, slope


def dot(left, right):
    return jnp.dot(left, right, preferred_element_type=jnp.float32)


def dot_nt(left, right):
    return lax.dot_general(
        left, right, (((1,), (1,)), ((), ())), preferred_element_type=jnp.float32
    )


def dot_tn(left, right):
    return lax.dot_general(
        left, right, (((0,), (0,)), ((), ())), preferred_element_type=jnp.float32
    )


def low(values):
    return values.astype(jnp.bfloat16)


def swap(values, bit):
    size = lax.axis_size("replica")
    return lax.ppermute(values, "replica", [(i, i ^ bit) for i in range(size)])


def cross(values):
    return lax.ppermute(values, "shard", [(0, 1), (1, 0)])


def has_bit(bit):
    return (lax.axis_index("replica") & bit) != 0


def choose(flag, left, right):
    return jnp.where(flag, left, right)


def in_order(bit, mine, other):
    flag = has_bit(bit)
    return jnp.concatenate([choose(flag, other, mine), choose(flag, mine, other)], axis=0)


def both_halves(weight, got):
    first = lax.axis_index("shard") == 0
    return jnp.concatenate([choose(first, weight, got), choose(first, got, weight)], axis=0)


def all_bits():
    bits, bit = [], 2
    while bit < lax.axis_size("replica"):
        bits.append(bit)
        bit *= 2
    return bits


def halves(values):
    rows = values.shape[0]
    size = -(-rows // 16) * 8
    return values[:size], values[rows - size :]


def reduce_rest(values, bits):
    stack = []
    for bit in bits[:-1]:
        lower, upper = halves(values)
        flag = has_bit(bit)
        sent = swap(choose(flag, lower, upper), bit)
        stack.append((bit, values.shape[0]))
        values = low(choose(flag, upper, lower).astype(jnp.float32) + sent.astype(jnp.float32))
    values = low(values.astype(jnp.float32) + swap(values, bits[-1]).astype(jnp.float32))
    for bit, rows in stack[::-1]:
        both = in_order(bit, values, swap(values, bit))
        size = values.shape[0]
        if 2 * size != rows:
            both = jnp.concatenate([both[: rows - size], both[size:]], axis=0)
        values = both
    return values


def columns_of(values, axis, index):
    size = values.shape[axis] // 2
    low_part = lax.slice_in_dim(values, 0, size, axis=axis)
    high_part = lax.slice_in_dim(values, size, 2 * size, axis=axis)
    return choose(index == 0, low_part, high_part)


VMEM_LIMIT = 60 * 1024 * 1024
CHUNK = 256


def _vmem(count):
    return [pl.BlockSpec(memory_space=pltpu.VMEM)] * count


def _call(kernel, name, in_specs, out_shapes, scratch, flops, moved):
    return pl.pallas_call(
        kernel,
        grid_spec=pltpu.PrefetchScalarGridSpec(
            num_scalar_prefetch=1, grid=(1,), in_specs=in_specs,
            out_specs=[pl.BlockSpec(memory_space=pltpu.VMEM)] * len(out_shapes),
            scratch_shapes=scratch,
        ),
        out_shape=out_shapes,
        compiler_params=pltpu.CompilerParams(vmem_limit_bytes=VMEM_LIMIT),
        cost_estimate=pl.CostEstimate(flops=flops, bytes_accessed=moved, transcendentals=0),
        name=name,
    )


def _fetch(own_ref, got_ref, full_ref, sems, pos, at, width):
    rows = own_ref.shape[0]
    cols = pl.ds(at, width)
    mine = pl.ds(pl.multiple_of(pos * rows, 16), rows)
    theirs = pl.ds(pl.multiple_of((1 - pos) * rows, 16), rows)
    return (
        pltpu.make_async_copy(own_ref.at[:, cols], full_ref.at[mine, cols], sems.at[0]),
        pltpu.make_async_copy(got_ref.at[:, cols], full_ref.at[theirs, cols], sems.at[1]),
    )


def up_kernel(pos_ref, nt_ref, bias_ref, own_ref, got_ref, act_ref, slope_ref, full_ref, sems):
    pos = pos_ref[0]
    units = own_ref.shape[1]
    count = units // CHUNK
    copies = [_fetch(own_ref, got_ref, full_ref, sems.at[j], pos, j * CHUNK, CHUNK) for j in range(count)]
    for pair in copies:
        for copy in pair:
            copy.start()
    normed = nt_ref[...]
    early = min(3, count)
    for j in range(early):
        for copy in copies[j]:
            copy.wait()

    for j in range(count):
        if j == early:
            for later in copies[early:]:
                for copy in later:
                    copy.wait()
        cols = pl.ds(j * CHUNK, CHUNK)
        hidden = _nn(normed, full_ref[:, cols]) + bias_ref[:, cols]
        value, slope = gelu_parts(hidden)
        value = value.astype(jnp.bfloat16)
        act_ref[:, cols] = value
        slope_ref[:, cols] = slope.astype(jnp.bfloat16)


def mlp_up(spot, normed, bias, own, got):
    rows, width = normed.shape
    units = own.shape[1]
    any_spec = pl.BlockSpec(memory_space=pl.ANY)
    return _call(
        up_kernel, "mlp_up", _vmem(2) + [any_spec] * 2,
        [
            jax.ShapeDtypeStruct((rows, units), jnp.bfloat16),
            jax.ShapeDtypeStruct((rows, units), jnp.bfloat16),
        ],
        [pltpu.VMEM((width, units), jnp.bfloat16), pltpu.SemaphoreType.DMA((units // CHUNK, 2))],
        2 * rows * width * units, 2 * units * (width + 3 * rows),
    )(spot, normed, bias, own, got)


def down_kernel(pos_ref, act_ref, own_ref, got_ref, middle_ref, bias_ref, out_ref):
    pos = pos_ref[0]
    half = own_ref.shape[1]
    mine = pl.ds(pl.multiple_of(pos * half, 128), half)
    theirs = pl.ds(pl.multiple_of((1 - pos) * half, 128), half)
    total = _nt(own_ref[...], act_ref[:, mine]) + _nt(got_ref[...], act_ref[:, theirs])
    out_ref[...] = (middle_ref[...] + total + bias_ref[...]).astype(out_ref.dtype)


def mlp_down(spot, active, own, got, middle, bias):
    width, rows = middle.shape
    half = own.shape[1]
    tile = width // 4
    return pl.pallas_call(
        down_kernel,
        grid_spec=pltpu.PrefetchScalarGridSpec(
            num_scalar_prefetch=1, grid=(width // tile,),
            in_specs=[
                pl.BlockSpec((rows, 2 * half), lambda i, p: (0, 0)),
                pl.BlockSpec((tile, half), lambda i, p: (i, 0)),
                pl.BlockSpec((tile, half), lambda i, p: (i, 0)),
                pl.BlockSpec((tile, rows), lambda i, p: (i, 0)),
                pl.BlockSpec((tile, 1), lambda i, p: (i, 0)),
            ],
            out_specs=pl.BlockSpec((tile, rows), lambda i, p: (i, 0)),
        ),
        out_shape=jax.ShapeDtypeStruct((width, rows), jnp.bfloat16),
        compiler_params=pltpu.CompilerParams(vmem_limit_bytes=VMEM_LIMIT),
        cost_estimate=pl.CostEstimate(flops=4 * rows * width * half, bytes_accessed=4 * half * (width + rows), transcendentals=0),
        name="mlp_down",
    )(spot, active, own, got, middle, bias)


def back_kernel(pos_ref, grad_ref, slope_ref, down_own, down_got, up_own, up_got,
                hidden_ref, normed_ref, sum_ref, down_full, up_full, sems):
    pos = pos_ref[0]
    half = down_own.shape[1]
    units = up_own.shape[1]
    mine = pl.ds(pl.multiple_of(pos * half, 128), half)
    theirs = pl.ds(pl.multiple_of((1 - pos) * half, 128), half)
    first = pltpu.make_async_copy(down_own, down_full.at[:, mine], sems.at[0])
    second = pltpu.make_async_copy(down_got, down_full.at[:, theirs], sems.at[1])
    first.start()
    second.start()
    rows_up = up_own.shape[0]
    third = pltpu.make_async_copy(up_own, up_full.at[pl.ds(pl.multiple_of(pos * rows_up, 16), rows_up), :], sems.at[2])
    fourth = pltpu.make_async_copy(up_got, up_full.at[pl.ds(pl.multiple_of((1 - pos) * rows_up, 16), rows_up), :], sems.at[3])
    third.start()
    fourth.start()
    first.wait()
    second.wait()
    grad = grad_ref[...]
    for j in range(units // CHUNK):
        cols = pl.ds(j * CHUNK, CHUNK)
        active = _nn(grad, down_full[:, cols])
        hidden = (active * slope_ref[:, cols].astype(jnp.float32)).astype(jnp.bfloat16)
        hidden_ref[:, cols] = hidden
        sum_ref[:, cols] = jnp.sum(hidden.astype(jnp.float32), axis=0, keepdims=True)
    third.wait()
    fourth.wait()
    hidden = hidden_ref[...]
    for at in range(0, rows_up * 2, CHUNK):
        size = min(CHUNK, rows_up * 2 - at)
        normed_ref[:, at : at + size] = _nt(hidden, up_full[at : at + size, :])


def mlp_back(spot, grad, slope, down_own, down_got, up_own, up_got):
    rows, width = grad.shape
    units = up_own.shape[1]
    any_spec = pl.BlockSpec(memory_space=pl.ANY)
    return _call(
        back_kernel, "mlp_back", _vmem(2) + [any_spec] * 4,
        [
            jax.ShapeDtypeStruct((rows, units), jnp.bfloat16),
            jax.ShapeDtypeStruct((rows, width), jnp.float32),
            jax.ShapeDtypeStruct((1, units), jnp.float32),
        ],
        [
            pltpu.VMEM((width, units), jnp.bfloat16),
            pltpu.VMEM((width, units), jnp.bfloat16),
            pltpu.SemaphoreType.DMA((4,)),
        ],
        4 * rows * width * units, 4 * units * (width + rows),
    )(spot, grad, slope, down_own, down_got, up_own, up_got)


def weight_kernel(pos_ref, left_own, left_sib, right_own, right_sib, give_ref, keep_ref, total_ref):
    pos = pos_ref[0]
    _, rows, tokens = left_own.shape
    own = left_own[...].reshape(2 * rows, tokens)
    sib = left_sib[...].reshape(2 * rows, tokens)
    total = _nn(own, right_own[...]) + _nn(sib, right_sib[...])
    total_ref[...] = total.astype(total_ref.dtype).reshape(total_ref.shape)
    give_ref[...] = total_ref[1 - pos]
    keep_ref[...] = total_ref[pos]


def weight_grads(spot, left_own, left_sib, right_own, right_sib, tile_rows, tile_cols, name):
    _, rows, tokens = left_own.shape
    columns = right_own.shape[1]
    left = pl.BlockSpec((2, tile_rows, tokens), lambda i, j, p: (0, i, 0))
    right = pl.BlockSpec((tokens, tile_cols), lambda i, j, p: (0, j))
    out = pl.BlockSpec((tile_rows, tile_cols), lambda i, j, p: (i, j))
    return pl.pallas_call(
        weight_kernel,
        grid_spec=pltpu.PrefetchScalarGridSpec(
            num_scalar_prefetch=1, grid=(rows // tile_rows, pl.cdiv(columns, tile_cols)),
            in_specs=[left, left, right, right], out_specs=[out, out],
            scratch_shapes=[pltpu.VMEM((2, tile_rows, tile_cols), jnp.bfloat16)],
        ),
        out_shape=[jax.ShapeDtypeStruct((rows, columns), jnp.bfloat16)] * 2,
        compiler_params=pltpu.CompilerParams(vmem_limit_bytes=VMEM_LIMIT),
        cost_estimate=pl.CostEstimate(flops=8 * rows * tokens * columns, bytes_accessed=4 * rows * columns + 4 * tokens * columns, transcendentals=0),
        name=name,
    )(spot, left_own, left_sib, right_own, right_sib)


def turned_kernel(pos_ref, left_own, left_sib, right_own, right_sib, give_ref, keep_ref):
    total = _nn(left_own[...], right_own[...]) + _nn(left_sib[...], right_sib[...])
    total = total.astype(give_ref.dtype)

    @pl.when(pl.program_id(0) == 0)
    def _():
        give_ref[...] = total

    @pl.when(pl.program_id(0) == 1)
    def _():
        keep_ref[...] = total


def turned_weight_grads(spot, left_own, left_sib, right_own, right_sib, tile_rows, name):
    rows, tokens = left_own.shape
    columns = right_own.shape[1] // 2
    last = rows // tile_rows - 1
    left = pl.BlockSpec((tile_rows, tokens), lambda i, j, p: (j, 0))
    right = pl.BlockSpec((tokens, columns), lambda i, j, p: (0, jnp.where(i == 0, 1 - p[0], p[0])))
    return pl.pallas_call(
        turned_kernel,
        grid_spec=pltpu.PrefetchScalarGridSpec(
            num_scalar_prefetch=1, grid=(2, last + 1),
            in_specs=[left, left, right, right],
            out_specs=[
                pl.BlockSpec((tile_rows, columns), lambda i, j, p: (jnp.where(i == 0, j, last), 0)),
                pl.BlockSpec((tile_rows, columns), lambda i, j, p: (jnp.where(i == 0, 0, j), 0)),
            ],
        ),
        out_shape=[jax.ShapeDtypeStruct((rows, columns), jnp.bfloat16)] * 2,
        compiler_params=pltpu.CompilerParams(vmem_limit_bytes=VMEM_LIMIT),
        cost_estimate=pl.CostEstimate(flops=8 * rows * tokens * columns, bytes_accessed=4 * rows * columns + 8 * tokens * columns, transcendentals=0),
        name=name,
    )(spot, left_own, left_sib, right_own, right_sib)


def qkv_weight_kernel(pos_ref, left_own, left_sib, q_own, q_sib, k_own, k_sib, v_own, v_sib,
                      give_ref, keep_ref, total_ref):
    pos = pos_ref[0]
    _, rows, length = left_own.shape
    span, width = q_own.shape
    mine = pl.ds(pl.multiple_of(pos * span, 128), span)

    def rows_of(ref, cols):
        return ref[:, :, cols].reshape(2 * rows, -1)

    whole = pl.ds(0, length)
    for at, cols, own, sib in ((0, mine, q_own, q_sib), (1, whole, k_own, k_sib), (2, whole, v_own, v_sib)):
        total = _nn(rows_of(left_own, cols), own[...]) + _nn(rows_of(left_sib, cols), sib[...])
        total_ref[...] = total.astype(total_ref.dtype).reshape(total_ref.shape)
        give_ref[:, at * width : (at + 1) * width] = total_ref[1 - pos]
        keep_ref[:, at * width : (at + 1) * width] = total_ref[pos]


def qkv_weight_grads(spot, left_own, left_sib, *rights):
    rows = left_own.shape[1]
    length = left_own.shape[2]
    width = rights[0].shape[1]
    return _call(
        qkv_weight_kernel, "qkv_weight_grads", _vmem(8),
        [jax.ShapeDtypeStruct((rows, 3 * width), jnp.bfloat16)] * 2,
        [pltpu.VMEM((2, rows, width), jnp.bfloat16)],
        8 * rows * width * length * 5 // 2, 2 * (rows * width * 6 + 10 * length // 2 * width),
    )(spot, left_own, left_sib, *rights)


def input_kernel(pos_ref, wq_ref, wk_ref, wv_ref, gq_ref, gk_ref, gv_ref, mine_ref, theirs_ref):
    pos = pos_ref[0]
    span = gq_ref.shape[0]
    mine = pl.ds(pl.multiple_of(pos * span, 16), span)
    theirs = pl.ds(pl.multiple_of((1 - pos) * span, 16), span)
    wk, wv = wk_ref[...], wv_ref[...]
    theirs_ref[...] = (_nt(wk, gk_ref[theirs, :]) + _nt(wv, gv_ref[theirs, :])).astype(theirs_ref.dtype)
    mine_ref[...] = _nt(wq_ref[...], gq_ref[...]) + _nt(wk, gk_ref[mine, :]) + _nt(wv, gv_ref[mine, :])


def input_grads(spot, wq, wk, wv, gq, gk, gv):
    span, width = gq.shape
    return _call(
        input_kernel, "input_grads", _vmem(6),
        [
            jax.ShapeDtypeStruct((width, span), jnp.float32),
            jax.ShapeDtypeStruct((width, span), jnp.bfloat16),
        ],
        [], 10 * span * width * width, 2 * (3 * width * width + 8 * span * width),
    )(spot, wq, wk, wv, gq, gk, gv)


def tie(values, *earlier):
    return lax.optimization_barrier((values, *earlier))[0]


def row_sum(values):
    return jnp.sum(values.astype(jnp.float32), axis=0)


def pick(values, index, axis):
    return lax.dynamic_index_in_dim(values, index, axis, keepdims=False)


def plus(left, right):
    return low(left.astype(jnp.float32) + right.astype(jnp.float32))


def total_of(packed):
    position = lax.axis_index("shard")
    kept = pick(packed, position, 0) + cross(pick(packed, 1 - position, 0))
    bit = 1
    while bit < lax.axis_size("replica"):
        kept = kept + swap(kept, bit)
        bit *= 2
    return kept


def spread(weight, bits):
    rows = weight.shape[0]
    count = 2 ** len(bits)
    size = -(-rows // (8 * count)) * 8
    index = jnp.int32(0)
    for bit in bits:
        index = index * 2 + has_bit(bit).astype(jnp.int32)
    piece = lax.dynamic_slice_in_dim(weight, jnp.minimum(index * size, rows - size), size, axis=0)
    got = yield cross(piece), piece
    for bit in bits[::-1]:
        other = yield swap(got, bit), got
        got = in_order(bit, got, other)
    extra = count * size - rows
    if extra:
        got = jnp.concatenate([got[: (count - 1) * size], got[(count - 1) * size + extra :]], axis=0)
    return got


def reduced(keep, give, bits):
    got = yield cross(give), give
    values = plus(keep, got)
    stack = []
    for bit in bits[:-1]:
        lower, upper = halves(values)
        flag = has_bit(bit)
        got = yield swap(choose(flag, lower, upper), bit), values
        stack.append((bit, values.shape[0]))
        values = plus(choose(flag, upper, lower), got)
    got = yield swap(values, bits[-1]), values
    values = plus(values, got)
    for bit, rows in stack[::-1]:
        got = yield swap(values, bit), values
        both = in_order(bit, values, got)
        size = values.shape[0]
        if 2 * size != rows:
            both = jnp.concatenate([both[: rows - size], both[size:]], axis=0)
        values = both
    got = yield swap(values, CORE_BIT), values
    return in_order(CORE_BIT, values, got).astype(jnp.float32)


class Steps:
    def __init__(self, chain):
        self.chain = chain
        self.got, self.latest = next(chain)

    def step(self, *gates):
        got = tie(self.got, *gates) if gates else self.got
        self.got, self.latest = self.chain.send(got)

    def finish(self):
        while True:
            try:
                self.step()
            except StopIteration as end:
                return end.value


def centred_down(values):
    off = values - jnp.mean(values, axis=0, keepdims=True)
    rstd = lax.rsqrt(jnp.mean(off * off, axis=0, keepdims=True) + EPSILON)
    return off * rstd, rstd


def on_device_pair(
    tokens, qkv_weight, out_weight, up_weight, down_weight, attn_gain, attn_shift, query_bias,
    value_bias, out_bias, mlp_gain, mlp_shift, up_bias, down_bias, cotangent,
):
    _, span, width = tokens.shape
    position = lax.axis_index("shard")
    spot = position.astype(jnp.int32).reshape(1)
    core = lax.axis_index("replica") & CORE_BIT
    bits = all_bits()
    fast_bits = [CORE_BIT] + bits[:2]
    turned_bits = [CORE_BIT] + bits[:2][::-1]
    first = position == 0

    own_turned = tokens.reshape(span, width).T
    down_turned = down_weight.T
    singles = (attn_gain, attn_shift, query_bias, value_bias, out_bias, mlp_gain, mlp_shift, down_bias)
    flat_vectors = jnp.concatenate(
        [item.reshape(1, -1) for item in singles] + [up_bias.reshape(-1, singles[0].shape[0])], axis=0
    )
    way_qkv = Steps(spread(qkv_weight, fast_bits))
    other_vectors = cross(flat_vectors)
    way_out = Steps(spread(out_weight, turned_bits))
    other_turned = cross(tie(own_turned, way_qkv.got))
    way_qkv.step()
    way_out.step()
    way_up = Steps(spread(tie(up_weight, other_turned), turned_bits))
    way_down = Steps(spread(tie(down_turned, way_up.got), turned_bits))
    grad_turned = cotangent.reshape(span, width).T
    grad_out = grad_turned.T
    grad_halves = grad_turned.reshape(2, width // 2, span)
    grad_left = pick(grad_halves, core, 0), swap(pick(grad_halves, 1 - core, 0), CORE_BIT)

    lower = choose(first, flat_vectors, other_vectors).astype(jnp.float32)
    upper = choose(first, other_vectors, flat_vectors).astype(jnp.float32)
    both = jnp.concatenate([lower, upper], axis=1)
    (gain_first, shift_first, bias_query, bias_value, bias_out, gain_second, shift_second,
     bias_down) = (both[i] for i in range(8))
    bias_up = jnp.concatenate([lower[8:].reshape(1, -1), upper[8:].reshape(1, -1)], axis=1)

    all_turned = jnp.concatenate(
        [choose(first, own_turned, other_turned), choose(first, other_turned, own_turned)], axis=1
    )
    unit_all, _ = centred_down(all_turned.astype(jnp.float32))
    normed_turned = low(unit_all * gain_first[:, None] + shift_first[:, None])
    normed_all = normed_turned.T
    normed = lax.dynamic_slice_in_dim(normed_all, position * span, span, axis=0)

    def for_cores(turned):
        parts = turned.reshape(2, 2, turned.shape[0] // 4, turned.shape[1])
        return pick(parts, core, 1), swap(pick(parts, 1 - core, 1), CORE_BIT)

    way_up.step(normed_all)
    full_qkv = both_halves(qkv_weight, way_qkv.finish())
    full_q, full_k, full_v = (full_qkv[:, i * width : (i + 1) * width] for i in range(3))
    full_out = both_halves(out_weight, way_out.finish())
    normed_all = tie(normed_all, way_up.latest)
    keys = low(dot(normed_all, full_k))
    values = low(dot(normed_all, full_v) + bias_value)
    queries = low(low(dot(normed, full_q) + bias_query) * SCALING)
    way_up.step(keys, values, queries)
    way_down.step(keys, values, queries)
    queries = tie(queries, way_up.latest, way_down.latest, full_out)
    context, context_t, lse = attention_forward(spot, queries, keys, values, 1, span)
    way_up.step(context)
    way_down.step(context)
    context = tie(context, way_up.latest, way_down.latest)
    normed_left = for_cores(normed_turned)
    flat = own_turned.T.astype(jnp.float32)
    middle = flat + dot(context, full_out) + bias_out
    unit_second, rstd_second = centred(middle)
    normed_two = low(unit_second * gain_second + shift_second)
    part_up = way_up.finish()
    active, slope = mlp_up(spot, normed_two, bias_up, up_weight, part_up)
    active_sib = swap(active, CORE_BIT)
    way_down.step(active)
    part_down = way_down.finish()
    block_out = mlp_down(spot, active, down_turned, part_down, middle.T, bias_down.reshape(-1, 1))

    give, keep_down = turned_weight_grads(
        spot, *grad_left, active, tie(active_sib, block_out), width // 4, "down_grads"
    )
    sum_down = Steps(reduced(keep_down, give, bits))

    grad_hidden, grad_normed_two, sum_hidden = mlp_back(
        spot, tie(grad_out, give), slope, down_turned, part_down, up_weight, part_up
    )
    hidden_sib = swap(grad_hidden, CORE_BIT)
    grad_middle = norm_pull(grad_normed_two, unit_second, rstd_second, gain_second)
    grad_middle = grad_middle + grad_out.astype(jnp.float32)
    grad_branch = low(grad_middle)
    branch_sib = swap(grad_branch, CORE_BIT)
    grad_context = low(dot_nt(grad_branch, full_out))
    two_left = for_cores(normed_two.T)
    give, keep_up = weight_grads(
        spot, *two_left, grad_hidden, hidden_sib, two_left[0].shape[1], 2 * CHUNK, "up_grads"
    )
    sum_up = Steps(reduced(keep_up, give, bits))
    context_left = for_cores(context_t)
    give_out, keep_out = weight_grads(
        spot, *context_left, grad_branch, branch_sib, context_left[0].shape[1], width, "out_grads"
    )
    sum_down.step(give, give_out, grad_context)
    grad_context = tie(grad_context, give, give_out, sum_down.latest)

    grad_q, grad_k, grad_v = attention_backward(
        spot, queries, keys, values, grad_context, context, lse, 1, span
    )
    sum_down.step(grad_q)
    rights = []
    for part in (grad_q, grad_k, grad_v):
        rights += [part, swap(part, CORE_BIT)]
    rights[0] = tie(grad_q, sum_down.latest)
    give, keep_qkv = qkv_weight_grads(spot, *normed_left, *rights)
    sum_down.step(give)
    sum_up.step(give)
    sum_qkv = Steps(reduced(keep_qkv, give, bits))

    mine, theirs = input_grads(
        spot, full_q, full_k, full_v, tie(grad_q, give, sum_down.latest, sum_up.latest), grad_k, grad_v
    )
    sum_out = Steps(reduced(keep_out, tie(give_out, mine), bits))
    grad_normed = mine + cross(theirs).astype(jnp.float32)
    unit_first, rstd_first = centred_down(own_turned.astype(jnp.float32))
    scaled = grad_normed * gain_first[:, None]
    pulled = rstd_first * (
        scaled - jnp.mean(scaled, axis=0, keepdims=True)
        - unit_first * jnp.mean(scaled * unit_first, axis=0, keepdims=True)
    )
    grad_tokens = low(pulled + grad_middle.T)

    sums = (
        jnp.sum(grad_normed * unit_first, axis=1),
        jnp.sum(grad_normed, axis=1),
        row_sum(grad_q),
        row_sum(grad_v),
        row_sum(grad_branch),
        row_sum(grad_normed_two * unit_second),
        row_sum(grad_normed_two),
        sum_hidden.reshape(-1),
        row_sum(grad_out),
    )
    packed = total_of(jnp.concatenate([item.reshape(2, -1) for item in sums], axis=1))
    outs, at = [], 0
    for item in sums:
        size = item.shape[0] // 2
        outs.append(packed[at : at + size])
        at += size

    return (
        block_out.T.reshape(1, span, width),
        grad_tokens.T.reshape(1, span, width),
        sum_qkv.finish(), sum_out.finish(), sum_up.finish(), sum_down.finish().T,
        *outs,
    )


def on_device_general(
    tokens, qkv_weight, out_weight, up_weight, down_weight, attn_gain, attn_shift, query_bias,
    value_bias, out_bias, mlp_gain, mlp_shift, up_bias, down_bias, cotangent,
):
    seqs, span, width = tokens.shape
    rows = seqs * span
    shards = lax.axis_size("shard")
    position = lax.axis_index("shard")
    core = lax.axis_index("replica") & CORE_BIT
    length = span * shards
    bits = all_bits()

    shards_of = (attn_gain, attn_shift, query_bias, value_bias, out_bias, mlp_gain, mlp_shift,
                 up_bias, down_bias)
    flat_vectors = jnp.concatenate(shards_of)
    all_vectors = lax.all_gather(flat_vectors, "shard", axis=0, tiled=False)
    vectors, at = [], 0
    for item in shards_of:
        size = item.shape[0]
        vectors.append(all_vectors[:, at : at + size].reshape(-1).astype(jnp.float32))
        at += size
    (gain_first, shift_first, bias_query, bias_value, bias_out, gain_second, shift_second, bias_up,
     bias_down) = vectors

    full_qkv, full_out, full_up, full_down = [
        lax.all_gather(item, "shard", axis=0, tiled=True)
        for item in (qkv_weight, out_weight, up_weight, down_weight)
    ]
    all_tokens = lax.all_gather(tokens, "shard", axis=1, tiled=True).reshape(-1, width)

    def own_rows(values):
        per_seq = values.reshape(seqs, length, values.shape[-1])
        return lax.dynamic_slice_in_dim(per_seq, position * span, span, axis=1).reshape(rows, -1)

    grad_out = cotangent.reshape(rows, width)
    grad_out_both = jnp.concatenate([grad_out, swap(grad_out, CORE_BIT)], axis=0)

    flat = tokens.reshape(rows, width).astype(jnp.float32)
    unit_all, rstd_all = centred(all_tokens.astype(jnp.float32))
    normed_all = low(unit_all * gain_first + shift_first)
    normed_sib = swap(normed_all, CORE_BIT)
    normed = own_rows(normed_all)
    full_q, full_k, full_v = (full_qkv[:, i * width : (i + 1) * width] for i in range(3))
    queries = low(low(dot(normed, full_q) + bias_query) * SCALING)
    keys = low(dot(normed_all, full_k))
    values = low(dot(normed_all, full_v) + bias_value)
    spot = position.astype(jnp.int32).reshape(1)
    context, context_t, lse = attention_forward(spot, queries, keys, values, seqs, span)
    context_sib = swap(context, CORE_BIT)
    middle = flat + dot(context, full_out) + bias_out
    unit_second, rstd_second = centred(middle)
    normed_two = low(unit_second * gain_second + shift_second)
    normed_two_sib = swap(normed_two, CORE_BIT)
    active_float, slope = gelu_parts(dot(normed_two, full_up) + bias_up)
    active = low(active_float)
    slope = low(slope)

    def split_rows(lhs, rhs):
        return lax.psum_scatter(low(dot_tn(lhs, rhs)), "shard", scatter_dimension=0, tiled=True)

    grouped = active.reshape(rows, shards, 2, -1)
    taken = jnp.where(core == 0, grouped[:, :, 0], grouped[:, :, 1]).reshape(rows, -1)
    given = jnp.where(core == 0, grouped[:, :, 1], grouped[:, :, 0]).reshape(rows, -1)
    active_both = jnp.concatenate([taken, swap(given, CORE_BIT)], axis=0)
    sum_down = split_rows(active_both, grad_out_both)
    sum_down = reduce_rest(sum_down, bits)
    sum_down = in_order(CORE_BIT, sum_down, swap(sum_down, CORE_BIT))

    result = middle + dot(active, full_down) + bias_down
    block_out = low(result).reshape(seqs, span, width)

    def by_columns(lhs_both, part):
        taken = columns_of(part, 1, core)
        given = columns_of(part, 1, 1 - core)
        return split_rows(lhs_both, jnp.concatenate([taken, swap(given, CORE_BIT)], axis=0))

    def join_columns(values):
        other = swap(values, CORE_BIT)
        left = choose(core == 0, values, other)
        right = choose(core == 0, other, values)
        return left, right

    grad_float = grad_out.astype(jnp.float32)
    grad_hidden = low(dot_nt(grad_out, full_down) * slope.astype(jnp.float32))
    normed_two_both = jnp.concatenate([normed_two, normed_two_sib], axis=0)
    sum_up = by_columns(normed_two_both, grad_hidden)
    sum_up = reduce_rest(sum_up, bits)
    sum_up = jnp.concatenate(join_columns(sum_up), axis=1)
    grad_normed_two = dot_nt(grad_hidden, full_up)
    grad_middle = norm_pull(grad_normed_two, unit_second, rstd_second, gain_second) + grad_float
    grad_branch = low(grad_middle)
    grad_context = low(dot_nt(grad_branch, full_out))
    context_both = jnp.concatenate([context, context_sib], axis=0)
    sum_out = by_columns(context_both, grad_branch)
    sum_out = reduce_rest(sum_out, bits)
    sum_out = jnp.concatenate(join_columns(sum_out), axis=1)

    grad_q, grad_k, grad_v = attention_backward(
        spot, queries, keys, values, grad_context, context, lse, seqs, span
    )
    normed_both = jnp.concatenate([normed_all, normed_sib], axis=0)
    own_both = jnp.concatenate([normed, own_rows(normed_sib)], axis=0)
    third = width // 2
    half_q, half_k, half_v = (
        jnp.concatenate(
            [columns_of(part, 1, core), swap(columns_of(part, 1, 1 - core), CORE_BIT)], axis=0
        )
        for part in (grad_q, grad_k, grad_v)
    )
    sum_qkv = lax.psum_scatter(
        low(jnp.concatenate(
            [dot_tn(own_both, half_q), dot_tn(normed_both, half_k), dot_tn(normed_both, half_v)],
            axis=1,
        )),
        "shard", scatter_dimension=0, tiled=True,
    )
    sum_qkv = reduce_rest(sum_qkv, bits)
    left, right = join_columns(sum_qkv)
    sum_qkv = jnp.concatenate(
        [part[:, i * third : (i + 1) * third] for i in range(3) for part in (left, right)], axis=1
    )

    from_query = dot_nt(grad_q, full_q)
    from_rest = dot_nt(grad_k, full_k) + dot_nt(grad_v, full_v)
    grad_normed = from_query + lax.psum_scatter(
        from_rest.reshape(seqs, length, width), "shard", scatter_dimension=1, tiled=True
    ).reshape(rows, width)
    unit_first, rstd_first = own_rows(unit_all), own_rows(rstd_all)
    grad_tokens = low(norm_pull(grad_normed, unit_first, rstd_first, gain_first) + grad_middle)

    def column_sum(values):
        return jnp.sum(values.astype(jnp.float32), axis=0)

    sums = (
        column_sum(grad_normed * unit_first),
        column_sum(grad_normed),
        column_sum(grad_q),
        column_sum(grad_v),
        column_sum(grad_branch),
        column_sum(grad_normed_two * unit_second),
        column_sum(grad_normed_two),
        column_sum(grad_hidden),
        column_sum(grad_float),
    )
    packed = jnp.concatenate([item.reshape(shards, -1) for item in sums], axis=1)
    packed = lax.psum(packed, ("replica", "shard"))
    packed = lax.dynamic_index_in_dim(packed, position, axis=0, keepdims=False)
    outs, at = [], 0
    for item in sums:
        size = item.shape[0] // shards
        outs.append(packed[at : at + size])
        at += size
    return (
        block_out,
        grad_tokens.reshape(seqs, span, width),
        sum_qkv.astype(jnp.float32),
        sum_out.astype(jnp.float32),
        sum_up.astype(jnp.float32),
        sum_down.astype(jnp.float32),
        *outs,
    )


def on_device(tokens, *rest):
    if lax.axis_size("shard") == 2 and lax.axis_size("replica") >= 8 and tokens.shape[0] == 1:
        return on_device_pair(tokens, *rest)
    return on_device_general(tokens, *rest)


def solution(mesh):
    vector, matrix, rows = P("shard"), P("shard", None), P("replica", "shard", None)
    return jax.shard_map(
        on_device,
        mesh=mesh,
        in_specs=(rows, *[matrix] * 4, *[vector] * 9, rows),
        out_specs=(rows, rows, *[matrix] * 4, *[vector] * 9),
        check_vma=False,
    )
```

```python
import functools
import jax
import jax.numpy as jnp
from jax import lax
from jax.experimental import pallas as pl
from jax.experimental.pallas import tpu as pltpu
from jax.sharding import PartitionSpec as P

HD = 64
SCALING = 0.125
NEG = -1e30
LANES = 128
QUICK = pl.CostEstimate(flops=1, bytes_accessed=1, transcendentals=0)


def _nt(a, b):
    return lax.dot_general(a, b, (((1,), (1,)), ((), ())), preferred_element_type=jnp.float32)


def _nn(a, b):
    return lax.dot_general(a, b, (((1,), (0,)), ((), ())), preferred_element_type=jnp.float32)


def _lane_valid(shape, width):
    left = width - pl.program_id(1) * LANES
    return lax.broadcasted_iota(jnp.int32, shape, 1) < left


def _clean(ref, width):
    block = ref[...]
    return jnp.where(_lane_valid(block.shape, width), block, jnp.zeros_like(block))


def _head_part(block, head):
    lane = lax.broadcasted_iota(jnp.int32, block.shape, 1)
    keep = (lane < HD) if head == 0 else (lane >= HD)
    return jnp.where(keep, block, jnp.zeros_like(block))


def _diag_mask(keys, rows, first):
    key_at = lax.broadcasted_iota(jnp.int32, (keys, rows), 0)
    row_at = lax.broadcasted_iota(jnp.int32, (keys, rows), 1) + first
    return key_at <= row_at


def forward_kernel(pos_ref, q_ref, k_ref, v_ref, ctx_ref, ctx_t_ref, lse_ref, kc_ref, vt_ref, *, span, width):
    pos = pos_ref[0]
    block = min(256, span)
    queries = _clean(q_ref, width)
    kc_ref[...] = _clean(k_ref, width)
    length = k_ref.shape[0]
    for j in range(length // span):
        vt_ref[j] = _clean(v_ref.at[pl.ds(j * span, span), :], width).T
    chains = []
    for head in range(2):
        part = _head_part(queries, head)
        for at in range(0, span, block):
            chains.append((part[at : at + block], at))

    def update(state, scores, vt):
        peak, total, acc = state
        top = jnp.maximum(peak, jnp.max(scores, axis=0, keepdims=True))
        fade = jnp.exp(peak - top)
        expons = jnp.exp(scores - top)
        total = total * fade + jnp.sum(expons, axis=0, keepdims=True)
        acc = acc * fade + _nn(vt, expons.astype(jnp.bfloat16))
        return top, total, acc

    states = []
    own_vt = vt_ref[pos]
    for part, at in chains:
        keys = at + block
        own_k = kc_ref[pl.ds(pl.multiple_of(pos * span, span), keys), :]
        scores = jnp.where(_diag_mask(keys, block, at), _nt(own_k, part), NEG)
        peak = jnp.max(scores, axis=0, keepdims=True)
        expons = jnp.exp(scores - peak)
        total = jnp.sum(expons, axis=0, keepdims=True)
        acc = _nn(own_vt[:, :keys], expons.astype(jnp.bfloat16))
        states.append((peak, total, acc))

    def past(j, states):
        key_block = kc_ref[pl.ds(pl.multiple_of(j * span, span), span), :]
        vt = vt_ref[j]
        return tuple(
            update(state, _nt(key_block, part), vt) for state, (part, _) in zip(states, chains)
        )

    states = lax.fori_loop(0, pos, past, tuple(states))
    per_head = len(chains) // 2
    for i in range(per_head):
        at = i * block
        (peak0, total0, acc0), (peak1, total1, acc1) = states[i], states[per_head + i]
        row = lax.broadcasted_iota(jnp.int32, acc0.shape, 0)
        both = jnp.where(row < HD, acc0 / total0, acc1 / total1)
        ctx_ref[at : at + block, :] = both.T.astype(ctx_ref.dtype)
        ctx_t_ref[:, at : at + block] = both.astype(ctx_t_ref.dtype)
        lse_ref[0, 0:1, at : at + block] = peak0 + jnp.log(total0)
        lse_ref[0, 1:2, at : at + block] = peak1 + jnp.log(total1)


def backward_kernel(pos_ref, q_ref, k_ref, v_ref, g_ref, ctx_ref, lse_ref, dq_ref, dk_ref, dv_ref,
                    kc_ref, vc_ref, kt_ref, dk_acc, dv_acc, *, span, width):
    pos = pos_ref[0]
    block = min(256, span)
    queries = _clean(q_ref, width)
    grads = _clean(g_ref, width)
    context = _clean(ctx_ref, width)
    kc_ref[...] = _clean(k_ref, width)
    vc_ref[...] = _clean(v_ref, width)
    length = k_ref.shape[0]
    for j in range(length // span):
        kt_ref[j] = kc_ref[pl.ds(j * span, span), :].T
    dk_acc[...] = jnp.zeros_like(dk_acc)
    dv_acc[...] = jnp.zeros_like(dv_acc)
    product = (grads.astype(jnp.float32) * context.astype(jnp.float32)).T
    chains = []
    for head in range(2):
        q_part = _head_part(queries, head)
        g_part = _head_part(grads, head)
        inner = jnp.sum(product[head * HD : (head + 1) * HD], axis=0, keepdims=True)
        for at in range(0, span, block):
            chains.append((
                q_part[at : at + block], g_part[at : at + block], inner[:, at : at + block],
                lse_ref[0, head : head + 1, at : at + block], at,
            ))

    def piece(chain, key_block, value_block, kt, masked):
        q_part, g_part, inner, lse, at = chain
        scores = _nt(key_block, q_part)
        if masked:
            scores = jnp.where(_diag_mask(key_block.shape[0], q_part.shape[0], at), scores, NEG)
        probs = jnp.exp(scores - lse)
        grad_probs = _nt(value_block, g_part)
        grad_scores = (probs * (grad_probs - inner)).astype(jnp.bfloat16)
        dq = _nn(kt, grad_scores)
        dk = _nn(grad_scores, q_part)
        dv = _nn(probs.astype(jnp.bfloat16), g_part)
        return dq, dk, dv

    start = pl.multiple_of(pos * span, span)
    own_kt = kt_ref[pos]
    dqs = []
    for chain in chains:
        keys = chain[4] + block
        where = pl.ds(start, keys)
        dq, dk, dv = piece(chain, kc_ref[where, :], vc_ref[where, :], own_kt[:, :keys], True)
        dk_acc[where, :] += dk
        dv_acc[where, :] += dv
        dqs.append(dq)

    def past(j, dqs):
        where = pl.ds(pl.multiple_of(j * span, span), span)
        key_block, value_block, kt = kc_ref[where, :], vc_ref[where, :], kt_ref[j]
        out, dk_sum, dv_sum = [], None, None
        for chain, dq_old in zip(chains, dqs):
            dq, dk, dv = piece(chain, key_block, value_block, kt, False)
            dk_sum = dk if dk_sum is None else dk_sum + dk
            dv_sum = dv if dv_sum is None else dv_sum + dv
            out.append(dq_old + dq)
        dk_acc[where, :] = dk_sum
        dv_acc[where, :] = dv_sum
        return tuple(out)

    dqs = lax.fori_loop(0, pos, past, tuple(dqs))
    per_head = len(chains) // 2
    for i in range(per_head):
        at = i * block
        row = lax.broadcasted_iota(jnp.int32, dqs[0].shape, 0)
        both = jnp.where(row < HD, dqs[i], dqs[per_head + i]) * SCALING
        dq_ref[at : at + block, :] = both.T.astype(dq_ref.dtype)
    dk_ref[...] = dk_acc[...].astype(dk_ref.dtype)
    dv_ref[...] = dv_acc[...].astype(dv_ref.dtype)


def attention_forward(position, queries, keys, values, seqs, span):
    rows, width = queries.shape
    length = keys.shape[0] // seqs
    pairs = pl.cdiv(width, LANES)
    own = pl.BlockSpec((span, LANES), lambda s, h, p: (s, h))
    whole = pl.BlockSpec((length, LANES), lambda s, h, p: (s, h))
    lse = pl.BlockSpec((1, 2, span), lambda s, h, p: (s * pairs + h, 0, 0))
    return pl.pallas_call(
        functools.partial(forward_kernel, span=span, width=width),
        grid_spec=pltpu.PrefetchScalarGridSpec(
            num_scalar_prefetch=1,
            grid=(seqs, pairs),
            in_specs=[own, whole, whole],
            out_specs=[own, pl.BlockSpec((LANES, span), lambda s, h, p: (h, s)), lse],
            scratch_shapes=[
                pltpu.VMEM((length, LANES), jnp.bfloat16),
                pltpu.VMEM((length // span, LANES, span), jnp.bfloat16),
            ],
        ),
        out_shape=[
            jax.ShapeDtypeStruct((rows, width), jnp.bfloat16),
            jax.ShapeDtypeStruct((width, rows), jnp.bfloat16),
            jax.ShapeDtypeStruct((seqs * pairs, 2, span), jnp.float32),
        ],
        compiler_params=pltpu.CompilerParams(vmem_limit_bytes=48 * 1024 * 1024),
        cost_estimate=QUICK,
        name="attention_forward",
    )(position, queries, keys, values)


def attention_backward(position, queries, keys, values, grads, context, lse_rows, seqs, span):
    rows, width = queries.shape
    length = keys.shape[0] // seqs
    pairs = pl.cdiv(width, LANES)
    own = pl.BlockSpec((span, LANES), lambda s, h, p: (s, h))
    whole = pl.BlockSpec((length, LANES), lambda s, h, p: (s, h))
    lse = pl.BlockSpec((1, 2, span), lambda s, h, p: (s * pairs + h, 0, 0))
    return pl.pallas_call(
        functools.partial(backward_kernel, span=span, width=width),
        grid_spec=pltpu.PrefetchScalarGridSpec(
            num_scalar_prefetch=1,
            grid=(seqs, pairs),
            in_specs=[own, whole, whole, own, own, lse],
            out_specs=[own, whole, whole],
            scratch_shapes=[
                pltpu.VMEM((length, LANES), jnp.bfloat16),
                pltpu.VMEM((length, LANES), jnp.bfloat16),
                pltpu.VMEM((length // span, LANES, span), jnp.bfloat16),
                pltpu.VMEM((length, LANES), jnp.float32),
                pltpu.VMEM((length, LANES), jnp.float32),
            ],
        ),
        out_shape=[
            jax.ShapeDtypeStruct((rows, pairs * LANES), jnp.bfloat16),
            jax.ShapeDtypeStruct((keys.shape[0], pairs * LANES), jnp.bfloat16),
            jax.ShapeDtypeStruct((keys.shape[0], pairs * LANES), jnp.bfloat16),
        ],
        compiler_params=pltpu.CompilerParams(vmem_limit_bytes=48 * 1024 * 1024),
        cost_estimate=QUICK,
        name="attention_backward",
    )(position, queries, keys, values, grads, context, lse_rows)


EPSILON = 1e-05
CORE_BIT = 1


def centred(values):
    average = jnp.mean(values, axis=-1, keepdims=True)
    off = values - average
    rstd = lax.rsqrt(jnp.mean(off * off, axis=-1, keepdims=True) + EPSILON)
    return off * rstd, rstd


def norm_pull(grad, unit, rstd, gain):
    scaled = grad * gain
    first = jnp.mean(scaled, axis=-1, keepdims=True)
    second = jnp.mean(scaled * unit, axis=-1, keepdims=True)
    return rstd * (scaled - first - unit * second)


def gelu_parts(values):
    square = values * values
    tanh = jnp.tanh(0.7978845608 * values * (1.0 + 0.044715 * square))
    half = 0.5 * (1.0 + tanh)
    slope = half + 0.5 * values * (1.0 - tanh * tanh) * (
        0.7978845608 * (1.0 + 3.0 * 0.044715 * square)
    )
    return values * half, slope


def dot(left, right):
    return jnp.dot(left, right, preferred_element_type=jnp.float32)


def dot_nt(left, right):
    return lax.dot_general(
        left, right, (((1,), (1,)), ((), ())), preferred_element_type=jnp.float32
    )


def dot_tn(left, right):
    return lax.dot_general(
        left, right, (((0,), (0,)), ((), ())), preferred_element_type=jnp.float32
    )


def low(values):
    return values.astype(jnp.bfloat16)


def swap(values, bit):
    size = lax.axis_size("replica")
    return lax.ppermute(values, "replica", [(i, i ^ bit) for i in range(size)])


def cross(values):
    return lax.ppermute(values, "shard", [(0, 1), (1, 0)])


def has_bit(bit):
    return (lax.axis_index("replica") & bit) != 0


def choose(flag, left, right):
    return jnp.where(flag, left, right)


def in_order(bit, mine, other):
    flag = has_bit(bit)
    return jnp.concatenate([choose(flag, other, mine), choose(flag, mine, other)], axis=0)


def both_halves(weight, got):
    first = lax.axis_index("shard") == 0
    return jnp.concatenate([choose(first, weight, got), choose(first, got, weight)], axis=0)


def all_bits():
    bits, bit = [], 2
    while bit < lax.axis_size("replica"):
        bits.append(bit)
        bit *= 2
    return bits


def halves(values):
    rows = values.shape[0]
    size = -(-rows // 16) * 8
    return values[:size], values[rows - size :]


def reduce_rest(values, bits):
    stack = []
    for bit in bits[:-1]:
        lower, upper = halves(values)
        flag = has_bit(bit)
        sent = swap(choose(flag, lower, upper), bit)
        stack.append((bit, values.shape[0]))
        values = low(choose(flag, upper, lower).astype(jnp.float32) + sent.astype(jnp.float32))
    values = low(values.astype(jnp.float32) + swap(values, bits[-1]).astype(jnp.float32))
    for bit, rows in stack[::-1]:
        both = in_order(bit, values, swap(values, bit))
        size = values.shape[0]
        if 2 * size != rows:
            both = jnp.concatenate([both[: rows - size], both[size:]], axis=0)
        values = both
    return values


def columns_of(values, axis, index):
    size = values.shape[axis] // 2
    low_part = lax.slice_in_dim(values, 0, size, axis=axis)
    high_part = lax.slice_in_dim(values, size, 2 * size, axis=axis)
    return choose(index == 0, low_part, high_part)


VMEM_LIMIT = 60 * 1024 * 1024
CHUNK = 256


def _vmem(count):
    return [pl.BlockSpec(memory_space=pltpu.VMEM)] * count


def _call(kernel, name, in_specs, out_shapes, scratch, flops, moved):
    return pl.pallas_call(
        kernel,
        grid_spec=pltpu.PrefetchScalarGridSpec(
            num_scalar_prefetch=1, grid=(1,), in_specs=in_specs,
            out_specs=[pl.BlockSpec(memory_space=pltpu.VMEM)] * len(out_shapes),
            scratch_shapes=scratch,
        ),
        out_shape=out_shapes,
        compiler_params=pltpu.CompilerParams(vmem_limit_bytes=VMEM_LIMIT),
        cost_estimate=QUICK,
        name=name,
    )


def _fetch(own_ref, got_ref, full_ref, sems, pos, at, width):
    rows = own_ref.shape[0]
    cols = pl.ds(at, width)
    mine = pl.ds(pl.multiple_of(pos * rows, 16), rows)
    theirs = pl.ds(pl.multiple_of((1 - pos) * rows, 16), rows)
    return (
        pltpu.make_async_copy(own_ref.at[:, cols], full_ref.at[mine, cols], sems.at[0]),
        pltpu.make_async_copy(got_ref.at[:, cols], full_ref.at[theirs, cols], sems.at[1]),
    )


def up_kernel(pos_ref, ctx_ref, out_w_ref, x_ref, vec_ref, bias_ref, own_ref, got_ref,
              act_ref, slope_ref, mid_t_ref, unit_ref, rstd_ref, nt_t_ref, nt_ref, full_ref, sems):
    pos = pos_ref[0]
    units = own_ref.shape[1]
    count = units // CHUNK
    copies = [_fetch(own_ref, got_ref, full_ref, sems.at[j], pos, j * CHUNK, CHUNK) for j in range(count)]
    for pair in copies:
        for copy in pair:
            copy.start()
    unit_ref[...] = _nn(ctx_ref[...], out_w_ref[...])
    rows = ctx_ref.shape[0]
    tile = 128
    for at in range(0, rows, tile):
        where = slice(at, at + tile)
        middle = x_ref[where, :].astype(jnp.float32) + (unit_ref[where, :] + vec_ref[0:1, :])
        unit, rstd = centred(middle)
        normed = unit * vec_ref[1:2, :] + vec_ref[2:3, :]
        unit_ref[where, :] = unit
        rstd_ref[where, :] = rstd
        mid_t_ref[:, where] = middle.T
        nt_ref[where, :] = normed.astype(jnp.bfloat16)
        nt_t_ref[:, where] = normed.T.astype(jnp.bfloat16)
    for pair in copies:
        for copy in pair:
            copy.wait()
    normed = nt_ref[...]
    for j in range(count):
        cols = pl.ds(j * CHUNK, CHUNK)
        hidden = _nn(normed, full_ref[:, cols]) + bias_ref[:, cols]
        value, slope = gelu_parts(hidden)
        act_ref[:, cols] = value.astype(jnp.bfloat16)
        slope_ref[:, cols] = slope.astype(jnp.bfloat16)


def mlp_up(spot, context, out_weight, tokens, vectors, bias, own, got):
    rows, width = tokens.shape
    units = own.shape[1]
    any_spec = pl.BlockSpec(memory_space=pl.ANY)
    return _call(
        up_kernel, "mlp_up", _vmem(5) + [any_spec] * 2,
        [
            jax.ShapeDtypeStruct((rows, units), jnp.bfloat16),
            jax.ShapeDtypeStruct((rows, units), jnp.bfloat16),
            jax.ShapeDtypeStruct((width, rows), jnp.float32),
            jax.ShapeDtypeStruct((rows, width), jnp.float32),
            jax.ShapeDtypeStruct((rows, 1), jnp.float32),
            jax.ShapeDtypeStruct((width, rows), jnp.bfloat16),
        ],
        [
            pltpu.VMEM((rows, width), jnp.bfloat16),
            pltpu.VMEM((width, units), jnp.bfloat16),
            pltpu.SemaphoreType.DMA((units // CHUNK, 2)),
        ],
        2 * rows * width * (units + width), 2 * units * (width + 2 * rows) + 18 * rows * width,
    )(spot, context, out_weight, tokens, vectors, bias, own, got)


def down_kernel(pos_ref, act_ref, own_ref, got_ref, middle_ref, bias_ref, out_ref):
    pos = pos_ref[0]
    half = own_ref.shape[1]
    mine = pl.ds(pl.multiple_of(pos * half, 128), half)
    theirs = pl.ds(pl.multiple_of((1 - pos) * half, 128), half)
    total = _nt(own_ref[...], act_ref[:, mine]) + _nt(got_ref[...], act_ref[:, theirs])
    out_ref[...] = (middle_ref[...] + total + bias_ref[...]).astype(out_ref.dtype)


def mlp_down(spot, active, own, got, middle, bias):
    width, rows = middle.shape
    half = own.shape[1]
    tile = width // 4
    return pl.pallas_call(
        down_kernel,
        grid_spec=pltpu.PrefetchScalarGridSpec(
            num_scalar_prefetch=1, grid=(width // tile,),
            in_specs=[
                pl.BlockSpec((rows, 2 * half), lambda i, p: (0, 0)),
                pl.BlockSpec((tile, half), lambda i, p: (i, 0)),
                pl.BlockSpec((tile, half), lambda i, p: (i, 0)),
                pl.BlockSpec((tile, rows), lambda i, p: (i, 0)),
                pl.BlockSpec((tile, 1), lambda i, p: (i, 0)),
            ],
            out_specs=pl.BlockSpec((tile, rows), lambda i, p: (i, 0)),
        ),
        out_shape=jax.ShapeDtypeStruct((width, rows), jnp.bfloat16),
        compiler_params=pltpu.CompilerParams(vmem_limit_bytes=VMEM_LIMIT),
        cost_estimate=QUICK,
        name="mlp_down",
    )(spot, active, own, got, middle, bias)


def back_kernel(pos_ref, grad_ref, slope_ref, unit_ref, rstd_ref, gain_ref, out_w_ref,
                down_own, down_got, up_own, up_got,
                hidden_ref, middle_ref, branch_ref, context_ref, wide_sum_ref, sum_ref,
                down_full, up_full, sems):
    pos = pos_ref[0]
    half = down_own.shape[1]
    units = up_own.shape[1]
    rows, width = grad_ref.shape
    mine = pl.ds(pl.multiple_of(pos * half, 128), half)
    theirs = pl.ds(pl.multiple_of((1 - pos) * half, 128), half)
    first = pltpu.make_async_copy(down_own, down_full.at[:, mine], sems.at[0])
    second = pltpu.make_async_copy(down_got, down_full.at[:, theirs], sems.at[1])
    first.start()
    second.start()
    rows_up = up_own.shape[0]
    third = pltpu.make_async_copy(up_own, up_full.at[pl.ds(pl.multiple_of(pos * rows_up, 16), rows_up), :], sems.at[2])
    fourth = pltpu.make_async_copy(up_got, up_full.at[pl.ds(pl.multiple_of((1 - pos) * rows_up, 16), rows_up), :], sems.at[3])
    third.start()
    fourth.start()
    first.wait()
    second.wait()
    grad = grad_ref[...]
    for j in range(units // CHUNK):
        cols = pl.ds(j * CHUNK, CHUNK)
        active = _nn(grad, down_full[:, cols])
        hidden = (active * slope_ref[:, cols].astype(jnp.float32)).astype(jnp.bfloat16)
        hidden_ref[:, cols] = hidden
        wide_sum_ref[:, cols] = jnp.sum(hidden.astype(jnp.float32), axis=0, keepdims=True)
    third.wait()
    fourth.wait()
    hidden = hidden_ref[...]
    for at in range(0, width, CHUNK):
        size = min(CHUNK, width - at)
        middle_ref[:, at : at + size] = _nt(hidden, up_full[at : at + size, :])
    sum_ref[...] = jnp.zeros_like(sum_ref)
    branch_ref[...] = jnp.zeros_like(branch_ref)
    tile = 128
    for at in range(0, rows, tile):
        where = slice(at, at + tile)
        normed = middle_ref[where, :]
        unit = unit_ref[where, :]
        out = norm_pull(normed, unit, rstd_ref[where, :], gain_ref[...])
        out = out + grad_ref[where, :].astype(jnp.float32)
        branch = out.astype(jnp.bfloat16)
        middle_ref[where, :] = out
        branch_ref[where, 0:width] = branch
        sum_ref[0:1, :] += jnp.sum(normed * unit, axis=0, keepdims=True)
        sum_ref[1:2, :] += jnp.sum(normed, axis=0, keepdims=True)
        sum_ref[2:3, :] += jnp.sum(branch.astype(jnp.float32), axis=0, keepdims=True)
    context_ref[...] = _nt(branch_ref[:, 0:width], out_w_ref[...]).astype(context_ref.dtype)


def mlp_back(spot, grad, slope, unit, rstd, gain, out_weight, down_own, down_got, up_own, up_got):
    rows, width = grad.shape
    units = up_own.shape[1]
    any_spec = pl.BlockSpec(memory_space=pl.ANY)
    return _call(
        back_kernel, "mlp_back", _vmem(6) + [any_spec] * 4,
        [
            jax.ShapeDtypeStruct((rows, units), jnp.bfloat16),
            jax.ShapeDtypeStruct((rows, width), jnp.float32),
            jax.ShapeDtypeStruct((rows, pl.cdiv(width, LANES) * LANES), jnp.bfloat16),
            jax.ShapeDtypeStruct((rows, width), jnp.bfloat16),
            jax.ShapeDtypeStruct((1, units), jnp.float32),
            jax.ShapeDtypeStruct((8, width), jnp.float32),
        ],
        [
            pltpu.VMEM((width, units), jnp.bfloat16),
            pltpu.VMEM((width, units), jnp.bfloat16),
            pltpu.SemaphoreType.DMA((4,)),
        ],
        4 * rows * width * units + 2 * rows * width * width, 4 * units * (width + rows) + 12 * rows * width,
    )(spot, grad, slope, unit, rstd, gain, out_weight, down_own, down_got, up_own, up_got)


def weight_kernel(pos_ref, left_own, left_sib, right_own, right_sib, give_ref, keep_ref, total_ref):
    pos = pos_ref[0]
    _, rows, tokens = left_own.shape
    own = left_own[...].reshape(2 * rows, tokens)
    sib = left_sib[...].reshape(2 * rows, tokens)
    total = _nn(own, right_own[...]) + _nn(sib, right_sib[...])
    total_ref[...] = total.astype(total_ref.dtype).reshape(total_ref.shape)
    give_ref[...] = total_ref[1 - pos]
    keep_ref[...] = total_ref[pos]


def weight_grads(spot, left_own, left_sib, right_own, right_sib, columns, tile_rows, tile_cols, name):
    _, rows, tokens = left_own.shape
    left = pl.BlockSpec((2, tile_rows, tokens), lambda i, j, p: (0, i, 0))
    right = pl.BlockSpec((tokens, tile_cols), lambda i, j, p: (0, j))
    out = pl.BlockSpec((tile_rows, tile_cols), lambda i, j, p: (i, j))
    return pl.pallas_call(
        weight_kernel,
        grid_spec=pltpu.PrefetchScalarGridSpec(
            num_scalar_prefetch=1, grid=(rows // tile_rows, pl.cdiv(columns, tile_cols)),
            in_specs=[left, left, right, right], out_specs=[out, out],
            scratch_shapes=[pltpu.VMEM((2, tile_rows, tile_cols), jnp.bfloat16)],
        ),
        out_shape=[jax.ShapeDtypeStruct((rows, columns), jnp.bfloat16)] * 2,
        compiler_params=pltpu.CompilerParams(vmem_limit_bytes=VMEM_LIMIT),
        cost_estimate=QUICK,
        name=name,
    )(spot, left_own, left_sib, right_own, right_sib)


def turned_kernel(pos_ref, left_own, left_sib, right_own, right_sib, give_ref, keep_ref):
    total = _nn(left_own[...], right_own[...]) + _nn(left_sib[...], right_sib[...])
    total = total.astype(give_ref.dtype)

    @pl.when(pl.program_id(0) == 0)
    def _():
        give_ref[...] = total

    @pl.when(pl.program_id(0) == 1)
    def _():
        keep_ref[...] = total


def turned_weight_grads(spot, left_own, left_sib, right_own, right_sib, tile_rows, name):
    rows, tokens = left_own.shape
    columns = right_own.shape[1] // 2
    last = rows // tile_rows - 1
    left = pl.BlockSpec((tile_rows, tokens), lambda i, j, p: (j, 0))
    right = pl.BlockSpec((tokens, columns), lambda i, j, p: (0, jnp.where(i == 0, 1 - p[0], p[0])))
    return pl.pallas_call(
        turned_kernel,
        grid_spec=pltpu.PrefetchScalarGridSpec(
            num_scalar_prefetch=1, grid=(2, last + 1),
            in_specs=[left, left, right, right],
            out_specs=[
                pl.BlockSpec((tile_rows, columns), lambda i, j, p: (jnp.where(i == 0, j, last), 0)),
                pl.BlockSpec((tile_rows, columns), lambda i, j, p: (jnp.where(i == 0, 0, j), 0)),
            ],
        ),
        out_shape=[jax.ShapeDtypeStruct((rows, columns), jnp.bfloat16)] * 2,
        compiler_params=pltpu.CompilerParams(vmem_limit_bytes=VMEM_LIMIT),
        cost_estimate=QUICK,
        name=name,
    )(spot, left_own, left_sib, right_own, right_sib)


def qkv_weight_kernel(pos_ref, left_own, left_sib, q_own, q_sib, k_own, k_sib, v_own, v_sib,
                      give_ref, keep_ref, total_ref):
    pos = pos_ref[0]
    _, rows, length = left_own.shape
    span = q_own.shape[0]
    width = total_ref.shape[2]
    mine = pl.ds(pl.multiple_of(pos * span, 128), span)

    def rows_of(ref, cols):
        return ref[:, :, cols].reshape(2 * rows, -1)

    whole = pl.ds(0, length)
    for at, cols, own, sib in ((0, mine, q_own, q_sib), (1, whole, k_own, k_sib), (2, whole, v_own, v_sib)):
        total = _nn(rows_of(left_own, cols), own[:, 0:width]) + _nn(rows_of(left_sib, cols), sib[:, 0:width])
        total_ref[...] = total.astype(total_ref.dtype).reshape(total_ref.shape)
        give_ref[:, at * width : (at + 1) * width] = total_ref[1 - pos]
        keep_ref[:, at * width : (at + 1) * width] = total_ref[pos]


def qkv_weight_grads(spot, width, left_own, left_sib, *rights):
    rows = left_own.shape[1]
    length = left_own.shape[2]
    return _call(
        qkv_weight_kernel, "qkv_weight_grads", _vmem(8),
        [jax.ShapeDtypeStruct((rows, 3 * width), jnp.bfloat16)] * 2,
        [pltpu.VMEM((2, rows, width), jnp.bfloat16)],
        8 * rows * width * length * 5 // 2, 2 * (rows * width * 6 + 10 * length // 2 * width),
    )(spot, left_own, left_sib, *rights)


def input_kernel(pos_ref, wq_ref, wk_ref, wv_ref, gq_ref, gk_ref, gv_ref, mine_ref, theirs_ref):
    pos = pos_ref[0]
    span = gq_ref.shape[0]
    cols = pl.ds(0, wq_ref.shape[1])
    mine = pl.ds(pl.multiple_of(pos * span, 16), span)
    theirs = pl.ds(pl.multiple_of((1 - pos) * span, 16), span)
    wk, wv = wk_ref[...], wv_ref[...]
    theirs_ref[...] = (_nt(wk, gk_ref[theirs, cols]) + _nt(wv, gv_ref[theirs, cols])).astype(theirs_ref.dtype)
    mine_ref[...] = (
        _nt(wq_ref[...], gq_ref[:, cols]) + _nt(wk, gk_ref[mine, cols]) + _nt(wv, gv_ref[mine, cols])
    )


def input_grads(spot, wq, wk, wv, gq, gk, gv):
    span, width = gq.shape[0], wq.shape[0]
    return _call(
        input_kernel, "input_grads", _vmem(6),
        [
            jax.ShapeDtypeStruct((width, span), jnp.float32),
            jax.ShapeDtypeStruct((width, span), jnp.bfloat16),
        ],
        [], 10 * span * width * width, 2 * (3 * width * width + 8 * span * width),
    )(spot, wq, wk, wv, gq, gk, gv)


def token_kernel(pos_ref, mine_ref, other_ref, x_ref, gain_ref, middle_ref, out_ref):
    unit, rstd = centred_down(x_ref[...].astype(jnp.float32))
    scaled = (mine_ref[...] + other_ref[...].astype(jnp.float32)) * gain_ref[...]
    pulled = rstd * (
        scaled - jnp.mean(scaled, axis=0, keepdims=True)
        - unit * jnp.mean(scaled * unit, axis=0, keepdims=True)
    )
    out_ref[...] = (pulled + middle_ref[...].T).astype(out_ref.dtype)


def token_grads(spot, mine, other, tokens, gain, middle):
    width, span = mine.shape
    tile = 128
    cols = pl.BlockSpec((width, tile), lambda i, p: (0, i))
    return pl.pallas_call(
        token_kernel,
        grid_spec=pltpu.PrefetchScalarGridSpec(
            num_scalar_prefetch=1, grid=(span // tile,),
            in_specs=[
                cols, cols, cols,
                pl.BlockSpec((width, 1), lambda i, p: (0, 0)),
                pl.BlockSpec((tile, width), lambda i, p: (i, 0)),
            ],
            out_specs=cols,
        ),
        out_shape=jax.ShapeDtypeStruct((width, span), jnp.bfloat16),
        compiler_params=pltpu.CompilerParams(vmem_limit_bytes=VMEM_LIMIT),
        cost_estimate=QUICK,
        name="token_grads",
    )(spot, mine, other, tokens, gain, middle)


TAIL = "udovquqtvdoquqvudoqvudoqvuq"


def tie(values, *earlier):
    return lax.optimization_barrier((values, *earlier))[0]


def row_sum(values):
    return jnp.sum(values.astype(jnp.float32), axis=0)


def pick(values, index, axis):
    return lax.dynamic_index_in_dim(values, index, axis, keepdims=False)


def plus(left, right):
    return low(left.astype(jnp.float32) + right.astype(jnp.float32))


def spread(weight, bits):
    rows = weight.shape[0]
    count = 2 ** len(bits)
    size = -(-rows // (8 * count)) * 8
    index = jnp.int32(0)
    for bit in bits:
        index = index * 2 + has_bit(bit).astype(jnp.int32)
    piece = lax.dynamic_slice_in_dim(weight, jnp.minimum(index * size, rows - size), size, axis=0)
    got = yield cross(piece), piece
    for bit in bits[::-1]:
        other = yield swap(got, bit), got
        flag = has_bit(bit)
        parts = lax.optimization_barrier((choose(flag, other, got), choose(flag, got, other)))
        extra = count * size - rows if bit == bits[0] else 0
        if extra:
            kept = parts[1].shape[0] - size
            parts = parts[0], parts[1][:kept], parts[1][kept + extra :]
        got = jnp.concatenate(parts, axis=0)
    return got


def reduced(keep, give, bits, cut=False):
    if cut:
        above, below = halves(give)
        above = yield cross(above), give
        below = yield cross(below), above
        got = jnp.concatenate([above, below], axis=0)
    else:
        got = yield cross(give), give
    values = plus(keep, got)
    stack = []
    for bit in bits[:-1]:
        lower, upper = halves(values)
        flag = has_bit(bit)
        got = yield swap(choose(flag, lower, upper), bit), values
        stack.append((bit, values.shape[0]))
        values = plus(choose(flag, upper, lower), got)
    got = yield swap(values, bits[-1]), values
    values = plus(values, got)
    for bit, rows in stack[::-1]:
        got = yield swap(values, bit), values
        both = in_order(bit, values, got)
        size = values.shape[0]
        if 2 * size != rows:
            both = jnp.concatenate([both[: rows - size], both[size:]], axis=0)
        values = both
    got = yield swap(values, CORE_BIT), values
    return in_order(CORE_BIT, values, got).astype(jnp.float32)


def vector_sum(packed):
    position = lax.axis_index("shard")
    got = yield swap(packed, CORE_BIT), packed
    packed = packed + got
    got = yield cross(pick(packed, 1 - position, 0)), packed
    kept = pick(packed, position, 0) + got
    for bit in all_bits():
        got = yield swap(kept, bit), kept
        kept = kept + got
    return kept


class Steps:
    def __init__(self, chain):
        self.chain = chain
        self.got, self.latest = next(chain)

    def step(self, *gates):
        got = tie(self.got, *gates) if gates else self.got
        self.got, self.latest = self.chain.send(got)

    def finish(self, *gates):
        if gates:
            self.got = tie(self.got, *gates)
        while True:
            try:
                self.step()
            except StopIteration as end:
                return end.value


def bound(values, *chains):
    parts = lax.optimization_barrier((*values, *[chain.got for chain in chains]))
    for chain, got in zip(chains, parts[len(values) :]):
        chain.got = got
    return parts[: len(values)]


def centred_down(values):
    off = values - jnp.mean(values, axis=0, keepdims=True)
    rstd = lax.rsqrt(jnp.mean(off * off, axis=0, keepdims=True) + EPSILON)
    return off * rstd, rstd


def on_device_pair(
    tokens, qkv_weight, out_weight, up_weight, down_weight, attn_gain, attn_shift, query_bias,
    value_bias, out_bias, mlp_gain, mlp_shift, up_bias, down_bias, cotangent,
):
    _, span, width = tokens.shape
    position = lax.axis_index("shard")
    spot = position.astype(jnp.int32).reshape(1)
    core = lax.axis_index("replica") & CORE_BIT
    bits = all_bits()
    fast_bits = [CORE_BIT] + bits[:2]
    turned_bits = [CORE_BIT] + bits[:2][::-1]
    first = position == 0

    own_turned = tokens.reshape(span, width).T
    down_turned = down_weight.T
    singles = (attn_gain, attn_shift, query_bias, value_bias, out_bias, mlp_gain, mlp_shift, down_bias)
    flat_vectors = jnp.concatenate(
        [item.reshape(1, -1) for item in singles] + [up_bias.reshape(-1, singles[0].shape[0])], axis=0
    )
    way_qkv = Steps(spread(qkv_weight, fast_bits))
    other_turned = cross(tie(own_turned, way_qkv.got))
    other_vectors = cross(tie(flat_vectors, way_qkv.got))
    way_qkv.step()
    way_out = Steps(spread(tie(out_weight, other_turned), turned_bits))
    way_up = Steps(spread(tie(up_weight, other_turned), turned_bits))
    way_down = Steps(spread(tie(down_turned, way_up.got), turned_bits))
    grad_turned = cotangent.reshape(span, width).T
    grad_out = grad_turned.T
    grad_halves = grad_turned.reshape(2, width // 2, span)
    grad_left = pick(grad_halves, core, 0), swap(pick(grad_halves, 1 - core, 0), CORE_BIT)

    lower = choose(first, flat_vectors, other_vectors).astype(jnp.float32)
    upper = choose(first, other_vectors, flat_vectors).astype(jnp.float32)
    both = jnp.concatenate([lower, upper], axis=1)
    (gain_first, shift_first, bias_query, bias_value, bias_out, gain_second, shift_second,
     bias_down) = (both[i] for i in range(8))
    bias_up = jnp.concatenate([lower[8:].reshape(1, -1), upper[8:].reshape(1, -1)], axis=1)

    own_tokens = own_turned.T
    second = jnp.stack([bias_out, gain_second, shift_second])
    bias_down = bias_down.reshape(-1, 1)
    bias_up, own_tokens, second, bias_down, grad_out = bound((bias_up, own_tokens, second, bias_down, grad_out))
    way_qkv.step(bias_up, own_tokens, second, bias_down, grad_out)
    all_turned = jnp.concatenate(
        [choose(first, own_turned, other_turned), choose(first, other_turned, own_turned)], axis=1
    )
    unit_all, _ = centred_down(all_turned.astype(jnp.float32))
    normed_turned = low(unit_all * gain_first[:, None] + shift_first[:, None])
    normed_all = normed_turned.T
    normed = lax.dynamic_slice_in_dim(normed_all, position * span, span, axis=0)

    def for_cores(turned):
        parts = turned.reshape(2, 2, turned.shape[0] // 4, turned.shape[1])
        return pick(parts, core, 1), swap(pick(parts, 1 - core, 1), CORE_BIT)

    full_qkv = both_halves(qkv_weight, way_qkv.finish())
    full_q, full_k, full_v = (full_qkv[:, i * width : (i + 1) * width] for i in range(3))
    way_out.step(full_v)
    way_up.step(full_v)
    values = low(dot(tie(normed_all, way_out.latest, way_up.latest), full_v) + bias_value)
    way_out.step(values)
    way_down.step(values)
    keys = low(dot(tie(normed_all, way_out.latest, way_down.latest), full_k))
    way_out.step(keys)
    queries = low(low(dot(tie(normed, way_out.latest), full_q) + bias_query) * SCALING)
    (queries,) = bound((queries,), way_up)
    way_up.step()
    context, context_t, lse = attention_forward(spot, tie(queries, way_up.latest), keys, values, 1, span)
    context, context_t, lse = bound((context, context_t, lse), way_up, way_down, way_out)
    full_out = both_halves(out_weight, way_out.finish())
    way_up.step()
    way_down.step()
    context = tie(context, way_up.latest, way_down.latest)
    normed_left = for_cores(normed_turned)
    part_up = way_up.finish()
    active, slope, middle_turned, unit_second, rstd_second, two_turned = mlp_up(
        spot, context, full_out, own_tokens, second, bias_up, up_weight, part_up
    )
    active, slope, middle_turned, unit_second, rstd_second, two_turned = bound(
        (active, slope, middle_turned, unit_second, rstd_second, two_turned), way_down
    )
    way_down.step()

    active_sib = swap(active, CORE_BIT)
    give, keep_down = turned_weight_grads(
        spot, *grad_left, tie(active, way_down.latest), active_sib, width // 4, "down_grads"
    )
    sum_down = Steps(reduced(keep_down, give, bits, True))
    part_down = way_down.finish(give)
    block_out = mlp_down(
        spot, tie(active, give), down_turned, part_down, middle_turned, bias_down
    )

    two_left = for_cores(two_turned)
    context_left = for_cores(context_t)
    results = mlp_back(
        spot, tie(grad_out, block_out, *two_left, *context_left), slope, unit_second, rstd_second,
        gain_second.reshape(1, -1), full_out, down_turned, part_down, up_weight, part_up,
    )
    grad_hidden, grad_middle, grad_branch, grad_context, sum_hidden, sum_rows = bound(results, sum_down)
    sum_down.step()
    hidden_sib = swap(grad_hidden, CORE_BIT)
    branch_sib = swap(grad_branch, CORE_BIT)
    give_out, keep_out = weight_grads(
        spot, *context_left, grad_branch, branch_sib, width, context_left[0].shape[1], grad_branch.shape[1],
        "out_grads"
    )
    sum_out = Steps(reduced(keep_out, give_out, bits))
    give, keep_up = weight_grads(
        spot, *two_left, grad_hidden, tie(hidden_sib, give_out), grad_hidden.shape[1], two_left[0].shape[1],
        2 * CHUNK, "up_grads"
    )
    give, keep_up = bound((give, keep_up), sum_down)
    sum_up = Steps(reduced(keep_up, give, bits))
    sum_down.step()
    grad_context = tie(grad_context, give, sum_down.latest)

    grad_q, grad_k, grad_v = attention_backward(
        spot, queries, keys, values, grad_context, context, lse, 1, span
    )
    grad_q, grad_k, grad_v = bound((grad_q, grad_k, grad_v), sum_down, sum_out)
    sum_down.step()
    sum_out.step()
    rights = []
    for part in (grad_q, grad_k, grad_v):
        rights += [part, swap(part, CORE_BIT)]
    mine, theirs = input_grads(
        spot, full_q, full_k, full_v, tie(grad_q, sum_down.latest, sum_out.latest), grad_k, grad_v
    )
    mine, theirs = bound((mine, theirs), sum_up, sum_down, sum_out)
    sum_up.step()
    sum_down.step()
    sum_out.step()
    rights[0] = tie(grad_q, sum_down.latest, sum_out.latest, sum_up.latest, theirs)
    give, keep_qkv = qkv_weight_grads(spot, width, *normed_left, *rights)
    give, keep_qkv = bound((give, keep_qkv), sum_out)
    sum_out.step()
    sum_qkv = Steps(reduced(keep_qkv, give, bits))

    other_part = cross(tie(theirs, sum_qkv.got))
    grad_middle, sum_rows, sum_hidden = bound((grad_middle, sum_rows, sum_hidden, give))[:3]

    unit_first, rstd_first = centred_down(own_turned.astype(jnp.float32))
    unit_other, _ = centred_down(other_turned.astype(jnp.float32))
    theirs_float = theirs.astype(jnp.float32)
    sums = (
        jnp.sum(mine * unit_first, axis=1) + jnp.sum(theirs_float * unit_other, axis=1),
        jnp.sum(mine, axis=1) + jnp.sum(theirs_float, axis=1),
        row_sum(grad_q)[:width],
        row_sum(grad_v)[:width],
        sum_rows[2],
        sum_rows[0],
        sum_rows[1],
        sum_hidden.reshape(-1),
        jnp.sum(grad_turned.astype(jnp.float32), axis=1),
    )
    small = jnp.stack([item.reshape(2, -1) for item in sums[:7] + sums[8:]], axis=1)
    small = jnp.concatenate([small, sums[7].reshape(2, -1, width // 2)], axis=1)
    sum_small = Steps(vector_sum(small))
    grad_tokens = token_grads(
        spot, mine, other_part, own_turned, gain_first.reshape(-1, 1), grad_middle
    )

    chains = {"d": sum_down, "u": sum_up, "q": sum_qkv, "o": sum_out, "v": sum_small}
    done = {}
    latest = give
    for name in TAIL:
        if name == "t":
            latest = grad_tokens
            continue
        chain = chains[name]
        try:
            chain.step(latest)
            latest = chain.latest
        except StopIteration as end:
            done[name] = latest = end.value
    vectors_out = done["v"]
    outs = [vectors_out[i] for i in range(7)] + [vectors_out[8:].reshape(-1), vectors_out[7]]

    return (
        block_out.T.reshape(1, span, width),
        grad_tokens.T.reshape(1, span, width),
        done["q"], done["o"], done["u"], done["d"].T,
        *outs,
    )


def on_device_general(
    tokens, qkv_weight, out_weight, up_weight, down_weight, attn_gain, attn_shift, query_bias,
    value_bias, out_bias, mlp_gain, mlp_shift, up_bias, down_bias, cotangent,
):
    seqs, span, width = tokens.shape
    rows = seqs * span
    shards = lax.axis_size("shard")
    position = lax.axis_index("shard")
    core = lax.axis_index("replica") & CORE_BIT
    length = span * shards
    bits = all_bits()

    shards_of = (attn_gain, attn_shift, query_bias, value_bias, out_bias, mlp_gain, mlp_shift,
                 up_bias, down_bias)
    flat_vectors = jnp.concatenate(shards_of)
    all_vectors = lax.all_gather(flat_vectors, "shard", axis=0, tiled=False)
    vectors, at = [], 0
    for item in shards_of:
        size = item.shape[0]
        vectors.append(all_vectors[:, at : at + size].reshape(-1).astype(jnp.float32))
        at += size
    (gain_first, shift_first, bias_query, bias_value, bias_out, gain_second, shift_second, bias_up,
     bias_down) = vectors

    full_qkv, full_out, full_up, full_down = [
        lax.all_gather(item, "shard", axis=0, tiled=True)
        for item in (qkv_weight, out_weight, up_weight, down_weight)
    ]
    all_tokens = lax.all_gather(tokens, "shard", axis=1, tiled=True).reshape(-1, width)

    def own_rows(values):
        per_seq = values.reshape(seqs, length, values.shape[-1])
        return lax.dynamic_slice_in_dim(per_seq, position * span, span, axis=1).reshape(rows, -1)

    grad_out = cotangent.reshape(rows, width)
    grad_out_both = jnp.concatenate([grad_out, swap(grad_out, CORE_BIT)], axis=0)

    flat = tokens.reshape(rows, width).astype(jnp.float32)
    unit_all, rstd_all = centred(all_tokens.astype(jnp.float32))
    normed_all = low(unit_all * gain_first + shift_first)
    normed_sib = swap(normed_all, CORE_BIT)
    normed = own_rows(normed_all)
    full_q, full_k, full_v = (full_qkv[:, i * width : (i + 1) * width] for i in range(3))
    queries = low(low(dot(normed, full_q) + bias_query) * SCALING)
    keys = low(dot(normed_all, full_k))
    values = low(dot(normed_all, full_v) + bias_value)
    spot = position.astype(jnp.int32).reshape(1)
    context, context_t, lse = attention_forward(spot, queries, keys, values, seqs, span)
    context_sib = swap(context, CORE_BIT)
    middle = flat + dot(context, full_out) + bias_out
    unit_second, rstd_second = centred(middle)
    normed_two = low(unit_second * gain_second + shift_second)
    normed_two_sib = swap(normed_two, CORE_BIT)
    active_float, slope = gelu_parts(dot(normed_two, full_up) + bias_up)
    active = low(active_float)
    slope = low(slope)

    def split_rows(lhs, rhs):
        return lax.psum_scatter(low(dot_tn(lhs, rhs)), "shard", scatter_dimension=0, tiled=True)

    grouped = active.reshape(rows, shards, 2, -1)
    taken = jnp.where(core == 0, grouped[:, :, 0], grouped[:, :, 1]).reshape(rows, -1)
    given = jnp.where(core == 0, grouped[:, :, 1], grouped[:, :, 0]).reshape(rows, -1)
    active_both = jnp.concatenate([taken, swap(given, CORE_BIT)], axis=0)
    sum_down = split_rows(active_both, grad_out_both)
    sum_down = reduce_rest(sum_down, bits)
    sum_down = in_order(CORE_BIT, sum_down, swap(sum_down, CORE_BIT))

    result = middle + dot(active, full_down) + bias_down
    block_out = low(result).reshape(seqs, span, width)

    def by_columns(lhs_both, part):
        taken = columns_of(part, 1, core)
        given = columns_of(part, 1, 1 - core)
        return split_rows(lhs_both, jnp.concatenate([taken, swap(given, CORE_BIT)], axis=0))

    def join_columns(values):
        other = swap(values, CORE_BIT)
        left = choose(core == 0, values, other)
        right = choose(core == 0, other, values)
        return left, right

    grad_float = grad_out.astype(jnp.float32)
    grad_hidden = low(dot_nt(grad_out, full_down) * slope.astype(jnp.float32))
    normed_two_both = jnp.concatenate([normed_two, normed_two_sib], axis=0)
    sum_up = by_columns(normed_two_both, grad_hidden)
    sum_up = reduce_rest(sum_up, bits)
    sum_up = jnp.concatenate(join_columns(sum_up), axis=1)
    grad_normed_two = dot_nt(grad_hidden, full_up)
    grad_middle = norm_pull(grad_normed_two, unit_second, rstd_second, gain_second) + grad_float
    grad_branch = low(grad_middle)
    grad_context = low(dot_nt(grad_branch, full_out))
    context_both = jnp.concatenate([context, context_sib], axis=0)
    sum_out = by_columns(context_both, grad_branch)
    sum_out = reduce_rest(sum_out, bits)
    sum_out = jnp.concatenate(join_columns(sum_out), axis=1)

    grad_q, grad_k, grad_v = attention_backward(
        spot, queries, keys, values, grad_context, context, lse, seqs, span
    )
    grad_q, grad_k, grad_v = grad_q[:, :width], grad_k[:, :width], grad_v[:, :width]
    normed_both = jnp.concatenate([normed_all, normed_sib], axis=0)
    own_both = jnp.concatenate([normed, own_rows(normed_sib)], axis=0)
    third = width // 2
    half_q, half_k, half_v = (
        jnp.concatenate(
            [columns_of(part, 1, core), swap(columns_of(part, 1, 1 - core), CORE_BIT)], axis=0
        )
        for part in (grad_q, grad_k, grad_v)
    )
    sum_qkv = lax.psum_scatter(
        low(jnp.concatenate(
            [dot_tn(own_both, half_q), dot_tn(normed_both, half_k), dot_tn(normed_both, half_v)],
            axis=1,
        )),
        "shard", scatter_dimension=0, tiled=True,
    )
    sum_qkv = reduce_rest(sum_qkv, bits)
    left, right = join_columns(sum_qkv)
    sum_qkv = jnp.concatenate(
        [part[:, i * third : (i + 1) * third] for i in range(3) for part in (left, right)], axis=1
    )

    from_query = dot_nt(grad_q, full_q)
    from_rest = dot_nt(grad_k, full_k) + dot_nt(grad_v, full_v)
    grad_normed = from_query + lax.psum_scatter(
        from_rest.reshape(seqs, length, width), "shard", scatter_dimension=1, tiled=True
    ).reshape(rows, width)
    unit_first, rstd_first = own_rows(unit_all), own_rows(rstd_all)
    grad_tokens = low(norm_pull(grad_normed, unit_first, rstd_first, gain_first) + grad_middle)

    def column_sum(values):
        return jnp.sum(values.astype(jnp.float32), axis=0)

    sums = (
        column_sum(grad_normed * unit_first),
        column_sum(grad_normed),
        column_sum(grad_q),
        column_sum(grad_v),
        column_sum(grad_branch),
        column_sum(grad_normed_two * unit_second),
        column_sum(grad_normed_two),
        column_sum(grad_hidden),
        column_sum(grad_float),
    )
    packed = jnp.concatenate([item.reshape(shards, -1) for item in sums], axis=1)
    packed = lax.psum(packed, ("replica", "shard"))
    packed = lax.dynamic_index_in_dim(packed, position, axis=0, keepdims=False)
    outs, at = [], 0
    for item in sums:
        size = item.shape[0] // shards
        outs.append(packed[at : at + size])
        at += size
    return (
        block_out,
        grad_tokens.reshape(seqs, span, width),
        sum_qkv.astype(jnp.float32),
        sum_out.astype(jnp.float32),
        sum_up.astype(jnp.float32),
        sum_down.astype(jnp.float32),
        *outs,
    )


def on_device(tokens, *rest):
    if lax.axis_size("shard") == 2 and lax.axis_size("replica") >= 8 and tokens.shape[0] == 1:
        return on_device_pair(tokens, *rest)
    return on_device_general(tokens, *rest)


def solution(mesh):
    vector, matrix, rows = P("shard"), P("shard", None), P("replica", "shard", None)
    return jax.shard_map(
        on_device,
        mesh=mesh,
        in_specs=(rows, *[matrix] * 4, *[vector] * 9, rows),
        out_specs=(rows, rows, *[matrix] * 4, *[vector] * 9),
        check_vma=False,
    )
```

```python
import functools
import jax
import jax.numpy as jnp
from jax import lax
from jax.experimental import pallas as pl
from jax.experimental.pallas import tpu as pltpu
from jax.sharding import PartitionSpec as P

HD = 64
SCALING = 0.125
NEG = -1e30
LANES = 128
QUICK = pl.CostEstimate(flops=1, bytes_accessed=1, transcendentals=0)


def _nt(a, b):
    return lax.dot_general(a, b, (((1,), (1,)), ((), ())), preferred_element_type=jnp.float32)


def _nn(a, b):
    return lax.dot_general(a, b, (((1,), (0,)), ((), ())), preferred_element_type=jnp.float32)


def _lane_valid(shape, width):
    left = width - pl.program_id(1) * LANES
    return lax.broadcasted_iota(jnp.int32, shape, 1) < left


def _clean(ref, width):
    block = ref[...]
    return jnp.where(_lane_valid(block.shape, width), block, jnp.zeros_like(block))


def _head_part(block, head):
    lane = lax.broadcasted_iota(jnp.int32, block.shape, 1)
    keep = (lane < HD) if head == 0 else (lane >= HD)
    return jnp.where(keep, block, jnp.zeros_like(block))


def _diag_mask(keys, rows, first):
    key_at = lax.broadcasted_iota(jnp.int32, (keys, rows), 0)
    row_at = lax.broadcasted_iota(jnp.int32, (keys, rows), 1) + first
    return key_at <= row_at


def forward_kernel(pos_ref, q_ref, k_ref, v_ref, ctx_ref, ctx_t_ref, lse_ref, kc_ref, vt_ref, *, span, width):
    pos = pos_ref[0]
    block = min(256, span)
    queries = _clean(q_ref, width)
    kc_ref[...] = _clean(k_ref, width)
    length = k_ref.shape[0]
    for j in range(length // span):
        vt_ref[j] = _clean(v_ref.at[pl.ds(j * span, span), :], width).T
    chains = []
    for head in range(2):
        part = _head_part(queries, head)
        for at in range(0, span, block):
            chains.append((part[at : at + block], at))

    def update(state, scores, vt):
        peak, total, acc = state
        top = jnp.maximum(peak, jnp.max(scores, axis=0, keepdims=True))
        fade = jnp.exp(peak - top)
        expons = jnp.exp(scores - top)
        total = total * fade + jnp.sum(expons, axis=0, keepdims=True)
        acc = acc * fade + _nn(vt, expons.astype(jnp.bfloat16))
        return top, total, acc

    states = []
    own_vt = vt_ref[pos]
    for part, at in chains:
        keys = at + block
        own_k = kc_ref[pl.ds(pl.multiple_of(pos * span, span), keys), :]
        scores = jnp.where(_diag_mask(keys, block, at), _nt(own_k, part), NEG)
        peak = jnp.max(scores, axis=0, keepdims=True)
        expons = jnp.exp(scores - peak)
        total = jnp.sum(expons, axis=0, keepdims=True)
        acc = _nn(own_vt[:, :keys], expons.astype(jnp.bfloat16))
        states.append((peak, total, acc))

    def past(j, states):
        key_block = kc_ref[pl.ds(pl.multiple_of(j * span, span), span), :]
        vt = vt_ref[j]
        return tuple(
            update(state, _nt(key_block, part), vt) for state, (part, _) in zip(states, chains)
        )

    states = lax.fori_loop(0, pos, past, tuple(states))
    per_head = len(chains) // 2
    for i in range(per_head):
        at = i * block
        (peak0, total0, acc0), (peak1, total1, acc1) = states[i], states[per_head + i]
        row = lax.broadcasted_iota(jnp.int32, acc0.shape, 0)
        both = jnp.where(row < HD, acc0 / total0, acc1 / total1)
        ctx_ref[at : at + block, :] = both.T.astype(ctx_ref.dtype)
        ctx_t_ref[:, at : at + block] = both.astype(ctx_t_ref.dtype)
        lse_ref[0, 0:1, at : at + block] = peak0 + jnp.log(total0)
        lse_ref[0, 1:2, at : at + block] = peak1 + jnp.log(total1)


def backward_kernel(pos_ref, q_ref, k_ref, v_ref, g_ref, ctx_ref, lse_ref, dq_ref, dk_ref, dv_ref,
                    kc_ref, vc_ref, kt_ref, dk_acc, dv_acc, *, span, width):
    pos = pos_ref[0]
    block = min(256, span)
    queries = _clean(q_ref, width)
    grads = _clean(g_ref, width)
    context = _clean(ctx_ref, width)
    kc_ref[...] = _clean(k_ref, width)
    vc_ref[...] = _clean(v_ref, width)
    length = k_ref.shape[0]
    for j in range(length // span):
        kt_ref[j] = kc_ref[pl.ds(j * span, span), :].T
    dk_acc[...] = jnp.zeros_like(dk_acc)
    dv_acc[...] = jnp.zeros_like(dv_acc)
    product = (grads.astype(jnp.float32) * context.astype(jnp.float32)).T
    chains = []
    for head in range(2):
        q_part = _head_part(queries, head)
        g_part = _head_part(grads, head)
        inner = jnp.sum(product[head * HD : (head + 1) * HD], axis=0, keepdims=True)
        for at in range(0, span, block):
            chains.append((
                q_part[at : at + block], g_part[at : at + block], inner[:, at : at + block],
                lse_ref[0, head : head + 1, at : at + block], at,
            ))

    def piece(chain, key_block, value_block, kt, masked):
        q_part, g_part, inner, lse, at = chain
        scores = _nt(key_block, q_part)
        if masked:
            scores = jnp.where(_diag_mask(key_block.shape[0], q_part.shape[0], at), scores, NEG)
        probs = jnp.exp(scores - lse)
        grad_probs = _nt(value_block, g_part)
        grad_scores = (probs * (grad_probs - inner)).astype(jnp.bfloat16)
        dq = _nn(kt, grad_scores)
        dk = _nn(grad_scores, q_part)
        dv = _nn(probs.astype(jnp.bfloat16), g_part)
        return dq, dk, dv

    start = pl.multiple_of(pos * span, span)
    own_kt = kt_ref[pos]
    dqs = []
    for chain in chains:
        keys = chain[4] + block
        where = pl.ds(start, keys)
        dq, dk, dv = piece(chain, kc_ref[where, :], vc_ref[where, :], own_kt[:, :keys], True)
        dk_acc[where, :] += dk
        dv_acc[where, :] += dv
        dqs.append(dq)

    def past(j, dqs):
        where = pl.ds(pl.multiple_of(j * span, span), span)
        key_block, value_block, kt = kc_ref[where, :], vc_ref[where, :], kt_ref[j]
        out, dk_sum, dv_sum = [], None, None
        for chain, dq_old in zip(chains, dqs):
            dq, dk, dv = piece(chain, key_block, value_block, kt, False)
            dk_sum = dk if dk_sum is None else dk_sum + dk
            dv_sum = dv if dv_sum is None else dv_sum + dv
            out.append(dq_old + dq)
        dk_acc[where, :] = dk_sum
        dv_acc[where, :] = dv_sum
        return tuple(out)

    dqs = lax.fori_loop(0, pos, past, tuple(dqs))
    per_head = len(chains) // 2
    for i in range(per_head):
        at = i * block
        row = lax.broadcasted_iota(jnp.int32, dqs[0].shape, 0)
        both = jnp.where(row < HD, dqs[i], dqs[per_head + i]) * SCALING
        dq_ref[at : at + block, :] = both.T.astype(dq_ref.dtype)
    dk_ref[...] = dk_acc[...].astype(dk_ref.dtype)
    dv_ref[...] = dv_acc[...].astype(dv_ref.dtype)


def attention_forward(position, queries, keys, values, seqs, span):
    rows, width = queries.shape
    length = keys.shape[0] // seqs
    pairs = pl.cdiv(width, LANES)
    own = pl.BlockSpec((span, LANES), lambda s, h, p: (s, h))
    whole = pl.BlockSpec((length, LANES), lambda s, h, p: (s, h))
    lse = pl.BlockSpec((1, 2, span), lambda s, h, p: (s * pairs + h, 0, 0))
    return pl.pallas_call(
        functools.partial(forward_kernel, span=span, width=width),
        grid_spec=pltpu.PrefetchScalarGridSpec(
            num_scalar_prefetch=1,
            grid=(seqs, pairs),
            in_specs=[own, whole, whole],
            out_specs=[own, pl.BlockSpec((LANES, span), lambda s, h, p: (h, s)), lse],
            scratch_shapes=[
                pltpu.VMEM((length, LANES), jnp.bfloat16),
                pltpu.VMEM((length // span, LANES, span), jnp.bfloat16),
            ],
        ),
        out_shape=[
            jax.ShapeDtypeStruct((rows, width), jnp.bfloat16),
            jax.ShapeDtypeStruct((width, rows), jnp.bfloat16),
            jax.ShapeDtypeStruct((seqs * pairs, 2, span), jnp.float32),
        ],
        compiler_params=pltpu.CompilerParams(vmem_limit_bytes=48 * 1024 * 1024),
        cost_estimate=QUICK,
        name="attention_forward",
    )(position, queries, keys, values)


def attention_backward(position, queries, keys, values, grads, context, lse_rows, seqs, span):
    rows, width = queries.shape
    length = keys.shape[0] // seqs
    pairs = pl.cdiv(width, LANES)
    own = pl.BlockSpec((span, LANES), lambda s, h, p: (s, h))
    whole = pl.BlockSpec((length, LANES), lambda s, h, p: (s, h))
    lse = pl.BlockSpec((1, 2, span), lambda s, h, p: (s * pairs + h, 0, 0))
    return pl.pallas_call(
        functools.partial(backward_kernel, span=span, width=width),
        grid_spec=pltpu.PrefetchScalarGridSpec(
            num_scalar_prefetch=1,
            grid=(seqs, pairs),
            in_specs=[own, whole, whole, own, own, lse],
            out_specs=[own, whole, whole],
            scratch_shapes=[
                pltpu.VMEM((length, LANES), jnp.bfloat16),
                pltpu.VMEM((length, LANES), jnp.bfloat16),
                pltpu.VMEM((length // span, LANES, span), jnp.bfloat16),
                pltpu.VMEM((length, LANES), jnp.float32),
                pltpu.VMEM((length, LANES), jnp.float32),
            ],
        ),
        out_shape=[
            jax.ShapeDtypeStruct((rows, pairs * LANES), jnp.bfloat16),
            jax.ShapeDtypeStruct((keys.shape[0], pairs * LANES), jnp.bfloat16),
            jax.ShapeDtypeStruct((keys.shape[0], pairs * LANES), jnp.bfloat16),
        ],
        compiler_params=pltpu.CompilerParams(vmem_limit_bytes=48 * 1024 * 1024),
        cost_estimate=QUICK,
        name="attention_backward",
    )(position, queries, keys, values, grads, context, lse_rows)


EPSILON = 1e-05
CORE_BIT = 1


def centred(values):
    average = jnp.mean(values, axis=-1, keepdims=True)
    off = values - average
    rstd = lax.rsqrt(jnp.mean(off * off, axis=-1, keepdims=True) + EPSILON)
    return off * rstd, rstd


def norm_pull(grad, unit, rstd, gain):
    scaled = grad * gain
    first = jnp.mean(scaled, axis=-1, keepdims=True)
    second = jnp.mean(scaled * unit, axis=-1, keepdims=True)
    return rstd * (scaled - first - unit * second)


def gelu_parts(values):
    square = values * values
    tanh = jnp.tanh(0.7978845608 * values * (1.0 + 0.044715 * square))
    half = 0.5 * (1.0 + tanh)
    slope = half + 0.5 * values * (1.0 - tanh * tanh) * (
        0.7978845608 * (1.0 + 3.0 * 0.044715 * square)
    )
    return values * half, slope


def dot(left, right):
    return jnp.dot(left, right, preferred_element_type=jnp.float32)


def dot_nt(left, right):
    return lax.dot_general(
        left, right, (((1,), (1,)), ((), ())), preferred_element_type=jnp.float32
    )


def dot_tn(left, right):
    return lax.dot_general(
        left, right, (((0,), (0,)), ((), ())), preferred_element_type=jnp.float32
    )


def low(values):
    return values.astype(jnp.bfloat16)


def swap(values, bit):
    size = lax.axis_size("replica")
    return lax.ppermute(values, "replica", [(i, i ^ bit) for i in range(size)])


def cross(values):
    return lax.ppermute(values, "shard", [(0, 1), (1, 0)])


def has_bit(bit):
    return (lax.axis_index("replica") & bit) != 0


def choose(flag, left, right):
    return jnp.where(flag, left, right)


def in_order(bit, mine, other):
    flag = has_bit(bit)
    return jnp.concatenate([choose(flag, other, mine), choose(flag, mine, other)], axis=0)


def both_halves(weight, got):
    first = lax.axis_index("shard") == 0
    return jnp.concatenate([choose(first, weight, got), choose(first, got, weight)], axis=0)


def all_bits():
    bits, bit = [], 2
    while bit < lax.axis_size("replica"):
        bits.append(bit)
        bit *= 2
    return bits


def halves(values):
    rows = values.shape[0]
    size = -(-rows // 16) * 8
    return values[:size], values[rows - size :]


def reduce_rest(values, bits):
    stack = []
    for bit in bits[:-1]:
        lower, upper = halves(values)
        flag = has_bit(bit)
        sent = swap(choose(flag, lower, upper), bit)
        stack.append((bit, values.shape[0]))
        values = low(choose(flag, upper, lower).astype(jnp.float32) + sent.astype(jnp.float32))
    values = low(values.astype(jnp.float32) + swap(values, bits[-1]).astype(jnp.float32))
    for bit, rows in stack[::-1]:
        both = in_order(bit, values, swap(values, bit))
        size = values.shape[0]
        if 2 * size != rows:
            both = jnp.concatenate([both[: rows - size], both[size:]], axis=0)
        values = both
    return values


def columns_of(values, axis, index):
    size = values.shape[axis] // 2
    low_part = lax.slice_in_dim(values, 0, size, axis=axis)
    high_part = lax.slice_in_dim(values, size, 2 * size, axis=axis)
    return choose(index == 0, low_part, high_part)


VMEM_LIMIT = 60 * 1024 * 1024
CHUNK = 256


def _vmem(count):
    return [pl.BlockSpec(memory_space=pltpu.VMEM)] * count


def _call(kernel, name, in_specs, out_shapes, scratch, flops, moved):
    return pl.pallas_call(
        kernel,
        grid_spec=pltpu.PrefetchScalarGridSpec(
            num_scalar_prefetch=1, grid=(1,), in_specs=in_specs,
            out_specs=[pl.BlockSpec(memory_space=pltpu.VMEM)] * len(out_shapes),
            scratch_shapes=scratch,
        ),
        out_shape=out_shapes,
        compiler_params=pltpu.CompilerParams(vmem_limit_bytes=VMEM_LIMIT),
        cost_estimate=QUICK,
        name=name,
    )


def _fetch(own_ref, got_ref, full_ref, sems, pos, at, width):
    rows = own_ref.shape[0]
    cols = pl.ds(at, width)
    mine = pl.ds(pl.multiple_of(pos * rows, 16), rows)
    theirs = pl.ds(pl.multiple_of((1 - pos) * rows, 16), rows)
    return (
        pltpu.make_async_copy(own_ref.at[:, cols], full_ref.at[mine, cols], sems.at[0]),
        pltpu.make_async_copy(got_ref.at[:, cols], full_ref.at[theirs, cols], sems.at[1]),
    )


def up_kernel(pos_ref, ctx_ref, out_w_ref, x_ref, vec_ref, bias_ref, own_ref, got_ref,
              act_ref, slope_ref, mid_t_ref, unit_ref, rstd_ref, nt_t_ref, nt_ref, full_ref, sems):
    pos = pos_ref[0]
    units = own_ref.shape[1]
    count = units // CHUNK
    copies = [_fetch(own_ref, got_ref, full_ref, sems.at[j], pos, j * CHUNK, CHUNK) for j in range(count)]
    for pair in copies:
        for copy in pair:
            copy.start()
    unit_ref[...] = _nn(ctx_ref[...], out_w_ref[...])
    rows = ctx_ref.shape[0]
    tile = 128
    for at in range(0, rows, tile):
        where = slice(at, at + tile)
        middle = x_ref[where, :].astype(jnp.float32) + (unit_ref[where, :] + vec_ref[0:1, :])
        unit, rstd = centred(middle)
        normed = unit * vec_ref[1:2, :] + vec_ref[2:3, :]
        unit_ref[where, :] = unit
        rstd_ref[where, :] = rstd
        mid_t_ref[:, where] = middle.T
        nt_ref[where, :] = normed.astype(jnp.bfloat16)
        nt_t_ref[:, where] = normed.T.astype(jnp.bfloat16)
    for pair in copies:
        for copy in pair:
            copy.wait()
    normed = nt_ref[...]
    for j in range(count):
        cols = pl.ds(j * CHUNK, CHUNK)
        hidden = _nn(normed, full_ref[:, cols]) + bias_ref[:, cols]
        value, slope = gelu_parts(hidden)
        act_ref[:, cols] = value.astype(jnp.bfloat16)
        slope_ref[:, cols] = slope.astype(jnp.bfloat16)


def mlp_up(spot, context, out_weight, tokens, vectors, bias, own, got):
    rows, width = tokens.shape
    units = own.shape[1]
    any_spec = pl.BlockSpec(memory_space=pl.ANY)
    return _call(
        up_kernel, "mlp_up", _vmem(5) + [any_spec] * 2,
        [
            jax.ShapeDtypeStruct((rows, units), jnp.bfloat16),
            jax.ShapeDtypeStruct((rows, units), jnp.bfloat16),
            jax.ShapeDtypeStruct((width, rows), jnp.float32),
            jax.ShapeDtypeStruct((rows, width), jnp.float32),
            jax.ShapeDtypeStruct((rows, 1), jnp.float32),
            jax.ShapeDtypeStruct((width, rows), jnp.bfloat16),
        ],
        [
            pltpu.VMEM((rows, width), jnp.bfloat16),
            pltpu.VMEM((width, units), jnp.bfloat16),
            pltpu.SemaphoreType.DMA((units // CHUNK, 2)),
        ],
        2 * rows * width * (units + width), 2 * units * (width + 2 * rows) + 18 * rows * width,
    )(spot, context, out_weight, tokens, vectors, bias, own, got)


def down_kernel(pos_ref, act_ref, own_ref, got_ref, middle_ref, bias_ref, out_ref):
    pos = pos_ref[0]
    half = own_ref.shape[1]
    mine = pl.ds(pl.multiple_of(pos * half, 128), half)
    theirs = pl.ds(pl.multiple_of((1 - pos) * half, 128), half)
    total = _nt(own_ref[...], act_ref[:, mine]) + _nt(got_ref[...], act_ref[:, theirs])
    out_ref[...] = (middle_ref[...] + total + bias_ref[...]).astype(out_ref.dtype)


def mlp_down(spot, active, own, got, middle, bias):
    width, rows = middle.shape
    half = own.shape[1]
    tile = width // 4
    return pl.pallas_call(
        down_kernel,
        grid_spec=pltpu.PrefetchScalarGridSpec(
            num_scalar_prefetch=1, grid=(width // tile,),
            in_specs=[
                pl.BlockSpec((rows, 2 * half), lambda i, p: (0, 0)),
                pl.BlockSpec((tile, half), lambda i, p: (i, 0)),
                pl.BlockSpec((tile, half), lambda i, p: (i, 0)),
                pl.BlockSpec((tile, rows), lambda i, p: (i, 0)),
                pl.BlockSpec((tile, 1), lambda i, p: (i, 0)),
            ],
            out_specs=pl.BlockSpec((tile, rows), lambda i, p: (i, 0)),
        ),
        out_shape=jax.ShapeDtypeStruct((width, rows), jnp.bfloat16),
        compiler_params=pltpu.CompilerParams(vmem_limit_bytes=VMEM_LIMIT),
        cost_estimate=QUICK,
        name="mlp_down",
    )(spot, active, own, got, middle, bias)


def back_kernel(pos_ref, grad_ref, slope_ref, unit_ref, rstd_ref, gain_ref, out_w_ref,
                down_own, down_got, up_own, up_got,
                hidden_ref, middle_ref, branch_ref, context_ref, wide_sum_ref, sum_ref,
                down_full, up_full, sems):
    pos = pos_ref[0]
    half = down_own.shape[1]
    units = up_own.shape[1]
    rows, width = grad_ref.shape
    mine = pl.ds(pl.multiple_of(pos * half, 128), half)
    theirs = pl.ds(pl.multiple_of((1 - pos) * half, 128), half)
    first = pltpu.make_async_copy(down_own, down_full.at[:, mine], sems.at[0])
    second = pltpu.make_async_copy(down_got, down_full.at[:, theirs], sems.at[1])
    first.start()
    second.start()
    rows_up = up_own.shape[0]
    third = pltpu.make_async_copy(up_own, up_full.at[pl.ds(pl.multiple_of(pos * rows_up, 16), rows_up), :], sems.at[2])
    fourth = pltpu.make_async_copy(up_got, up_full.at[pl.ds(pl.multiple_of((1 - pos) * rows_up, 16), rows_up), :], sems.at[3])
    third.start()
    fourth.start()
    first.wait()
    second.wait()
    grad = grad_ref[...]
    for j in range(units // CHUNK):
        cols = pl.ds(j * CHUNK, CHUNK)
        active = _nn(grad, down_full[:, cols])
        hidden = (active * slope_ref[:, cols].astype(jnp.float32)).astype(jnp.bfloat16)
        hidden_ref[:, cols] = hidden
        wide_sum_ref[:, cols] = jnp.sum(hidden.astype(jnp.float32), axis=0, keepdims=True)
    third.wait()
    fourth.wait()
    hidden = hidden_ref[...]
    for at in range(0, width, CHUNK):
        size = min(CHUNK, width - at)
        middle_ref[:, at : at + size] = _nt(hidden, up_full[at : at + size, :])
    sum_ref[...] = jnp.zeros_like(sum_ref)
    branch_ref[...] = jnp.zeros_like(branch_ref)
    tile = 128
    for at in range(0, rows, tile):
        where = slice(at, at + tile)
        normed = middle_ref[where, :]
        unit = unit_ref[where, :]
        out = norm_pull(normed, unit, rstd_ref[where, :], gain_ref[...])
        out = out + grad_ref[where, :].astype(jnp.float32)
        branch = out.astype(jnp.bfloat16)
        middle_ref[where, :] = out
        branch_ref[where, 0:width] = branch
        sum_ref[0:1, :] += jnp.sum(normed * unit, axis=0, keepdims=True)
        sum_ref[1:2, :] += jnp.sum(normed, axis=0, keepdims=True)
        sum_ref[2:3, :] += jnp.sum(branch.astype(jnp.float32), axis=0, keepdims=True)
    context_ref[...] = _nt(branch_ref[:, 0:width], out_w_ref[...]).astype(context_ref.dtype)


def mlp_back(spot, grad, slope, unit, rstd, gain, out_weight, down_own, down_got, up_own, up_got):
    rows, width = grad.shape
    units = up_own.shape[1]
    any_spec = pl.BlockSpec(memory_space=pl.ANY)
    return _call(
        back_kernel, "mlp_back", _vmem(6) + [any_spec] * 4,
        [
            jax.ShapeDtypeStruct((rows, units), jnp.bfloat16),
            jax.ShapeDtypeStruct((rows, width), jnp.float32),
            jax.ShapeDtypeStruct((rows, pl.cdiv(width, LANES) * LANES), jnp.bfloat16),
            jax.ShapeDtypeStruct((rows, width), jnp.bfloat16),
            jax.ShapeDtypeStruct((1, units), jnp.float32),
            jax.ShapeDtypeStruct((8, width), jnp.float32),
        ],
        [
            pltpu.VMEM((width, units), jnp.bfloat16),
            pltpu.VMEM((width, units), jnp.bfloat16),
            pltpu.SemaphoreType.DMA((4,)),
        ],
        4 * rows * width * units + 2 * rows * width * width, 4 * units * (width + rows) + 12 * rows * width,
    )(spot, grad, slope, unit, rstd, gain, out_weight, down_own, down_got, up_own, up_got)


def weight_kernel(pos_ref, left_own, left_sib, right_own, right_sib, give_ref, keep_ref, total_ref):
    pos = pos_ref[0]
    _, rows, tokens = left_own.shape
    own = left_own[...].reshape(2 * rows, tokens)
    sib = left_sib[...].reshape(2 * rows, tokens)
    total = _nn(own, right_own[...]) + _nn(sib, right_sib[...])
    total_ref[...] = total.astype(total_ref.dtype).reshape(total_ref.shape)
    give_ref[...] = total_ref[1 - pos]
    keep_ref[...] = total_ref[pos]


def weight_grads(spot, left_own, left_sib, right_own, right_sib, columns, tile_rows, tile_cols, name):
    _, rows, tokens = left_own.shape
    left = pl.BlockSpec((2, tile_rows, tokens), lambda i, j, p: (0, i, 0))
    right = pl.BlockSpec((tokens, tile_cols), lambda i, j, p: (0, j))
    out = pl.BlockSpec((tile_rows, tile_cols), lambda i, j, p: (i, j))
    return pl.pallas_call(
        weight_kernel,
        grid_spec=pltpu.PrefetchScalarGridSpec(
            num_scalar_prefetch=1, grid=(rows // tile_rows, pl.cdiv(columns, tile_cols)),
            in_specs=[left, left, right, right], out_specs=[out, out],
            scratch_shapes=[pltpu.VMEM((2, tile_rows, tile_cols), jnp.bfloat16)],
        ),
        out_shape=[jax.ShapeDtypeStruct((rows, columns), jnp.bfloat16)] * 2,
        compiler_params=pltpu.CompilerParams(vmem_limit_bytes=VMEM_LIMIT),
        cost_estimate=QUICK,
        name=name,
    )(spot, left_own, left_sib, right_own, right_sib)


def turned_kernel(pos_ref, left_own, left_sib, right_own, right_sib, give_ref, keep_ref):
    total = _nn(left_own[...], right_own[...]) + _nn(left_sib[...], right_sib[...])
    total = total.astype(give_ref.dtype)

    @pl.when(pl.program_id(0) == 0)
    def _():
        give_ref[...] = total

    @pl.when(pl.program_id(0) == 1)
    def _():
        keep_ref[...] = total


def turned_weight_grads(spot, left_own, left_sib, right_own, right_sib, tile_rows, name):
    rows, tokens = left_own.shape
    columns = right_own.shape[1] // 2
    last = rows // tile_rows - 1
    left = pl.BlockSpec((tile_rows, tokens), lambda i, j, p: (j, 0))
    right = pl.BlockSpec((tokens, columns), lambda i, j, p: (0, jnp.where(i == 0, 1 - p[0], p[0])))
    return pl.pallas_call(
        turned_kernel,
        grid_spec=pltpu.PrefetchScalarGridSpec(
            num_scalar_prefetch=1, grid=(2, last + 1),
            in_specs=[left, left, right, right],
            out_specs=[
                pl.BlockSpec((tile_rows, columns), lambda i, j, p: (jnp.where(i == 0, j, last), 0)),
                pl.BlockSpec((tile_rows, columns), lambda i, j, p: (jnp.where(i == 0, 0, j), 0)),
            ],
        ),
        out_shape=[jax.ShapeDtypeStruct((rows, columns), jnp.bfloat16)] * 2,
        compiler_params=pltpu.CompilerParams(vmem_limit_bytes=VMEM_LIMIT),
        cost_estimate=QUICK,
        name=name,
    )(spot, left_own, left_sib, right_own, right_sib)


def qkv_weight_kernel(pos_ref, left_own, left_sib, q_own, q_sib, k_own, k_sib, v_own, v_sib,
                      give_ref, keep_ref, total_ref):
    pos = pos_ref[0]
    _, rows, length = left_own.shape
    span = q_own.shape[0]
    width = total_ref.shape[2]
    mine = pl.ds(pl.multiple_of(pos * span, 128), span)

    def rows_of(ref, cols):
        return ref[:, :, cols].reshape(2 * rows, -1)

    whole = pl.ds(0, length)
    for at, cols, own, sib in ((0, mine, q_own, q_sib), (1, whole, k_own, k_sib), (2, whole, v_own, v_sib)):
        total = _nn(rows_of(left_own, cols), own[:, 0:width]) + _nn(rows_of(left_sib, cols), sib[:, 0:width])
        total_ref[...] = total.astype(total_ref.dtype).reshape(total_ref.shape)
        give_ref[:, at * width : (at + 1) * width] = total_ref[1 - pos]
        keep_ref[:, at * width : (at + 1) * width] = total_ref[pos]


def qkv_weight_grads(spot, width, left_own, left_sib, *rights):
    rows = left_own.shape[1]
    length = left_own.shape[2]
    return _call(
        qkv_weight_kernel, "qkv_weight_grads", _vmem(8),
        [jax.ShapeDtypeStruct((rows, 3 * width), jnp.bfloat16)] * 2,
        [pltpu.VMEM((2, rows, width), jnp.bfloat16)],
        8 * rows * width * length * 5 // 2, 2 * (rows * width * 6 + 10 * length // 2 * width),
    )(spot, left_own, left_sib, *rights)


def input_kernel(pos_ref, wq_ref, wk_ref, wv_ref, gq_ref, gk_ref, gv_ref, mine_ref, theirs_ref):
    pos = pos_ref[0]
    span = gq_ref.shape[0]
    cols = pl.ds(0, wq_ref.shape[1])
    mine = pl.ds(pl.multiple_of(pos * span, 16), span)
    theirs = pl.ds(pl.multiple_of((1 - pos) * span, 16), span)
    wk, wv = wk_ref[...], wv_ref[...]
    theirs_ref[...] = (_nt(wk, gk_ref[theirs, cols]) + _nt(wv, gv_ref[theirs, cols])).astype(theirs_ref.dtype)
    mine_ref[...] = (
        _nt(wq_ref[...], gq_ref[:, cols]) + _nt(wk, gk_ref[mine, cols]) + _nt(wv, gv_ref[mine, cols])
    )


def input_grads(spot, wq, wk, wv, gq, gk, gv):
    span, width = gq.shape[0], wq.shape[0]
    return _call(
        input_kernel, "input_grads", _vmem(6),
        [
            jax.ShapeDtypeStruct((width, span), jnp.float32),
            jax.ShapeDtypeStruct((width, span), jnp.bfloat16),
        ],
        [], 10 * span * width * width, 2 * (3 * width * width + 8 * span * width),
    )(spot, wq, wk, wv, gq, gk, gv)


def token_kernel(pos_ref, mine_ref, other_ref, x_ref, gain_ref, middle_ref, out_ref):
    unit, rstd = centred_down(x_ref[...].astype(jnp.float32))
    scaled = (mine_ref[...] + other_ref[...].astype(jnp.float32)) * gain_ref[...]
    pulled = rstd * (
        scaled - jnp.mean(scaled, axis=0, keepdims=True)
        - unit * jnp.mean(scaled * unit, axis=0, keepdims=True)
    )
    out_ref[...] = (pulled + middle_ref[...].T).astype(out_ref.dtype)


def token_grads(spot, mine, other, tokens, gain, middle):
    width, span = mine.shape
    tile = 128
    cols = pl.BlockSpec((width, tile), lambda i, p: (0, i))
    return pl.pallas_call(
        token_kernel,
        grid_spec=pltpu.PrefetchScalarGridSpec(
            num_scalar_prefetch=1, grid=(span // tile,),
            in_specs=[
                cols, cols, cols,
                pl.BlockSpec((width, 1), lambda i, p: (0, 0)),
                pl.BlockSpec((tile, width), lambda i, p: (i, 0)),
            ],
            out_specs=cols,
        ),
        out_shape=jax.ShapeDtypeStruct((width, span), jnp.bfloat16),
        compiler_params=pltpu.CompilerParams(vmem_limit_bytes=VMEM_LIMIT),
        cost_estimate=QUICK,
        name="token_grads",
    )(spot, mine, other, tokens, gain, middle)


TAIL = "udovudoqququdotvqvqvudovquq"


def tie(values, *earlier):
    return lax.optimization_barrier((values, *earlier))[0]


def row_sum(values):
    return jnp.sum(values.astype(jnp.float32), axis=0)


def pick(values, index, axis):
    return lax.dynamic_index_in_dim(values, index, axis, keepdims=False)


def plus(left, right):
    return low(left.astype(jnp.float32) + right.astype(jnp.float32))


def spread(weight, bits):
    rows = weight.shape[0]
    count = 2 ** len(bits)
    size = -(-rows // (8 * count)) * 8
    index = jnp.int32(0)
    for bit in bits:
        index = index * 2 + has_bit(bit).astype(jnp.int32)
    piece = lax.dynamic_slice_in_dim(weight, jnp.minimum(index * size, rows - size), size, axis=0)
    got = yield cross(piece), piece
    for bit in bits[::-1]:
        other = yield swap(got, bit), got
        flag = has_bit(bit)
        parts = lax.optimization_barrier((choose(flag, other, got), choose(flag, got, other)))
        extra = count * size - rows if bit == bits[0] else 0
        if extra:
            kept = parts[1].shape[0] - size
            parts = parts[0], parts[1][:kept], parts[1][kept + extra :]
        got = jnp.concatenate(parts, axis=0)
    return got


def reduced(keep, give, bits, cut=False):
    if cut:
        most = give.shape[0] // 32 * 24
        above, below = give[:most], give[most:]
        above = yield cross(above), give
        below = yield cross(below), above
        got = jnp.concatenate([above, below], axis=0)
    else:
        got = yield cross(give), give
    values = plus(keep, got)
    stack = []
    for bit in bits[:-1]:
        lower, upper = halves(values)
        flag = has_bit(bit)
        got = yield swap(choose(flag, lower, upper), bit), values
        stack.append((bit, values.shape[0]))
        values = plus(choose(flag, upper, lower), got)
    got = yield swap(values, bits[-1]), values
    values = plus(values, got)
    for bit, rows in stack[::-1]:
        got = yield swap(values, bit), values
        both = in_order(bit, values, got)
        size = values.shape[0]
        if 2 * size != rows:
            both = jnp.concatenate([both[: rows - size], both[size:]], axis=0)
        values = both
    got = yield swap(values, CORE_BIT), values
    return in_order(CORE_BIT, values, got).astype(jnp.float32)


def vector_sum(packed):
    position = lax.axis_index("shard")
    got = yield swap(packed, CORE_BIT), packed
    packed = packed + got
    got = yield cross(pick(packed, 1 - position, 0)), packed
    kept = pick(packed, position, 0) + got
    for bit in all_bits():
        got = yield swap(kept, bit), kept
        kept = kept + got
    return kept


class Steps:
    def __init__(self, chain):
        self.chain = chain
        self.got, self.latest = next(chain)

    def step(self, *gates):
        got = tie(self.got, *gates) if gates else self.got
        self.got, self.latest = self.chain.send(got)

    def finish(self, *gates):
        if gates:
            self.got = tie(self.got, *gates)
        while True:
            try:
                self.step()
            except StopIteration as end:
                return end.value


def bound(values, *chains):
    parts = lax.optimization_barrier((*values, *[chain.got for chain in chains]))
    for chain, got in zip(chains, parts[len(values) :]):
        chain.got = got
    return parts[: len(values)]


def centred_down(values):
    off = values - jnp.mean(values, axis=0, keepdims=True)
    rstd = lax.rsqrt(jnp.mean(off * off, axis=0, keepdims=True) + EPSILON)
    return off * rstd, rstd


def on_device_pair(
    tokens, qkv_weight, out_weight, up_weight, down_weight, attn_gain, attn_shift, query_bias,
    value_bias, out_bias, mlp_gain, mlp_shift, up_bias, down_bias, cotangent,
):
    _, span, width = tokens.shape
    position = lax.axis_index("shard")
    spot = position.astype(jnp.int32).reshape(1)
    core = lax.axis_index("replica") & CORE_BIT
    bits = all_bits()
    fast_bits = [CORE_BIT] + bits[:2]
    turned_bits = [CORE_BIT] + bits[:2][::-1]
    first = position == 0

    own_turned = tokens.reshape(span, width).T
    down_turned = down_weight.T
    singles = (attn_gain, attn_shift, query_bias, value_bias, out_bias, mlp_gain, mlp_shift, down_bias)
    flat_vectors = jnp.concatenate(
        [item.reshape(1, -1) for item in singles] + [up_bias.reshape(-1, singles[0].shape[0])], axis=0
    )
    way_qkv = Steps(spread(qkv_weight, fast_bits))
    other_turned = cross(tie(own_turned, way_qkv.got))
    other_vectors = cross(tie(flat_vectors, way_qkv.got))
    way_qkv.step()
    way_out = Steps(spread(tie(out_weight, other_turned), turned_bits))
    way_up = Steps(spread(tie(up_weight, other_turned), turned_bits))
    grad_turned = cotangent.reshape(span, width).T
    grad_out = grad_turned.T
    grad_halves = grad_turned.reshape(2, width // 2, span)
    grad_left = pick(grad_halves, core, 0), swap(pick(grad_halves, 1 - core, 0), CORE_BIT)

    lower = choose(first, flat_vectors, other_vectors).astype(jnp.float32)
    upper = choose(first, other_vectors, flat_vectors).astype(jnp.float32)
    both = jnp.concatenate([lower, upper], axis=1)
    (gain_first, shift_first, bias_query, bias_value, bias_out, gain_second, shift_second,
     bias_down) = (both[i] for i in range(8))
    bias_up = jnp.concatenate([lower[8:].reshape(1, -1), upper[8:].reshape(1, -1)], axis=1)

    own_tokens = own_turned.T
    second = jnp.stack([bias_out, gain_second, shift_second])
    bias_down = bias_down.reshape(-1, 1)
    bias_up, own_tokens, second, bias_down, grad_out = bound((bias_up, own_tokens, second, bias_down, grad_out))
    way_qkv.step(bias_up, own_tokens, second, bias_down, grad_out)
    all_turned = jnp.concatenate(
        [choose(first, own_turned, other_turned), choose(first, other_turned, own_turned)], axis=1
    )
    unit_all, _ = centred_down(all_turned.astype(jnp.float32))
    normed_turned = low(unit_all * gain_first[:, None] + shift_first[:, None])
    normed_all = normed_turned.T
    normed = lax.dynamic_slice_in_dim(normed_all, position * span, span, axis=0)

    def for_cores(turned):
        parts = turned.reshape(2, 2, turned.shape[0] // 4, turned.shape[1])
        return pick(parts, core, 1), swap(pick(parts, 1 - core, 1), CORE_BIT)

    full_qkv = both_halves(qkv_weight, way_qkv.finish())
    full_q, full_k, full_v = (full_qkv[:, i * width : (i + 1) * width] for i in range(3))
    way_out.step(full_v)
    values = low(dot(tie(normed_all, way_out.latest), full_v) + bias_value)
    way_up.step(values)
    way_out.step(values)
    way_down = Steps(spread(tie(down_turned, way_up.latest), turned_bits))
    keys = low(dot(tie(normed_all, way_out.latest, way_up.latest), full_k))
    way_out.step(keys)
    queries = low(low(dot(tie(normed, way_out.latest), full_q) + bias_query) * SCALING)
    (queries,) = bound((queries,), way_up, way_down)
    way_up.step()
    way_down.step()
    context, context_t, lse = attention_forward(
        spot, tie(queries, way_up.latest, way_down.latest), keys, values, 1, span
    )
    context, context_t, lse = bound((context, context_t, lse), way_up, way_down, way_out)
    full_out = both_halves(out_weight, way_out.finish())
    way_up.step()
    way_down.step()
    context = tie(context, way_up.latest, way_down.latest)
    normed_left = for_cores(normed_turned)
    part_up = way_up.finish()
    active, slope, middle_turned, unit_second, rstd_second, two_turned = mlp_up(
        spot, context, full_out, own_tokens, second, bias_up, up_weight, part_up
    )
    active, slope, middle_turned, unit_second, rstd_second, two_turned = bound(
        (active, slope, middle_turned, unit_second, rstd_second, two_turned), way_down
    )
    way_down.step()

    active_sib = swap(active, CORE_BIT)
    give, keep_down = turned_weight_grads(
        spot, *grad_left, tie(active, way_down.latest), active_sib, width // 2, "down_grads"
    )
    sum_down = Steps(reduced(keep_down, give, bits, True))
    part_down = way_down.finish(give)
    block_out = mlp_down(
        spot, tie(active, give), down_turned, part_down, middle_turned, bias_down
    )

    two_left = for_cores(two_turned)
    context_left = for_cores(context_t)
    results = mlp_back(
        spot, tie(grad_out, block_out, *two_left, *context_left), slope, unit_second, rstd_second,
        gain_second.reshape(1, -1), full_out, down_turned, part_down, up_weight, part_up,
    )
    grad_hidden, grad_middle, grad_branch, grad_context, sum_hidden, sum_rows = bound(results, sum_down)
    sum_down.step()
    hidden_sib = swap(grad_hidden, CORE_BIT)
    branch_sib = swap(grad_branch, CORE_BIT)
    give_out, keep_out = weight_grads(
        spot, *context_left, grad_branch, branch_sib, width, context_left[0].shape[1], grad_branch.shape[1],
        "out_grads"
    )
    sum_out = Steps(reduced(keep_out, give_out, bits))
    give, keep_up = weight_grads(
        spot, *two_left, grad_hidden, tie(hidden_sib, give_out), grad_hidden.shape[1], two_left[0].shape[1],
        grad_hidden.shape[1] // 2, "up_grads"
    )
    give, keep_up = bound((give, keep_up), sum_down)
    sum_up = Steps(reduced(keep_up, give, bits, True))
    sum_down.step()
    grad_context = tie(grad_context, give, sum_down.latest)

    grad_q, grad_k, grad_v = attention_backward(
        spot, queries, keys, values, grad_context, context, lse, 1, span
    )
    grad_q, grad_k, grad_v = bound((grad_q, grad_k, grad_v), sum_down, sum_out, sum_up)
    sum_down.step()
    sum_out.step()
    sum_up.step()
    rights = []
    for part in (grad_q, grad_k, grad_v):
        rights += [part, swap(part, CORE_BIT)]
    mine, theirs = input_grads(
        spot, full_q, full_k, full_v, tie(grad_q, sum_down.latest, sum_out.latest, sum_up.latest), grad_k, grad_v
    )
    mine, theirs = bound((mine, theirs), sum_up, sum_down, sum_out)
    sum_up.step()
    sum_down.step()
    sum_out.step()
    rights[0] = tie(grad_q, sum_down.latest, sum_out.latest, sum_up.latest, theirs)
    give, keep_qkv = qkv_weight_grads(spot, width, *normed_left, *rights)
    give, keep_qkv = bound((give, keep_qkv), sum_out)
    sum_out.step()
    sum_qkv = Steps(reduced(keep_qkv, give, bits))

    other_part = cross(tie(theirs, sum_qkv.got))
    grad_middle, sum_rows, sum_hidden = bound((grad_middle, sum_rows, sum_hidden, give))[:3]

    unit_first, rstd_first = centred_down(own_turned.astype(jnp.float32))
    unit_other, _ = centred_down(other_turned.astype(jnp.float32))
    theirs_float = theirs.astype(jnp.float32)
    sums = (
        jnp.sum(mine * unit_first, axis=1) + jnp.sum(theirs_float * unit_other, axis=1),
        jnp.sum(mine, axis=1) + jnp.sum(theirs_float, axis=1),
        row_sum(grad_q)[:width],
        row_sum(grad_v)[:width],
        sum_rows[2],
        sum_rows[0],
        sum_rows[1],
        sum_hidden.reshape(-1),
        jnp.sum(grad_turned.astype(jnp.float32), axis=1),
    )
    small = jnp.stack([item.reshape(2, -1) for item in sums[:7] + sums[8:]], axis=1)
    small = jnp.concatenate([small, sums[7].reshape(2, -1, width // 2)], axis=1)
    sum_small = Steps(vector_sum(small))
    grad_tokens = token_grads(
        spot, mine, other_part, own_turned, gain_first.reshape(-1, 1), grad_middle
    )

    chains = {"d": sum_down, "u": sum_up, "q": sum_qkv, "o": sum_out, "v": sum_small}
    done = {}
    latest = give
    for name in TAIL:
        if name == "t":
            latest = grad_tokens
            continue
        chain = chains[name]
        try:
            chain.step(latest)
            latest = chain.latest
        except StopIteration as end:
            value = end.value
            if name in "do":
                (value,) = bound((value,), sum_qkv)
            done[name] = latest = value
    vectors_out = done["v"]
    outs = [vectors_out[i] for i in range(7)] + [vectors_out[8:].reshape(-1), vectors_out[7]]

    return (
        block_out.T.reshape(1, span, width),
        grad_tokens.T.reshape(1, span, width),
        done["q"], done["o"], done["u"], done["d"].T,
        *outs,
    )


def on_device_general(
    tokens, qkv_weight, out_weight, up_weight, down_weight, attn_gain, attn_shift, query_bias,
    value_bias, out_bias, mlp_gain, mlp_shift, up_bias, down_bias, cotangent,
):
    seqs, span, width = tokens.shape
    rows = seqs * span
    shards = lax.axis_size("shard")
    position = lax.axis_index("shard")
    core = lax.axis_index("replica") & CORE_BIT
    length = span * shards
    bits = all_bits()

    shards_of = (attn_gain, attn_shift, query_bias, value_bias, out_bias, mlp_gain, mlp_shift,
                 up_bias, down_bias)
    flat_vectors = jnp.concatenate(shards_of)
    all_vectors = lax.all_gather(flat_vectors, "shard", axis=0, tiled=False)
    vectors, at = [], 0
    for item in shards_of:
        size = item.shape[0]
        vectors.append(all_vectors[:, at : at + size].reshape(-1).astype(jnp.float32))
        at += size
    (gain_first, shift_first, bias_query, bias_value, bias_out, gain_second, shift_second, bias_up,
     bias_down) = vectors

    full_qkv, full_out, full_up, full_down = [
        lax.all_gather(item, "shard", axis=0, tiled=True)
        for item in (qkv_weight, out_weight, up_weight, down_weight)
    ]
    all_tokens = lax.all_gather(tokens, "shard", axis=1, tiled=True).reshape(-1, width)

    def own_rows(values):
        per_seq = values.reshape(seqs, length, values.shape[-1])
        return lax.dynamic_slice_in_dim(per_seq, position * span, span, axis=1).reshape(rows, -1)

    grad_out = cotangent.reshape(rows, width)
    grad_out_both = jnp.concatenate([grad_out, swap(grad_out, CORE_BIT)], axis=0)

    flat = tokens.reshape(rows, width).astype(jnp.float32)
    unit_all, rstd_all = centred(all_tokens.astype(jnp.float32))
    normed_all = low(unit_all * gain_first + shift_first)
    normed_sib = swap(normed_all, CORE_BIT)
    normed = own_rows(normed_all)
    full_q, full_k, full_v = (full_qkv[:, i * width : (i + 1) * width] for i in range(3))
    queries = low(low(dot(normed, full_q) + bias_query) * SCALING)
    keys = low(dot(normed_all, full_k))
    values = low(dot(normed_all, full_v) + bias_value)
    spot = position.astype(jnp.int32).reshape(1)
    context, context_t, lse = attention_forward(spot, queries, keys, values, seqs, span)
    context_sib = swap(context, CORE_BIT)
    middle = flat + dot(context, full_out) + bias_out
    unit_second, rstd_second = centred(middle)
    normed_two = low(unit_second * gain_second + shift_second)
    normed_two_sib = swap(normed_two, CORE_BIT)
    active_float, slope = gelu_parts(dot(normed_two, full_up) + bias_up)
    active = low(active_float)
    slope = low(slope)

    def split_rows(lhs, rhs):
        return lax.psum_scatter(low(dot_tn(lhs, rhs)), "shard", scatter_dimension=0, tiled=True)

    grouped = active.reshape(rows, shards, 2, -1)
    taken = jnp.where(core == 0, grouped[:, :, 0], grouped[:, :, 1]).reshape(rows, -1)
    given = jnp.where(core == 0, grouped[:, :, 1], grouped[:, :, 0]).reshape(rows, -1)
    active_both = jnp.concatenate([taken, swap(given, CORE_BIT)], axis=0)
    sum_down = split_rows(active_both, grad_out_both)
    sum_down = reduce_rest(sum_down, bits)
    sum_down = in_order(CORE_BIT, sum_down, swap(sum_down, CORE_BIT))

    result = middle + dot(active, full_down) + bias_down
    block_out = low(result).reshape(seqs, span, width)

    def by_columns(lhs_both, part):
        taken = columns_of(part, 1, core)
        given = columns_of(part, 1, 1 - core)
        return split_rows(lhs_both, jnp.concatenate([taken, swap(given, CORE_BIT)], axis=0))

    def join_columns(values):
        other = swap(values, CORE_BIT)
        left = choose(core == 0, values, other)
        right = choose(core == 0, other, values)
        return left, right

    grad_float = grad_out.astype(jnp.float32)
    grad_hidden = low(dot_nt(grad_out, full_down) * slope.astype(jnp.float32))
    normed_two_both = jnp.concatenate([normed_two, normed_two_sib], axis=0)
    sum_up = by_columns(normed_two_both, grad_hidden)
    sum_up = reduce_rest(sum_up, bits)
    sum_up = jnp.concatenate(join_columns(sum_up), axis=1)
    grad_normed_two = dot_nt(grad_hidden, full_up)
    grad_middle = norm_pull(grad_normed_two, unit_second, rstd_second, gain_second) + grad_float
    grad_branch = low(grad_middle)
    grad_context = low(dot_nt(grad_branch, full_out))
    context_both = jnp.concatenate([context, context_sib], axis=0)
    sum_out = by_columns(context_both, grad_branch)
    sum_out = reduce_rest(sum_out, bits)
    sum_out = jnp.concatenate(join_columns(sum_out), axis=1)

    grad_q, grad_k, grad_v = attention_backward(
        spot, queries, keys, values, grad_context, context, lse, seqs, span
    )
    grad_q, grad_k, grad_v = grad_q[:, :width], grad_k[:, :width], grad_v[:, :width]
    normed_both = jnp.concatenate([normed_all, normed_sib], axis=0)
    own_both = jnp.concatenate([normed, own_rows(normed_sib)], axis=0)
    third = width // 2
    half_q, half_k, half_v = (
        jnp.concatenate(
            [columns_of(part, 1, core), swap(columns_of(part, 1, 1 - core), CORE_BIT)], axis=0
        )
        for part in (grad_q, grad_k, grad_v)
    )
    sum_qkv = lax.psum_scatter(
        low(jnp.concatenate(
            [dot_tn(own_both, half_q), dot_tn(normed_both, half_k), dot_tn(normed_both, half_v)],
            axis=1,
        )),
        "shard", scatter_dimension=0, tiled=True,
    )
    sum_qkv = reduce_rest(sum_qkv, bits)
    left, right = join_columns(sum_qkv)
    sum_qkv = jnp.concatenate(
        [part[:, i * third : (i + 1) * third] for i in range(3) for part in (left, right)], axis=1
    )

    from_query = dot_nt(grad_q, full_q)
    from_rest = dot_nt(grad_k, full_k) + dot_nt(grad_v, full_v)
    grad_normed = from_query + lax.psum_scatter(
        from_rest.reshape(seqs, length, width), "shard", scatter_dimension=1, tiled=True
    ).reshape(rows, width)
    unit_first, rstd_first = own_rows(unit_all), own_rows(rstd_all)
    grad_tokens = low(norm_pull(grad_normed, unit_first, rstd_first, gain_first) + grad_middle)

    def column_sum(values):
        return jnp.sum(values.astype(jnp.float32), axis=0)

    sums = (
        column_sum(grad_normed * unit_first),
        column_sum(grad_normed),
        column_sum(grad_q),
        column_sum(grad_v),
        column_sum(grad_branch),
        column_sum(grad_normed_two * unit_second),
        column_sum(grad_normed_two),
        column_sum(grad_hidden),
        column_sum(grad_float),
    )
    packed = jnp.concatenate([item.reshape(shards, -1) for item in sums], axis=1)
    packed = lax.psum(packed, ("replica", "shard"))
    packed = lax.dynamic_index_in_dim(packed, position, axis=0, keepdims=False)
    outs, at = [], 0
    for item in sums:
        size = item.shape[0] // shards
        outs.append(packed[at : at + size])
        at += size
    return (
        block_out,
        grad_tokens.reshape(seqs, span, width),
        sum_qkv.astype(jnp.float32),
        sum_out.astype(jnp.float32),
        sum_up.astype(jnp.float32),
        sum_down.astype(jnp.float32),
        *outs,
    )


def on_device(tokens, *rest):
    if lax.axis_size("shard") == 2 and lax.axis_size("replica") >= 8 and tokens.shape[0] == 1:
        return on_device_pair(tokens, *rest)
    return on_device_general(tokens, *rest)


def solution(mesh):
    vector, matrix, rows = P("shard"), P("shard", None), P("replica", "shard", None)
    return jax.shard_map(
        on_device,
        mesh=mesh,
        in_specs=(rows, *[matrix] * 4, *[vector] * 9, rows),
        out_specs=(rows, rows, *[matrix] * 4, *[vector] * 9),
        check_vma=False,
    )
```

```python
import functools
import jax
import jax.numpy as jnp
from jax import lax
from jax.experimental import pallas as pl
from jax.experimental.pallas import tpu as pltpu
from jax.sharding import PartitionSpec as P

HD = 64
SCALING = 0.125
NEG = -1e30
LANES = 128
QUICK = pl.CostEstimate(flops=1, bytes_accessed=1, transcendentals=0)


def _nt(a, b):
    return lax.dot_general(a, b, (((1,), (1,)), ((), ())), preferred_element_type=jnp.float32)


def _nn(a, b):
    return lax.dot_general(a, b, (((1,), (0,)), ((), ())), preferred_element_type=jnp.float32)


def _lane_valid(shape, width):
    left = width - pl.program_id(1) * LANES
    return lax.broadcasted_iota(jnp.int32, shape, 1) < left


def _clean(ref, width):
    block = ref[...]
    return jnp.where(_lane_valid(block.shape, width), block, jnp.zeros_like(block))


def _head_part(block, head):
    lane = lax.broadcasted_iota(jnp.int32, block.shape, 1)
    keep = (lane < HD) if head == 0 else (lane >= HD)
    return jnp.where(keep, block, jnp.zeros_like(block))


def _diag_mask(keys, rows, first):
    key_at = lax.broadcasted_iota(jnp.int32, (keys, rows), 0)
    row_at = lax.broadcasted_iota(jnp.int32, (keys, rows), 1) + first
    return key_at <= row_at


def forward_kernel(pos_ref, q_ref, k_ref, v_ref, ctx_ref, ctx_t_ref, lse_ref, kc_ref, vt_ref, *, span, width):
    pos = pos_ref[0]
    block = min(512, span)
    queries = _clean(q_ref, width)
    kc_ref[...] = _clean(k_ref, width)
    length = k_ref.shape[0]
    for j in range(length // span):
        vt_ref[j] = _clean(v_ref.at[pl.ds(j * span, span), :], width).T
    chains = []
    for head in range(2):
        part = _head_part(queries, head)
        for at in range(0, span, block):
            chains.append((part[at : at + block], at))

    def update(state, scores, vt):
        peak, total, acc = state
        top = jnp.maximum(peak, jnp.max(scores, axis=0, keepdims=True))
        fade = jnp.exp(peak - top)
        expons = jnp.exp(scores - top)
        total = total * fade + jnp.sum(expons, axis=0, keepdims=True)
        acc = acc * fade + _nn(vt, expons.astype(jnp.bfloat16))
        return top, total, acc

    states = []
    own_vt = vt_ref[pos]
    for part, at in chains:
        keys = at + block
        own_k = kc_ref[pl.ds(pl.multiple_of(pos * span, span), keys), :]
        scores = jnp.where(_diag_mask(keys, block, at), _nt(own_k, part), NEG)
        peak = jnp.max(scores, axis=0, keepdims=True)
        expons = jnp.exp(scores - peak)
        total = jnp.sum(expons, axis=0, keepdims=True)
        acc = _nn(own_vt[:, :keys], expons.astype(jnp.bfloat16))
        states.append((peak, total, acc))

    def past(j, states):
        key_block = kc_ref[pl.ds(pl.multiple_of(j * span, span), span), :]
        vt = vt_ref[j]
        return tuple(
            update(state, _nt(key_block, part), vt) for state, (part, _) in zip(states, chains)
        )

    states = lax.fori_loop(0, pos, past, tuple(states))
    per_head = len(chains) // 2
    for i in range(per_head):
        at = i * block
        (peak0, total0, acc0), (peak1, total1, acc1) = states[i], states[per_head + i]
        row = lax.broadcasted_iota(jnp.int32, acc0.shape, 0)
        both = jnp.where(row < HD, acc0 / total0, acc1 / total1)
        ctx_ref[at : at + block, :] = both.T.astype(ctx_ref.dtype)
        ctx_t_ref[:, at : at + block] = both.astype(ctx_t_ref.dtype)
        lse_ref[0, 0:1, at : at + block] = peak0 + jnp.log(total0)
        lse_ref[0, 1:2, at : at + block] = peak1 + jnp.log(total1)


def backward_kernel(pos_ref, q_ref, k_ref, v_ref, g_ref, ctx_ref, lse_ref, dq_ref, dk_ref, dv_ref,
                    kc_ref, vc_ref, kt_ref, dk_acc, dv_acc, *, span, width):
    pos = pos_ref[0]
    block = min(512, span)
    queries = _clean(q_ref, width)
    grads = _clean(g_ref, width)
    context = _clean(ctx_ref, width)
    kc_ref[...] = _clean(k_ref, width)
    vc_ref[...] = _clean(v_ref, width)
    length = k_ref.shape[0]
    for j in range(length // span):
        kt_ref[j] = kc_ref[pl.ds(j * span, span), :].T
    dk_acc[...] = jnp.zeros_like(dk_acc)
    dv_acc[...] = jnp.zeros_like(dv_acc)
    product = (grads.astype(jnp.float32) * context.astype(jnp.float32)).T
    chains = []
    for head in range(2):
        q_part = _head_part(queries, head)
        g_part = _head_part(grads, head)
        inner = jnp.sum(product[head * HD : (head + 1) * HD], axis=0, keepdims=True)
        for at in range(0, span, block):
            chains.append((
                q_part[at : at + block], g_part[at : at + block], inner[:, at : at + block],
                lse_ref[0, head : head + 1, at : at + block], at,
            ))

    def piece(chain, key_block, value_block, kt, masked):
        q_part, g_part, inner, lse, at = chain
        scores = _nt(key_block, q_part)
        if masked:
            scores = jnp.where(_diag_mask(key_block.shape[0], q_part.shape[0], at), scores, NEG)
        probs = jnp.exp(scores - lse)
        grad_probs = _nt(value_block, g_part)
        grad_scores = (probs * (grad_probs - inner)).astype(jnp.bfloat16)
        dq = _nn(kt, grad_scores)
        dk = _nn(grad_scores, q_part)
        dv = _nn(probs.astype(jnp.bfloat16), g_part)
        return dq, dk, dv

    start = pl.multiple_of(pos * span, span)
    own_kt = kt_ref[pos]
    dqs = []
    for chain in chains:
        keys = chain[4] + block
        where = pl.ds(start, keys)
        dq, dk, dv = piece(chain, kc_ref[where, :], vc_ref[where, :], own_kt[:, :keys], True)
        dk_acc[where, :] += dk
        dv_acc[where, :] += dv
        dqs.append(dq)

    def past(j, dqs):
        where = pl.ds(pl.multiple_of(j * span, span), span)
        key_block, value_block, kt = kc_ref[where, :], vc_ref[where, :], kt_ref[j]
        out, dk_sum, dv_sum = [], None, None
        for chain, dq_old in zip(chains, dqs):
            dq, dk, dv = piece(chain, key_block, value_block, kt, False)
            dk_sum = dk if dk_sum is None else dk_sum + dk
            dv_sum = dv if dv_sum is None else dv_sum + dv
            out.append(dq_old + dq)
        dk_acc[where, :] = dk_sum
        dv_acc[where, :] = dv_sum
        return tuple(out)

    dqs = lax.fori_loop(0, pos, past, tuple(dqs))
    per_head = len(chains) // 2
    for i in range(per_head):
        at = i * block
        row = lax.broadcasted_iota(jnp.int32, dqs[0].shape, 0)
        both = jnp.where(row < HD, dqs[i], dqs[per_head + i]) * SCALING
        dq_ref[at : at + block, :] = both.T.astype(dq_ref.dtype)
    dk_ref[...] = dk_acc[...].astype(dk_ref.dtype)
    dv_ref[...] = dv_acc[...].astype(dv_ref.dtype)


def attention_forward(position, queries, keys, values, seqs, span):
    rows, width = queries.shape
    length = keys.shape[0] // seqs
    pairs = pl.cdiv(width, LANES)
    own = pl.BlockSpec((span, LANES), lambda s, h, p: (s, h))
    whole = pl.BlockSpec((length, LANES), lambda s, h, p: (s, h))
    lse = pl.BlockSpec((1, 2, span), lambda s, h, p: (s * pairs + h, 0, 0))
    return pl.pallas_call(
        functools.partial(forward_kernel, span=span, width=width),
        grid_spec=pltpu.PrefetchScalarGridSpec(
            num_scalar_prefetch=1,
            grid=(seqs, pairs),
            in_specs=[own, whole, whole],
            out_specs=[own, pl.BlockSpec((LANES, span), lambda s, h, p: (h, s)), lse],
            scratch_shapes=[
                pltpu.VMEM((length, LANES), jnp.bfloat16),
                pltpu.VMEM((length // span, LANES, span), jnp.bfloat16),
            ],
        ),
        out_shape=[
            jax.ShapeDtypeStruct((rows, width), jnp.bfloat16),
            jax.ShapeDtypeStruct((width, rows), jnp.bfloat16),
            jax.ShapeDtypeStruct((seqs * pairs, 2, span), jnp.float32),
        ],
        compiler_params=pltpu.CompilerParams(vmem_limit_bytes=48 * 1024 * 1024),
        cost_estimate=QUICK,
        name="attention_forward",
    )(position, queries, keys, values)


def attention_backward(position, queries, keys, values, grads, context, lse_rows, seqs, span):
    rows, width = queries.shape
    length = keys.shape[0] // seqs
    pairs = pl.cdiv(width, LANES)
    own = pl.BlockSpec((span, LANES), lambda s, h, p: (s, h))
    whole = pl.BlockSpec((length, LANES), lambda s, h, p: (s, h))
    lse = pl.BlockSpec((1, 2, span), lambda s, h, p: (s * pairs + h, 0, 0))
    return pl.pallas_call(
        functools.partial(backward_kernel, span=span, width=width),
        grid_spec=pltpu.PrefetchScalarGridSpec(
            num_scalar_prefetch=1,
            grid=(seqs, pairs),
            in_specs=[own, whole, whole, own, own, lse],
            out_specs=[own, whole, whole],
            scratch_shapes=[
                pltpu.VMEM((length, LANES), jnp.bfloat16),
                pltpu.VMEM((length, LANES), jnp.bfloat16),
                pltpu.VMEM((length // span, LANES, span), jnp.bfloat16),
                pltpu.VMEM((length, LANES), jnp.float32),
                pltpu.VMEM((length, LANES), jnp.float32),
            ],
        ),
        out_shape=[
            jax.ShapeDtypeStruct((rows, pairs * LANES), jnp.bfloat16),
            jax.ShapeDtypeStruct((keys.shape[0], pairs * LANES), jnp.bfloat16),
            jax.ShapeDtypeStruct((keys.shape[0], pairs * LANES), jnp.bfloat16),
        ],
        compiler_params=pltpu.CompilerParams(vmem_limit_bytes=48 * 1024 * 1024),
        cost_estimate=QUICK,
        name="attention_backward",
    )(position, queries, keys, values, grads, context, lse_rows)


EPSILON = 1e-05
CORE_BIT = 1


def centred(values):
    average = jnp.mean(values, axis=-1, keepdims=True)
    off = values - average
    rstd = lax.rsqrt(jnp.mean(off * off, axis=-1, keepdims=True) + EPSILON)
    return off * rstd, rstd


def norm_pull(grad, unit, rstd, gain):
    scaled = grad * gain
    first = jnp.mean(scaled, axis=-1, keepdims=True)
    second = jnp.mean(scaled * unit, axis=-1, keepdims=True)
    return rstd * (scaled - first - unit * second)


def gelu_parts(values):
    square = values * values
    tanh = jnp.tanh(0.7978845608 * values * (1.0 + 0.044715 * square))
    half = 0.5 * (1.0 + tanh)
    slope = half + 0.5 * values * (1.0 - tanh * tanh) * (
        0.7978845608 * (1.0 + 3.0 * 0.044715 * square)
    )
    return values * half, slope


def dot(left, right):
    return jnp.dot(left, right, preferred_element_type=jnp.float32)


def dot_nt(left, right):
    return lax.dot_general(
        left, right, (((1,), (1,)), ((), ())), preferred_element_type=jnp.float32
    )


def dot_tn(left, right):
    return lax.dot_general(
        left, right, (((0,), (0,)), ((), ())), preferred_element_type=jnp.float32
    )


def low(values):
    return values.astype(jnp.bfloat16)


def swap(values, bit):
    size = lax.axis_size("replica")
    return lax.ppermute(values, "replica", [(i, i ^ bit) for i in range(size)])


def cross(values):
    return lax.ppermute(values, "shard", [(0, 1), (1, 0)])


def has_bit(bit):
    return (lax.axis_index("replica") & bit) != 0


def choose(flag, left, right):
    return jnp.where(flag, left, right)


def in_order(bit, mine, other):
    flag = has_bit(bit)
    return jnp.concatenate([choose(flag, other, mine), choose(flag, mine, other)], axis=0)


def both_halves(weight, got):
    first = lax.axis_index("shard") == 0
    return jnp.concatenate([choose(first, weight, got), choose(first, got, weight)], axis=0)


def all_bits():
    bits, bit = [], 2
    while bit < lax.axis_size("replica"):
        bits.append(bit)
        bit *= 2
    return bits


def halves(values):
    rows = values.shape[0]
    size = -(-rows // 16) * 8
    return values[:size], values[rows - size :]


def reduce_rest(values, bits):
    stack = []
    for bit in bits[:-1]:
        lower, upper = halves(values)
        flag = has_bit(bit)
        sent = swap(choose(flag, lower, upper), bit)
        stack.append((bit, values.shape[0]))
        values = low(choose(flag, upper, lower).astype(jnp.float32) + sent.astype(jnp.float32))
    values = low(values.astype(jnp.float32) + swap(values, bits[-1]).astype(jnp.float32))
    for bit, rows in stack[::-1]:
        both = in_order(bit, values, swap(values, bit))
        size = values.shape[0]
        if 2 * size != rows:
            both = jnp.concatenate([both[: rows - size], both[size:]], axis=0)
        values = both
    return values


def columns_of(values, axis, index):
    size = values.shape[axis] // 2
    low_part = lax.slice_in_dim(values, 0, size, axis=axis)
    high_part = lax.slice_in_dim(values, size, 2 * size, axis=axis)
    return choose(index == 0, low_part, high_part)


VMEM_LIMIT = 60 * 1024 * 1024
CHUNK = 256


def _vmem(count):
    return [pl.BlockSpec(memory_space=pltpu.VMEM)] * count


def _call(kernel, name, in_specs, out_shapes, scratch, flops, moved):
    return pl.pallas_call(
        kernel,
        grid_spec=pltpu.PrefetchScalarGridSpec(
            num_scalar_prefetch=1, grid=(1,), in_specs=in_specs,
            out_specs=[pl.BlockSpec(memory_space=pltpu.VMEM)] * len(out_shapes),
            scratch_shapes=scratch,
        ),
        out_shape=out_shapes,
        compiler_params=pltpu.CompilerParams(vmem_limit_bytes=VMEM_LIMIT),
        cost_estimate=QUICK,
        name=name,
    )


def _fetch(own_ref, got_ref, full_ref, sems, pos, at, width):
    rows = own_ref.shape[0]
    cols = pl.ds(at, width)
    mine = pl.ds(pl.multiple_of(pos * rows, 16), rows)
    theirs = pl.ds(pl.multiple_of((1 - pos) * rows, 16), rows)
    return (
        pltpu.make_async_copy(own_ref.at[:, cols], full_ref.at[mine, cols], sems.at[0]),
        pltpu.make_async_copy(got_ref.at[:, cols], full_ref.at[theirs, cols], sems.at[1]),
    )


def up_kernel(pos_ref, ctx_ref, out_w_ref, x_ref, vec_ref, bias_ref, own_ref, got_ref,
              act_ref, slope_ref, mid_t_ref, unit_ref, rstd_ref, nt_t_ref, nt_ref, full_ref, sems):
    pos = pos_ref[0]
    units = own_ref.shape[1]
    count = units // CHUNK
    copies = [_fetch(own_ref, got_ref, full_ref, sems.at[j], pos, j * CHUNK, CHUNK) for j in range(count)]
    for pair in copies:
        for copy in pair:
            copy.start()
    unit_ref[...] = _nn(ctx_ref[...], out_w_ref[...])
    rows = ctx_ref.shape[0]
    tile = 128
    for at in range(0, rows, tile):
        where = slice(at, at + tile)
        middle = x_ref[where, :].astype(jnp.float32) + (unit_ref[where, :] + vec_ref[0:1, :])
        unit, rstd = centred(middle)
        normed = unit * vec_ref[1:2, :] + vec_ref[2:3, :]
        unit_ref[where, :] = unit
        rstd_ref[where, :] = rstd
        mid_t_ref[:, where] = middle.T
        nt_ref[where, :] = normed.astype(jnp.bfloat16)
        nt_t_ref[:, where] = normed.T.astype(jnp.bfloat16)
    for pair in copies:
        for copy in pair:
            copy.wait()
    normed = nt_ref[...]
    for j in range(count):
        cols = pl.ds(j * CHUNK, CHUNK)
        hidden = _nn(normed, full_ref[:, cols]) + bias_ref[:, cols]
        value, slope = gelu_parts(hidden)
        act_ref[:, cols] = value.astype(jnp.bfloat16)
        slope_ref[:, cols] = slope.astype(jnp.bfloat16)


def mlp_up(spot, context, out_weight, tokens, vectors, bias, own, got):
    rows, width = tokens.shape
    units = own.shape[1]
    any_spec = pl.BlockSpec(memory_space=pl.ANY)
    return _call(
        up_kernel, "mlp_up", _vmem(5) + [any_spec] * 2,
        [
            jax.ShapeDtypeStruct((rows, units), jnp.bfloat16),
            jax.ShapeDtypeStruct((rows, units), jnp.bfloat16),
            jax.ShapeDtypeStruct((width, rows), jnp.float32),
            jax.ShapeDtypeStruct((rows, width), jnp.float32),
            jax.ShapeDtypeStruct((rows, 1), jnp.float32),
            jax.ShapeDtypeStruct((width, rows), jnp.bfloat16),
        ],
        [
            pltpu.VMEM((rows, width), jnp.bfloat16),
            pltpu.VMEM((width, units), jnp.bfloat16),
            pltpu.SemaphoreType.DMA((units // CHUNK, 2)),
        ],
        2 * rows * width * (units + width), 2 * units * (width + 2 * rows) + 18 * rows * width,
    )(spot, context, out_weight, tokens, vectors, bias, own, got)


def down_kernel(pos_ref, act_ref, own_ref, got_ref, middle_ref, bias_ref, out_ref):
    pos = pos_ref[0]
    half = own_ref.shape[1]
    mine = pl.ds(pl.multiple_of(pos * half, 128), half)
    theirs = pl.ds(pl.multiple_of((1 - pos) * half, 128), half)
    total = _nt(own_ref[...], act_ref[:, mine]) + _nt(got_ref[...], act_ref[:, theirs])
    out_ref[...] = (middle_ref[...] + total + bias_ref[...]).astype(out_ref.dtype)


def mlp_down(spot, active, own, got, middle, bias):
    width, rows = middle.shape
    half = own.shape[1]
    tile = width // 4
    return pl.pallas_call(
        down_kernel,
        grid_spec=pltpu.PrefetchScalarGridSpec(
            num_scalar_prefetch=1, grid=(width // tile,),
            in_specs=[
                pl.BlockSpec((rows, 2 * half), lambda i, p: (0, 0)),
                pl.BlockSpec((tile, half), lambda i, p: (i, 0)),
                pl.BlockSpec((tile, half), lambda i, p: (i, 0)),
                pl.BlockSpec((tile, rows), lambda i, p: (i, 0)),
                pl.BlockSpec((tile, 1), lambda i, p: (i, 0)),
            ],
            out_specs=pl.BlockSpec((tile, rows), lambda i, p: (i, 0)),
        ),
        out_shape=jax.ShapeDtypeStruct((width, rows), jnp.bfloat16),
        compiler_params=pltpu.CompilerParams(vmem_limit_bytes=VMEM_LIMIT),
        cost_estimate=QUICK,
        name="mlp_down",
    )(spot, active, own, got, middle, bias)


def back_kernel(pos_ref, grad_ref, slope_ref, unit_ref, rstd_ref, gain_ref, out_w_ref,
                down_own, down_got, up_own, up_got,
                hidden_ref, middle_ref, branch_ref, context_ref, wide_sum_ref, sum_ref,
                down_full, up_full, sems):
    pos = pos_ref[0]
    half = down_own.shape[1]
    units = up_own.shape[1]
    rows, width = grad_ref.shape
    mine = pl.ds(pl.multiple_of(pos * half, 128), half)
    theirs = pl.ds(pl.multiple_of((1 - pos) * half, 128), half)
    first = pltpu.make_async_copy(down_own, down_full.at[:, mine], sems.at[0])
    second = pltpu.make_async_copy(down_got, down_full.at[:, theirs], sems.at[1])
    first.start()
    second.start()
    rows_up = up_own.shape[0]
    third = pltpu.make_async_copy(up_own, up_full.at[pl.ds(pl.multiple_of(pos * rows_up, 16), rows_up), :], sems.at[2])
    fourth = pltpu.make_async_copy(up_got, up_full.at[pl.ds(pl.multiple_of((1 - pos) * rows_up, 16), rows_up), :], sems.at[3])
    third.start()
    fourth.start()
    first.wait()
    second.wait()
    grad = grad_ref[...]
    for j in range(units // CHUNK):
        cols = pl.ds(j * CHUNK, CHUNK)
        active = _nn(grad, down_full[:, cols])
        hidden = (active * slope_ref[:, cols].astype(jnp.float32)).astype(jnp.bfloat16)
        hidden_ref[:, cols] = hidden
        wide_sum_ref[:, cols] = jnp.sum(hidden.astype(jnp.float32), axis=0, keepdims=True)
    third.wait()
    fourth.wait()
    hidden = hidden_ref[...]
    for at in range(0, width, CHUNK):
        size = min(CHUNK, width - at)
        middle_ref[:, at : at + size] = _nt(hidden, up_full[at : at + size, :])
    sum_ref[...] = jnp.zeros_like(sum_ref)
    branch_ref[...] = jnp.zeros_like(branch_ref)
    tile = 128
    for at in range(0, rows, tile):
        where = slice(at, at + tile)
        normed = middle_ref[where, :]
        unit = unit_ref[where, :]
        out = norm_pull(normed, unit, rstd_ref[where, :], gain_ref[...])
        out = out + grad_ref[where, :].astype(jnp.float32)
        branch = out.astype(jnp.bfloat16)
        middle_ref[where, :] = out
        branch_ref[where, 0:width] = branch
        sum_ref[0:1, :] += jnp.sum(normed * unit, axis=0, keepdims=True)
        sum_ref[1:2, :] += jnp.sum(normed, axis=0, keepdims=True)
        sum_ref[2:3, :] += jnp.sum(branch.astype(jnp.float32), axis=0, keepdims=True)
    context_ref[...] = _nt(branch_ref[:, 0:width], out_w_ref[...]).astype(context_ref.dtype)


def mlp_back(spot, grad, slope, unit, rstd, gain, out_weight, down_own, down_got, up_own, up_got):
    rows, width = grad.shape
    units = up_own.shape[1]
    any_spec = pl.BlockSpec(memory_space=pl.ANY)
    return _call(
        back_kernel, "mlp_back", _vmem(6) + [any_spec] * 4,
        [
            jax.ShapeDtypeStruct((rows, units), jnp.bfloat16),
            jax.ShapeDtypeStruct((rows, width), jnp.float32),
            jax.ShapeDtypeStruct((rows, pl.cdiv(width, LANES) * LANES), jnp.bfloat16),
            jax.ShapeDtypeStruct((rows, width), jnp.bfloat16),
            jax.ShapeDtypeStruct((1, units), jnp.float32),
            jax.ShapeDtypeStruct((8, width), jnp.float32),
        ],
        [
            pltpu.VMEM((width, units), jnp.bfloat16),
            pltpu.VMEM((width, units), jnp.bfloat16),
            pltpu.SemaphoreType.DMA((4,)),
        ],
        4 * rows * width * units + 2 * rows * width * width, 4 * units * (width + rows) + 12 * rows * width,
    )(spot, grad, slope, unit, rstd, gain, out_weight, down_own, down_got, up_own, up_got)


def weight_kernel(pos_ref, left_own, left_sib, right_own, right_sib, give_ref, keep_ref, total_ref):
    pos = pos_ref[0]
    _, rows, tokens = left_own.shape
    own = left_own[...].reshape(2 * rows, tokens)
    sib = left_sib[...].reshape(2 * rows, tokens)
    total = _nn(own, right_own[...]) + _nn(sib, right_sib[...])
    total_ref[...] = total.astype(total_ref.dtype).reshape(total_ref.shape)
    give_ref[...] = total_ref[1 - pos]
    keep_ref[...] = total_ref[pos]


def weight_grads(spot, left_own, left_sib, right_own, right_sib, columns, tile_rows, tile_cols, name):
    _, rows, tokens = left_own.shape
    left = pl.BlockSpec((2, tile_rows, tokens), lambda i, j, p: (0, i, 0))
    right = pl.BlockSpec((tokens, tile_cols), lambda i, j, p: (0, j))
    out = pl.BlockSpec((tile_rows, tile_cols), lambda i, j, p: (i, j))
    return pl.pallas_call(
        weight_kernel,
        grid_spec=pltpu.PrefetchScalarGridSpec(
            num_scalar_prefetch=1, grid=(rows // tile_rows, pl.cdiv(columns, tile_cols)),
            in_specs=[left, left, right, right], out_specs=[out, out],
            scratch_shapes=[pltpu.VMEM((2, tile_rows, tile_cols), jnp.bfloat16)],
        ),
        out_shape=[jax.ShapeDtypeStruct((rows, columns), jnp.bfloat16)] * 2,
        compiler_params=pltpu.CompilerParams(vmem_limit_bytes=VMEM_LIMIT),
        cost_estimate=QUICK,
        name=name,
    )(spot, left_own, left_sib, right_own, right_sib)


def turned_kernel(pos_ref, left_own, left_sib, right_own, right_sib, give_ref, keep_ref):
    total = _nn(left_own[...], right_own[...]) + _nn(left_sib[...], right_sib[...])
    total = total.astype(give_ref.dtype)

    @pl.when(pl.program_id(0) == 0)
    def _():
        give_ref[...] = total

    @pl.when(pl.program_id(0) == 1)
    def _():
        keep_ref[...] = total


def turned_weight_grads(spot, left_own, left_sib, right_own, right_sib, tile_rows, name):
    rows, tokens = left_own.shape
    columns = right_own.shape[1] // 2
    last = rows // tile_rows - 1
    left = pl.BlockSpec((tile_rows, tokens), lambda i, j, p: (j, 0))
    right = pl.BlockSpec((tokens, columns), lambda i, j, p: (0, jnp.where(i == 0, 1 - p[0], p[0])))
    return pl.pallas_call(
        turned_kernel,
        grid_spec=pltpu.PrefetchScalarGridSpec(
            num_scalar_prefetch=1, grid=(2, last + 1),
            in_specs=[left, left, right, right],
            out_specs=[
                pl.BlockSpec((tile_rows, columns), lambda i, j, p: (jnp.where(i == 0, j, last), 0)),
                pl.BlockSpec((tile_rows, columns), lambda i, j, p: (jnp.where(i == 0, 0, j), 0)),
            ],
        ),
        out_shape=[jax.ShapeDtypeStruct((rows, columns), jnp.bfloat16)] * 2,
        compiler_params=pltpu.CompilerParams(vmem_limit_bytes=VMEM_LIMIT),
        cost_estimate=QUICK,
        name=name,
    )(spot, left_own, left_sib, right_own, right_sib)


def qkv_weight_kernel(pos_ref, left_own, left_sib, q_own, q_sib, k_own, k_sib, v_own, v_sib,
                      give_ref, keep_ref, total_ref):
    pos = pos_ref[0]
    _, rows, length = left_own.shape
    span = q_own.shape[0]
    width = total_ref.shape[2]
    mine = pl.ds(pl.multiple_of(pos * span, 128), span)

    def rows_of(ref, cols):
        return ref[:, :, cols].reshape(2 * rows, -1)

    whole = pl.ds(0, length)
    for at, cols, own, sib in ((0, mine, q_own, q_sib), (1, whole, k_own, k_sib), (2, whole, v_own, v_sib)):
        total = _nn(rows_of(left_own, cols), own[:, 0:width]) + _nn(rows_of(left_sib, cols), sib[:, 0:width])
        total_ref[...] = total.astype(total_ref.dtype).reshape(total_ref.shape)
        give_ref[:, at * width : (at + 1) * width] = total_ref[1 - pos]
        keep_ref[:, at * width : (at + 1) * width] = total_ref[pos]


def qkv_weight_grads(spot, width, left_own, left_sib, *rights):
    rows = left_own.shape[1]
    length = left_own.shape[2]
    return _call(
        qkv_weight_kernel, "qkv_weight_grads", _vmem(8),
        [jax.ShapeDtypeStruct((rows, 3 * width), jnp.bfloat16)] * 2,
        [pltpu.VMEM((2, rows, width), jnp.bfloat16)],
        8 * rows * width * length * 5 // 2, 2 * (rows * width * 6 + 10 * length // 2 * width),
    )(spot, left_own, left_sib, *rights)


def input_kernel(pos_ref, wq_ref, wk_ref, wv_ref, gq_ref, gk_ref, gv_ref, mine_ref, theirs_ref):
    pos = pos_ref[0]
    span = gq_ref.shape[0]
    cols = pl.ds(0, wq_ref.shape[1])
    mine = pl.ds(pl.multiple_of(pos * span, 16), span)
    theirs = pl.ds(pl.multiple_of((1 - pos) * span, 16), span)
    wk, wv = wk_ref[...], wv_ref[...]
    theirs_ref[...] = (_nt(wk, gk_ref[theirs, cols]) + _nt(wv, gv_ref[theirs, cols])).astype(theirs_ref.dtype)
    mine_ref[...] = (
        _nt(wq_ref[...], gq_ref[:, cols]) + _nt(wk, gk_ref[mine, cols]) + _nt(wv, gv_ref[mine, cols])
    )


def input_grads(spot, wq, wk, wv, gq, gk, gv):
    span, width = gq.shape[0], wq.shape[0]
    return _call(
        input_kernel, "input_grads", _vmem(6),
        [
            jax.ShapeDtypeStruct((width, span), jnp.float32),
            jax.ShapeDtypeStruct((width, span), jnp.bfloat16),
        ],
        [], 10 * span * width * width, 2 * (3 * width * width + 8 * span * width),
    )(spot, wq, wk, wv, gq, gk, gv)


def token_kernel(pos_ref, mine_ref, other_ref, x_ref, gain_ref, middle_ref, out_ref):
    unit, rstd = centred_down(x_ref[...].astype(jnp.float32))
    scaled = (mine_ref[...] + other_ref[...].astype(jnp.float32)) * gain_ref[...]
    pulled = rstd * (
        scaled - jnp.mean(scaled, axis=0, keepdims=True)
        - unit * jnp.mean(scaled * unit, axis=0, keepdims=True)
    )
    out_ref[...] = (pulled + middle_ref[...].T).astype(out_ref.dtype)


def token_grads(spot, mine, other, tokens, gain, middle):
    width, span = mine.shape
    tile = 128
    cols = pl.BlockSpec((width, tile), lambda i, p: (0, i))
    return pl.pallas_call(
        token_kernel,
        grid_spec=pltpu.PrefetchScalarGridSpec(
            num_scalar_prefetch=1, grid=(span // tile,),
            in_specs=[
                cols, cols, cols,
                pl.BlockSpec((width, 1), lambda i, p: (0, 0)),
                pl.BlockSpec((tile, width), lambda i, p: (i, 0)),
            ],
            out_specs=cols,
        ),
        out_shape=jax.ShapeDtypeStruct((width, span), jnp.bfloat16),
        compiler_params=pltpu.CompilerParams(vmem_limit_bytes=VMEM_LIMIT),
        cost_estimate=QUICK,
        name="token_grads",
    )(spot, mine, other, tokens, gain, middle)


TAIL = "udovudoqququdotvqvqvudovquq"


def tie(values, *earlier):
    return lax.optimization_barrier((values, *earlier))[0]


def row_sum(values):
    return jnp.sum(values.astype(jnp.float32), axis=0)


def pick(values, index, axis):
    return lax.dynamic_index_in_dim(values, index, axis, keepdims=False)


def plus(left, right):
    return low(left.astype(jnp.float32) + right.astype(jnp.float32))


def spread(weight, bits):
    rows = weight.shape[0]
    count = 2 ** len(bits)
    size = -(-rows // (8 * count)) * 8
    index = jnp.int32(0)
    for bit in bits:
        index = index * 2 + has_bit(bit).astype(jnp.int32)
    piece = lax.dynamic_slice_in_dim(weight, jnp.minimum(index * size, rows - size), size, axis=0)
    got = yield cross(piece), piece
    for bit in bits[::-1]:
        other = yield swap(got, bit), got
        flag = has_bit(bit)
        parts = lax.optimization_barrier((choose(flag, other, got), choose(flag, got, other)))
        extra = count * size - rows if bit == bits[0] else 0
        if extra:
            kept = parts[1].shape[0] - size
            parts = parts[0], parts[1][:kept], parts[1][kept + extra :]
        got = jnp.concatenate(parts, axis=0)
    return got


def reduced(keep, give, bits, cut=False):
    if cut:
        most = give.shape[0] // 32 * 24
        above, below = give[:most], give[most:]
        above = yield cross(above), give
        below = yield cross(below), above
        got = jnp.concatenate([above, below], axis=0)
    else:
        got = yield cross(give), give
    values = plus(keep, got)
    stack = []
    for bit in bits[:-1]:
        lower, upper = halves(values)
        flag = has_bit(bit)
        got = yield swap(choose(flag, lower, upper), bit), values
        stack.append((bit, values.shape[0]))
        values = plus(choose(flag, upper, lower), got)
    got = yield swap(values, bits[-1]), values
    values = plus(values, got)
    for bit, rows in stack[::-1]:
        got = yield swap(values, bit), values
        both = in_order(bit, values, got)
        size = values.shape[0]
        if 2 * size != rows:
            both = jnp.concatenate([both[: rows - size], both[size:]], axis=0)
        values = both
    got = yield swap(values, CORE_BIT), values
    return in_order(CORE_BIT, values, got).astype(jnp.float32)


def vector_sum(packed):
    position = lax.axis_index("shard")
    got = yield swap(packed, CORE_BIT), packed
    packed = packed + got
    got = yield cross(pick(packed, 1 - position, 0)), packed
    kept = pick(packed, position, 0) + got
    for bit in all_bits():
        got = yield swap(kept, bit), kept
        kept = kept + got
    return kept


class Steps:
    def __init__(self, chain):
        self.chain = chain
        self.got, self.latest = next(chain)

    def step(self, *gates):
        got = tie(self.got, *gates) if gates else self.got
        self.got, self.latest = self.chain.send(got)

    def finish(self, *gates):
        if gates:
            self.got = tie(self.got, *gates)
        while True:
            try:
                self.step()
            except StopIteration as end:
                return end.value


def bound(values, *chains):
    parts = lax.optimization_barrier((*values, *[chain.got for chain in chains]))
    for chain, got in zip(chains, parts[len(values) :]):
        chain.got = got
    return parts[: len(values)]


def centred_down(values):
    off = values - jnp.mean(values, axis=0, keepdims=True)
    rstd = lax.rsqrt(jnp.mean(off * off, axis=0, keepdims=True) + EPSILON)
    return off * rstd, rstd


def on_device_pair(
    tokens, qkv_weight, out_weight, up_weight, down_weight, attn_gain, attn_shift, query_bias,
    value_bias, out_bias, mlp_gain, mlp_shift, up_bias, down_bias, cotangent,
):
    _, span, width = tokens.shape
    position = lax.axis_index("shard")
    spot = position.astype(jnp.int32).reshape(1)
    core = lax.axis_index("replica") & CORE_BIT
    bits = all_bits()
    fast_bits = [CORE_BIT] + bits[:2]
    turned_bits = [CORE_BIT] + bits[:2][::-1]
    first = position == 0

    own_turned = tokens.reshape(span, width).T
    down_turned = down_weight.T
    singles = (attn_gain, attn_shift, query_bias, value_bias, out_bias, mlp_gain, mlp_shift, down_bias)
    flat_vectors = jnp.concatenate(
        [item.reshape(1, -1) for item in singles] + [up_bias.reshape(-1, singles[0].shape[0])], axis=0
    )
    way_qkv = Steps(spread(qkv_weight, fast_bits))
    other_turned = cross(tie(own_turned, way_qkv.got))
    other_vectors = cross(tie(flat_vectors, way_qkv.got))
    way_qkv.step()
    way_out = Steps(spread(tie(out_weight, other_turned), turned_bits))
    way_up = Steps(spread(tie(up_weight, other_turned), turned_bits))
    grad_turned = cotangent.reshape(span, width).T
    grad_out = grad_turned.T
    grad_halves = grad_turned.reshape(2, width // 2, span)
    grad_left = pick(grad_halves, core, 0), swap(pick(grad_halves, 1 - core, 0), CORE_BIT)

    lower = choose(first, flat_vectors, other_vectors).astype(jnp.float32)
    upper = choose(first, other_vectors, flat_vectors).astype(jnp.float32)
    both = jnp.concatenate([lower, upper], axis=1)
    (gain_first, shift_first, bias_query, bias_value, bias_out, gain_second, shift_second,
     bias_down) = (both[i] for i in range(8))
    bias_up = jnp.concatenate([lower[8:].reshape(1, -1), upper[8:].reshape(1, -1)], axis=1)

    own_tokens = own_turned.T
    second = jnp.stack([bias_out, gain_second, shift_second])
    bias_down = bias_down.reshape(-1, 1)
    bias_up, own_tokens, second, bias_down, grad_out = bound((bias_up, own_tokens, second, bias_down, grad_out))
    way_qkv.step(bias_up, own_tokens, second, bias_down, grad_out)
    all_turned = jnp.concatenate(
        [choose(first, own_turned, other_turned), choose(first, other_turned, own_turned)], axis=1
    )
    unit_all, _ = centred_down(all_turned.astype(jnp.float32))
    normed_turned = low(unit_all * gain_first[:, None] + shift_first[:, None])
    normed_all = normed_turned.T
    normed = lax.dynamic_slice_in_dim(normed_all, position * span, span, axis=0)

    def for_cores(turned):
        parts = turned.reshape(2, 2, turned.shape[0] // 4, turned.shape[1])
        return pick(parts, core, 1), swap(pick(parts, 1 - core, 1), CORE_BIT)

    full_qkv = both_halves(qkv_weight, way_qkv.finish())
    full_q, full_k, full_v = (full_qkv[:, i * width : (i + 1) * width] for i in range(3))
    way_out.step(full_v)
    values = low(dot(tie(normed_all, way_out.latest), full_v) + bias_value)
    way_up.step(values)
    way_out.step(values)
    way_down = Steps(spread(tie(down_turned, way_up.latest), turned_bits))
    keys = low(dot(tie(normed_all, way_out.latest, way_up.latest), full_k))
    way_out.step(keys)
    queries = low(low(dot(tie(normed, way_out.latest), full_q) + bias_query) * SCALING)
    (queries,) = bound((queries,), way_up, way_down)
    way_up.step()
    way_down.step()
    context, context_t, lse = attention_forward(
        spot, tie(queries, way_up.latest, way_down.latest), keys, values, 1, span
    )
    context, context_t, lse = bound((context, context_t, lse), way_up, way_down, way_out)
    full_out = both_halves(out_weight, way_out.finish())
    way_up.step()
    way_down.step()
    context = tie(context, way_up.latest, way_down.latest)
    part_up = way_up.finish()
    active, slope, middle_turned, unit_second, rstd_second, two_turned = mlp_up(
        spot, context, full_out, own_tokens, second, bias_up, up_weight, part_up
    )
    active, slope, middle_turned, unit_second, rstd_second, two_turned = bound(
        (active, slope, middle_turned, unit_second, rstd_second, two_turned), way_down
    )
    way_down.step()

    active_sib = swap(active, CORE_BIT)
    normed_left = for_cores(normed_turned)
    give, keep_down = turned_weight_grads(
        spot, *grad_left, tie(active, way_down.latest, normed_left[0]), active_sib, width // 2, "down_grads"
    )
    sum_down = Steps(reduced(keep_down, give, bits, True))
    part_down = way_down.finish(give)
    block_out = mlp_down(
        spot, tie(active, give), down_turned, part_down, middle_turned, bias_down
    )

    two_left = for_cores(two_turned)
    context_left = for_cores(context_t)
    results = mlp_back(
        spot, tie(grad_out, block_out, *two_left, *context_left), slope, unit_second, rstd_second,
        gain_second.reshape(1, -1), full_out, down_turned, part_down, up_weight, part_up,
    )
    grad_hidden, grad_middle, grad_branch, grad_context, sum_hidden, sum_rows = bound(results, sum_down)
    sum_down.step()
    hidden_sib = swap(grad_hidden, CORE_BIT)
    branch_sib = swap(grad_branch, CORE_BIT)
    give_out, keep_out = weight_grads(
        spot, *context_left, grad_branch, branch_sib, width, context_left[0].shape[1], grad_branch.shape[1],
        "out_grads"
    )
    sum_out = Steps(reduced(keep_out, give_out, bits))
    give, keep_up = weight_grads(
        spot, *two_left, grad_hidden, tie(hidden_sib, give_out), grad_hidden.shape[1], two_left[0].shape[1],
        grad_hidden.shape[1] // 2, "up_grads"
    )
    give, keep_up = bound((give, keep_up), sum_down)
    sum_up = Steps(reduced(keep_up, give, bits, True))
    sum_down.step()
    grad_context = tie(grad_context, give, sum_down.latest)

    grad_q, grad_k, grad_v = attention_backward(
        spot, queries, keys, values, grad_context, context, lse, 1, span
    )
    grad_q, grad_k, grad_v = bound((grad_q, grad_k, grad_v), sum_down, sum_out, sum_up)
    sum_down.step()
    sum_out.step()
    sum_up.step()
    rights = []
    for part in (grad_q, grad_k, grad_v):
        rights += [part, swap(part, CORE_BIT)]
    mine, theirs = input_grads(
        spot, full_q, full_k, full_v, tie(grad_q, sum_down.latest, sum_out.latest, sum_up.latest), grad_k, grad_v
    )
    mine, theirs = bound((mine, theirs), sum_up, sum_down, sum_out)
    sum_up.step()
    sum_down.step()
    sum_out.step()
    rights[0] = tie(grad_q, sum_down.latest, sum_out.latest, sum_up.latest, theirs)
    give, keep_qkv = qkv_weight_grads(spot, width, *normed_left, *rights)
    give, keep_qkv = bound((give, keep_qkv), sum_out)
    sum_out.step()
    sum_qkv = Steps(reduced(keep_qkv, give, bits))

    other_part = cross(tie(theirs, sum_qkv.got))
    grad_middle, sum_rows, sum_hidden = bound((grad_middle, sum_rows, sum_hidden, give))[:3]

    unit_first, rstd_first = centred_down(own_turned.astype(jnp.float32))
    unit_other, _ = centred_down(other_turned.astype(jnp.float32))
    theirs_float = theirs.astype(jnp.float32)
    sums = (
        jnp.sum(mine * unit_first, axis=1) + jnp.sum(theirs_float * unit_other, axis=1),
        jnp.sum(mine, axis=1) + jnp.sum(theirs_float, axis=1),
        row_sum(grad_q)[:width],
        row_sum(grad_v)[:width],
        sum_rows[2],
        sum_rows[0],
        sum_rows[1],
        sum_hidden.reshape(-1),
        jnp.sum(grad_turned.astype(jnp.float32), axis=1),
    )
    small = jnp.stack([item.reshape(2, -1) for item in sums[:7] + sums[8:]], axis=1)
    small = jnp.concatenate([small, sums[7].reshape(2, -1, width // 2)], axis=1)
    sum_small = Steps(vector_sum(small))
    grad_tokens = token_grads(
        spot, mine, other_part, own_turned, gain_first.reshape(-1, 1), grad_middle
    )

    chains = {"d": sum_down, "u": sum_up, "q": sum_qkv, "o": sum_out, "v": sum_small}
    done = {}
    latest = give
    for name in TAIL:
        if name == "t":
            latest = grad_tokens
            continue
        chain = chains[name]
        try:
            chain.step(latest)
            latest = chain.latest
        except StopIteration as end:
            value = end.value
            if name in "do":
                (value,) = bound((value,), sum_qkv)
            done[name] = latest = value
    vectors_out = done["v"]
    outs = [vectors_out[i] for i in range(7)] + [vectors_out[8:].reshape(-1), vectors_out[7]]

    return (
        block_out.T.reshape(1, span, width),
        grad_tokens.T.reshape(1, span, width),
        done["q"], done["o"], done["u"], done["d"].T,
        *outs,
    )


def on_device_general(
    tokens, qkv_weight, out_weight, up_weight, down_weight, attn_gain, attn_shift, query_bias,
    value_bias, out_bias, mlp_gain, mlp_shift, up_bias, down_bias, cotangent,
):
    seqs, span, width = tokens.shape
    rows = seqs * span
    shards = lax.axis_size("shard")
    position = lax.axis_index("shard")
    core = lax.axis_index("replica") & CORE_BIT
    length = span * shards
    bits = all_bits()

    shards_of = (attn_gain, attn_shift, query_bias, value_bias, out_bias, mlp_gain, mlp_shift,
                 up_bias, down_bias)
    flat_vectors = jnp.concatenate(shards_of)
    all_vectors = lax.all_gather(flat_vectors, "shard", axis=0, tiled=False)
    vectors, at = [], 0
    for item in shards_of:
        size = item.shape[0]
        vectors.append(all_vectors[:, at : at + size].reshape(-1).astype(jnp.float32))
        at += size
    (gain_first, shift_first, bias_query, bias_value, bias_out, gain_second, shift_second, bias_up,
     bias_down) = vectors

    full_qkv, full_out, full_up, full_down = [
        lax.all_gather(item, "shard", axis=0, tiled=True)
        for item in (qkv_weight, out_weight, up_weight, down_weight)
    ]
    all_tokens = lax.all_gather(tokens, "shard", axis=1, tiled=True).reshape(-1, width)

    def own_rows(values):
        per_seq = values.reshape(seqs, length, values.shape[-1])
        return lax.dynamic_slice_in_dim(per_seq, position * span, span, axis=1).reshape(rows, -1)

    grad_out = cotangent.reshape(rows, width)
    grad_out_both = jnp.concatenate([grad_out, swap(grad_out, CORE_BIT)], axis=0)

    flat = tokens.reshape(rows, width).astype(jnp.float32)
    unit_all, rstd_all = centred(all_tokens.astype(jnp.float32))
    normed_all = low(unit_all * gain_first + shift_first)
    normed_sib = swap(normed_all, CORE_BIT)
    normed = own_rows(normed_all)
    full_q, full_k, full_v = (full_qkv[:, i * width : (i + 1) * width] for i in range(3))
    queries = low(low(dot(normed, full_q) + bias_query) * SCALING)
    keys = low(dot(normed_all, full_k))
    values = low(dot(normed_all, full_v) + bias_value)
    spot = position.astype(jnp.int32).reshape(1)
    context, context_t, lse = attention_forward(spot, queries, keys, values, seqs, span)
    context_sib = swap(context, CORE_BIT)
    middle = flat + dot(context, full_out) + bias_out
    unit_second, rstd_second = centred(middle)
    normed_two = low(unit_second * gain_second + shift_second)
    normed_two_sib = swap(normed_two, CORE_BIT)
    active_float, slope = gelu_parts(dot(normed_two, full_up) + bias_up)
    active = low(active_float)
    slope = low(slope)

    def split_rows(lhs, rhs):
        return lax.psum_scatter(low(dot_tn(lhs, rhs)), "shard", scatter_dimension=0, tiled=True)

    grouped = active.reshape(rows, shards, 2, -1)
    taken = jnp.where(core == 0, grouped[:, :, 0], grouped[:, :, 1]).reshape(rows, -1)
    given = jnp.where(core == 0, grouped[:, :, 1], grouped[:, :, 0]).reshape(rows, -1)
    active_both = jnp.concatenate([taken, swap(given, CORE_BIT)], axis=0)
    sum_down = split_rows(active_both, grad_out_both)
    sum_down = reduce_rest(sum_down, bits)
    sum_down = in_order(CORE_BIT, sum_down, swap(sum_down, CORE_BIT))

    result = middle + dot(active, full_down) + bias_down
    block_out = low(result).reshape(seqs, span, width)

    def by_columns(lhs_both, part):
        taken = columns_of(part, 1, core)
        given = columns_of(part, 1, 1 - core)
        return split_rows(lhs_both, jnp.concatenate([taken, swap(given, CORE_BIT)], axis=0))

    def join_columns(values):
        other = swap(values, CORE_BIT)
        left = choose(core == 0, values, other)
        right = choose(core == 0, other, values)
        return left, right

    grad_float = grad_out.astype(jnp.float32)
    grad_hidden = low(dot_nt(grad_out, full_down) * slope.astype(jnp.float32))
    normed_two_both = jnp.concatenate([normed_two, normed_two_sib], axis=0)
    sum_up = by_columns(normed_two_both, grad_hidden)
    sum_up = reduce_rest(sum_up, bits)
    sum_up = jnp.concatenate(join_columns(sum_up), axis=1)
    grad_normed_two = dot_nt(grad_hidden, full_up)
    grad_middle = norm_pull(grad_normed_two, unit_second, rstd_second, gain_second) + grad_float
    grad_branch = low(grad_middle)
    grad_context = low(dot_nt(grad_branch, full_out))
    context_both = jnp.concatenate([context, context_sib], axis=0)
    sum_out = by_columns(context_both, grad_branch)
    sum_out = reduce_rest(sum_out, bits)
    sum_out = jnp.concatenate(join_columns(sum_out), axis=1)

    grad_q, grad_k, grad_v = attention_backward(
        spot, queries, keys, values, grad_context, context, lse, seqs, span
    )
    grad_q, grad_k, grad_v = grad_q[:, :width], grad_k[:, :width], grad_v[:, :width]
    normed_both = jnp.concatenate([normed_all, normed_sib], axis=0)
    own_both = jnp.concatenate([normed, own_rows(normed_sib)], axis=0)
    third = width // 2
    half_q, half_k, half_v = (
        jnp.concatenate(
            [columns_of(part, 1, core), swap(columns_of(part, 1, 1 - core), CORE_BIT)], axis=0
        )
        for part in (grad_q, grad_k, grad_v)
    )
    sum_qkv = lax.psum_scatter(
        low(jnp.concatenate(
            [dot_tn(own_both, half_q), dot_tn(normed_both, half_k), dot_tn(normed_both, half_v)],
            axis=1,
        )),
        "shard", scatter_dimension=0, tiled=True,
    )
    sum_qkv = reduce_rest(sum_qkv, bits)
    left, right = join_columns(sum_qkv)
    sum_qkv = jnp.concatenate(
        [part[:, i * third : (i + 1) * third] for i in range(3) for part in (left, right)], axis=1
    )

    from_query = dot_nt(grad_q, full_q)
    from_rest = dot_nt(grad_k, full_k) + dot_nt(grad_v, full_v)
    grad_normed = from_query + lax.psum_scatter(
        from_rest.reshape(seqs, length, width), "shard", scatter_dimension=1, tiled=True
    ).reshape(rows, width)
    unit_first, rstd_first = own_rows(unit_all), own_rows(rstd_all)
    grad_tokens = low(norm_pull(grad_normed, unit_first, rstd_first, gain_first) + grad_middle)

    def column_sum(values):
        return jnp.sum(values.astype(jnp.float32), axis=0)

    sums = (
        column_sum(grad_normed * unit_first),
        column_sum(grad_normed),
        column_sum(grad_q),
        column_sum(grad_v),
        column_sum(grad_branch),
        column_sum(grad_normed_two * unit_second),
        column_sum(grad_normed_two),
        column_sum(grad_hidden),
        column_sum(grad_float),
    )
    packed = jnp.concatenate([item.reshape(shards, -1) for item in sums], axis=1)
    packed = lax.psum(packed, ("replica", "shard"))
    packed = lax.dynamic_index_in_dim(packed, position, axis=0, keepdims=False)
    outs, at = [], 0
    for item in sums:
        size = item.shape[0] // shards
        outs.append(packed[at : at + size])
        at += size
    return (
        block_out,
        grad_tokens.reshape(seqs, span, width),
        sum_qkv.astype(jnp.float32),
        sum_out.astype(jnp.float32),
        sum_up.astype(jnp.float32),
        sum_down.astype(jnp.float32),
        *outs,
    )


def on_device(tokens, *rest):
    if lax.axis_size("shard") == 2 and lax.axis_size("replica") >= 8 and tokens.shape[0] == 1:
        return on_device_pair(tokens, *rest)
    return on_device_general(tokens, *rest)


def solution(mesh):
    vector, matrix, rows = P("shard"), P("shard", None), P("replica", "shard", None)
    return jax.shard_map(
        on_device,
        mesh=mesh,
        in_specs=(rows, *[matrix] * 4, *[vector] * 9, rows),
        out_specs=(rows, rows, *[matrix] * 4, *[vector] * 9),
        check_vma=False,
    )
```
